32 devices in a mesh: gx: 2 (over x), gy: 4 (over y, core), gz: 4 (over z).
Axes of the slice: x: 2, y: 2, z: 4, core: 2. Of those that a mesh axis runs over, the one named last changes fastest.
Arguments:
- features: bfloat16 [32, 8, 256, 512], P(None, 'gx', 'gy', 'gz'), may hold values from -6 to 6
- conv_weight: bfloat16 [27, 32], replicated, may hold values from -0.21875 to 0.21875
- mask: int32 [8, 256, 512], P('gx', 'gy', 'gz'), may hold values from 0 to 1, as said below
Outputs:
- score: float32 [8, 256, 512], P('gx', 'gy', 'gz')
- depth: float32 [8, 256, 512], P('gx', 'gy', 'gz')
The draws below stay inside these ranges and needn't reach their ends.
Inputs may be any that keep to these rules, and one draw needn't show every extreme that they name: `mask`: 1 marks a foreground voxel and 0 a background voxel; every draw holds both.
All inputs are finite; a program needn't handle non-finite values.
Results may differ from the reference program's by a relative error of at most 0.0003.
Values may be sent and summed in bfloat16 or wider, within the bound.
No kernel may reach another device: no remote copies, remote signals or barrier semaphores. Data moves between devices by JAX's collectives and lax.ppermute only.
A program may use at most 128 MiB of HBM per device.

```python
import jax
import jax.numpy as jnp
from jax import lax

CH = 32
RADIUS = 128
NX = 8
NY = 256
NZ = 512


def draw_mask(key, part):
    count = max(2, NX * NY * NZ // (2 * RADIUS ** 3))
    centre_x = jax.random.randint(jax.random.fold_in(key, 11), (count,), 0, NX, dtype=jnp.int32)
    centre_y = jax.random.randint(jax.random.fold_in(key, 12), (count,), 0, NY, dtype=jnp.int32)
    centre_z = jax.random.randint(jax.random.fold_in(key, 13), (count,), 0, NZ, dtype=jnp.int32)
    radius_all = jax.random.randint(jax.random.fold_in(key, 14), (count,), RADIUS // 2, 3 * RADIUS // 2, dtype=jnp.int32)
    empty_x = jax.random.randint(jax.random.fold_in(key, 15), (), 0, NX, dtype=jnp.int32)
    empty_y = jax.random.randint(jax.random.fold_in(key, 16), (), 0, NY, dtype=jnp.int32)
    empty_z = (centre_z[0] + NZ // 2) % NZ
    apart = (centre_x - empty_x) ** 2 + (centre_y - empty_y) ** 2 + (centre_z - empty_z) ** 2
    trials = jnp.arange(3 * RADIUS // 2, dtype=jnp.int32)
    largest = jnp.sum((trials[None, :] * trials[None, :] < apart[:, None]).astype(jnp.int32), axis=1) - 1
    first_radius = jnp.minimum(radius_all[0], largest[0])
    grid_x = jnp.arange(NX, dtype=jnp.int32)[:, None, None]
    grid_y = jnp.arange(NY, dtype=jnp.int32)[None, :, None]
    grid_z = jnp.arange(NZ, dtype=jnp.int32)[None, None, :]
    inside = jnp.zeros((NX, NY, NZ), jnp.bool_)
    for which in range(count):
        if which == 0:
            extent = first_radius
        else:
            extent = radius_all[which]
        spread = (grid_x - centre_x[which]) ** 2 + (grid_y - centre_y[which]) ** 2 + (grid_z - centre_z[which]) ** 2
        member = spread <= extent * extent
        if which > 0:
            member = member & (extent * extent < apart[which])
        inside = inside | member
    return inside.astype(jnp.int32)


def level_of(rng, shape, cuts, smallest, high):
    level, own = 1.0, jax.random.fold_in(rng, 6)
    for position, shards_of in cuts:
        steps = jnp.exp(jax.random.uniform(jax.random.fold_in(own, position), (shards_of,), jnp.float32, smallest / len(cuts), high / len(cuts)))
        level = level * jnp.repeat(steps, shape[position] // shards_of).reshape([-1 if axis == position else 1 for axis in range(len(shape))])
    return level


def bell_draw(rng, shape, scale, most, cuts=(), kind=jnp.bfloat16):
    drawn = scale * jax.random.normal(rng, shape, jnp.float32)
    if cuts:
        drawn = drawn * level_of(rng, shape, cuts, -0.22, 0.18)
    return jnp.clip(drawn, -most, most).astype(kind)


def setup_inputs(seed: int = 0) -> dict:
    key_of = jax.random.split(jax.random.key(seed), 4)
    return {
        "features": bell_draw(key_of[0], (CH, NX, NY, NZ), 1.0, 6.0, ((1, 2), (2, 4), (3, 4))),
        "conv_weight": bell_draw(key_of[1], (27, CH), (27 * CH) ** -0.5, 0.21875),
        "mask": draw_mask(jax.random.fold_in(key_of[3], 71), 0),
    }


def window_min(padded, axis, length, radius):
    center = lax.slice_in_dim(padded, radius, radius + length, axis=axis)

    def step(shift, acc):
        shift = jnp.asarray(shift).astype(jnp.int32)
        lower = lax.dynamic_slice_in_dim(padded, (radius - shift).astype(jnp.int32), length, axis)
        upper = lax.dynamic_slice_in_dim(padded, (radius + shift).astype(jnp.int32), length, axis)
        square = (shift * shift).astype(jnp.float32)
        return jnp.minimum(acc, jnp.minimum(lower, upper) + square)

    return lax.fori_loop(1, radius + 1, step, center)


def line_pass(values, axis, radius, ceiling):
    widths = [(0, 0), (0, 0), (0, 0)]
    widths[axis] = (radius, radius)
    padded = jnp.pad(values, widths, constant_values=ceiling)
    return window_min(padded, axis, values.shape[axis], radius)


def reference(features, conv_weight, mask):
    kernel = jnp.transpose(conv_weight).reshape(1, CH, 3, 3, 3)
    score = lax.conv_general_dilated(features[None], kernel, (1, 1, 1), "SAME", dimension_numbers=("NCDHW", "OIDHW", "NCDHW"), preferred_element_type=jnp.float32)[0, 0]
    ceiling = float(RADIUS * RADIUS)
    cost = jnp.where(mask == 1, jnp.float32(ceiling), ceiling * jax.nn.sigmoid(score))
    along_x = line_pass(cost, 0, RADIUS, ceiling)
    along_y = line_pass(along_x, 1, RADIUS, ceiling)
    distance = line_pass(along_y, 2, RADIUS, ceiling)
    return score, distance / RADIUS
```

```python
import functools

import jax
import jax.numpy as jnp
from jax import lax
from jax.experimental import pallas as pl
from jax.experimental.pallas import tpu as pltpu
from jax.sharding import PartitionSpec as P

RADIUS = 128
CEILING = float(RADIUS * RADIUS)
HUGE = 1e30
LANES = 128
ROWS = 24
VMEM = pl.BlockSpec(memory_space=pltpu.VMEM)


def params(mib):
    return pltpu.CompilerParams(vmem_limit_bytes=mib * 1024 * 1024)


def call(kernel, outs, scratch=(), mib=8, in_specs=None):
    shapes = [jax.ShapeDtypeStruct(s, jnp.float32) for s in outs]

    def run(*args):
        return pl.pallas_call(
            kernel,
            out_shape=shapes,
            in_specs=in_specs or [VMEM] * len(args),
            out_specs=[VMEM] * len(shapes),
            scratch_shapes=list(scratch),
            compiler_params=params(mib),
        )(*args)

    return run


def lane_of(shape):
    return lax.broadcasted_iota(jnp.int32, shape, len(shape) - 1)


def row_of(shape):
    return lax.broadcasted_iota(jnp.int32, shape, len(shape) - 2)


def cost_of(score):
    return CEILING / (1.0 + jnp.exp(-score))


def conv_kernel(f_ref, w_ref, se_ref, he_ref, face_ref, f_vmem, w_big, acc, sems):
    channels, size_x, size_y, _ = f_vmem.shape
    tiles = size_y // 16
    depth = channels * 16
    copies = [
        pltpu.make_async_copy(f_ref.at[:, x], f_vmem.at[:, x], sems.at[x])
        for x in range(size_x)
    ]
    for copy in copies:
        copy.start()

    spread = (
        lax.broadcasted_iota(jnp.int32, (channels, depth), 1) // 16
        == lax.broadcasted_iota(jnp.int32, (channels, depth), 0)
    ).astype(jnp.bfloat16)
    wide = jnp.dot(w_ref[...], spread, preferred_element_type=jnp.float32)
    row = lax.broadcasted_iota(jnp.int32, (ROWS, depth), 0)
    y_in = lax.broadcasted_iota(jnp.int32, (ROWS, depth), 1) % 16
    y_out = jnp.where(row <= 16, row, jnp.where(row == ROWS - 1, -1, 64))
    tap = y_in - y_out + 1
    blocks = []
    for a in range(3):
        for c in range(3):
            block = jnp.zeros((ROWS, depth), jnp.float32)
            for b in range(3):
                k = 9 * a + 3 * b + c
                block = jnp.where(tap == b, wide[k : k + 1, :], block)
            blocks.append(block)
    blocks.append(jnp.zeros((8, depth), jnp.float32))
    w_big[...] = jnp.concatenate(blocks, axis=0).astype(jnp.bfloat16)

    acc[...] = jnp.zeros_like(acc)
    for x in range(size_x):
        copies[x].wait()
        right = jnp.concatenate(
            [f_vmem[:, x, 16 * t : 16 * t + 16, :].reshape(depth, LANES) for t in range(tiles)],
            axis=1,
        )
        got = jnp.dot(w_big[...], right, preferred_element_type=jnp.float32)
        for a in range(3):
            at = x + 2 - a
            for c in range(3):
                first = (3 * a + c) * ROWS
                acc[at, c] = acc[at, c] + got[first : first + ROWS, :]

    shape = (8, LANES)
    row, lane = row_of(shape), lane_of(shape)
    groups = size_y // 8
    for at in range(size_x + 2):
        for g in range(groups + 1):
            sums = []
            for c in range(3):

                def piece(tile, low, c=c):
                    return acc[at, c, low : low + 8, tile * LANES : tile * LANES + LANES]

                if g == groups:
                    part = jnp.where(row == 0, piece(tiles - 1, 16), 0.0) + jnp.where(
                        row == 7, piece(0, 16), 0.0
                    )
                else:
                    tile, low = g // 2, 8 * (g % 2)
                    part = piece(tile, low)
                    if low == 0 and tile > 0:
                        part = part + jnp.where(row == 0, piece(tile - 1, 16), 0.0)
                    if low == 8 and tile < tiles - 1:
                        part = part + jnp.where(row == 7, piece(tile + 1, 16), 0.0)
                sums.append(part)
            ahead = pltpu.roll(sums[0], 1, 1)
            behind = pltpu.roll(sums[2], LANES - 1, 1)
            inner = (
                sums[1] + jnp.where(lane == 0, 0.0, ahead) + jnp.where(lane == LANES - 1, 0.0, behind)
            )
            outer = jnp.where(lane == 0, ahead, jnp.where(lane == LANES - 1, behind, 0.0))
            span = slice(8 * g, 8 * g + 8)
            if 1 <= at <= size_x:
                se_ref[at - 1, span, :] = inner
                he_ref[at - 1, span, :] = outer
            else:
                side = 0 if at == 0 else 1
                face_ref[side, 0, span, :] = inner
                face_ref[side, 1, span, :] = outer


def xy_sum(se_ref, he_ref, xs, ys, x, rows):
    size_x = se_ref.shape[0]
    own = [se_ref[x, rows, :], he_ref[x, rows, :]]
    if x == 0:
        own = [v + xs[0][k, rows, :] for k, v in enumerate(own)]
    if x == size_x - 1:
        own = [v + xs[1][k, rows, :] for k, v in enumerate(own)]
    return own


def edge_kernel(se_ref, he_ref, low_ref, high_ref, out_ref):
    size_x, size = se_ref.shape[0], se_ref.shape[1]
    rows = slice(size - 8, size)
    for x in range(size_x):
        s, h = xy_sum(se_ref, he_ref, (low_ref, high_ref), None, x, rows)
        out_ref[x, 0] = s
        out_ref[x, 1] = h


def turn_kernel(se_ref, he_ref, low_ref, high_ref, ylow_ref, yhigh_ref, mask_ref, score_ref, zm_ref):
    size_x, size = se_ref.shape[0], se_ref.shape[1]
    size_y = size - 8
    rows = slice(0, size_y)
    shape = (size_y, LANES)
    row, lane = row_of(shape), lane_of(shape)
    border = (lane == 0) | (lane == LANES - 1)
    sends, outers = [], []
    for x in range(size_x):
        parts = xy_sum(se_ref, he_ref, (low_ref, high_ref), None, x, rows)
        full = []
        for k in range(2):
            low = jnp.concatenate([ylow_ref[x, k], jnp.zeros((size_y - 8, LANES), jnp.float32)], axis=0)
            high = jnp.concatenate([jnp.zeros((size_y - 8, LANES), jnp.float32), yhigh_ref[x, k]], axis=0)
            full.append(
                parts[k] + jnp.where(row == 0, low, 0.0) + jnp.where(row == size_y - 1, high, 0.0)
            )
        s, h = full
        score_ref[x] = s
        masked = jnp.where(mask_ref[x] == 1, HUGE, s)
        sends.append(jnp.where(border, masked, cost_of(masked)))
        outers.append(h)
    send = jnp.concatenate(sends, axis=0)
    outer = jnp.concatenate(outers, axis=0)
    zm_ref[0:LANES, :] = send.T
    turned = outer.T
    top = row_of((8, turned.shape[1]))
    zm_ref[LANES : LANES + 8, :] = jnp.where(top == 7, turned[LANES - 8 : LANES], turned[0:8])


def fill_squares(table, low, high):
    s = row_of((8, LANES)).astype(jnp.float32)
    for d in range(low, high + 1):
        v = s + float(d)
        table[d - low] = v * v


def z_own_kernel(zm_ref, out_ref, table):
    lines = zm_ref.shape[1]
    parts = lines // LANES
    count = LANES // 8
    low = -(LANES - 1)
    fill_squares(table, low, LANES - 8)

    def body(j, accs):
        base = pl.multiple_of(j * 8, 8)
        accs = list(accs)
        at = row_of((8, LANES)) + base
        hide = (at == 0) | (at == LANES - 1)
        tiles = [
            jnp.where(hide, HUGE, zm_ref[pl.ds(base, 8), k * LANES : (k + 1) * LANES])
            for k in range(parts)
        ]
        for r in range(8):
            rows = [jnp.broadcast_to(t[r : r + 1, :], (8, LANES)) for t in tiles]
            for b in range(count):
                square = table[8 * b - r - low - base]
                for k in range(parts):
                    i = b * parts + k
                    accs[i] = jnp.minimum(accs[i], rows[k] + square)
        return tuple(accs)

    start = tuple(jnp.full((8, LANES), HUGE, jnp.float32) for _ in range(count * parts))
    accs = lax.fori_loop(0, LANES // 8, body, start)
    for b in range(count):
        for k in range(parts):
            out_ref[8 * b : 8 * b + 8, k * LANES : (k + 1) * LANES] = accs[b * parts + k]


def z_far_kernel(axis, acc_ref, zm_ref, low_ref, high_ref, score_in, score_ref, out_ref, table):
    index, last = lax.axis_index(axis), lax.axis_size(axis) - 1
    has_low, has_high = index > 0, index < last
    lines = zm_ref.shape[1]
    parts = lines // LANES
    count = LANES // 8
    floor = -(LANES + 6)
    fill_squares(table, floor, LANES - 1)
    size_x, size_y = score_in.shape[0], score_in.shape[1]

    from_low = jnp.where(has_low, low_ref[LANES : LANES + 1, :], 0.0)
    from_high = jnp.where(has_high, high_ref[LANES + 7 : LANES + 8, :], 0.0)
    own_first = cost_of(zm_ref[0:1, :] + from_low)
    own_last = cost_of(zm_ref[LANES - 1 : LANES, :] + from_high)
    low_last = cost_of(low_ref[LANES - 1 : LANES, :] + zm_ref[LANES + 7 : LANES + 8, :])
    high_first = cost_of(high_ref[0:1, :] + zm_ref[LANES : LANES + 1, :])

    for k in range(parts):
        cols = slice(k * LANES, (k + 1) * LANES)

        def spread(v, valid=None):
            v = jnp.broadcast_to(v, (8, LANES))
            return v if valid is None else jnp.where(valid, v, HUGE)

        accs = [acc_ref[8 * b : 8 * b + 8, cols] for b in range(count)]
        for source, q in ((own_first, 0), (own_last, LANES - 1)):
            v = spread(source[:, cols])
            for b in range(count):
                accs[b] = jnp.minimum(accs[b], v + table[8 * b - q - floor])
        for q in range(1, LANES):
            v = low_last[:, cols] if q == LANES - 1 else low_ref[q : q + 1, cols]
            v = spread(v, has_low)
            for b in range((q - 1) // 8 + 1):
                accs[b] = jnp.minimum(accs[b], v + table[8 * b - q + LANES - floor])
        for q in range(0, LANES - 1):
            v = high_first[:, cols] if q == 0 else high_ref[q : q + 1, cols]
            v = spread(v, has_high)
            for b in range(max(0, -((6 - q) // 8)), count):
                accs[b] = jnp.minimum(accs[b], v + table[8 * b - LANES - q - floor])
        best = jnp.concatenate(accs, axis=0).T
        middle = jnp.zeros((LANES - 2, LANES), jnp.float32)
        more = jnp.concatenate([from_low[:, cols], middle, from_high[:, cols]], axis=0).T
        per = LANES // size_y
        for i in range(per):
            x = k * per + i
            rows = slice(i * size_y, (i + 1) * size_y)
            out_ref[x] = best[rows]
            score_ref[x] = score_in[x] + more[rows]


def x_kernel(axis, own_ref, *refs):
    out_ref = refs[-1]
    index = lax.axis_index(axis)
    size_x = own_ref.shape[0]
    best = []
    for i in range(size_x):
        v = own_ref[i]
        for j in range(size_x):
            if j != i:
                v = jnp.minimum(v, own_ref[j] + float((i - j) ** 2))
        best.append(v)
    for k, ref in enumerate(refs[:-1]):
        away = ((index ^ (k + 1)) - index) * size_x
        for i in range(size_x):
            for j in range(size_x):
                far = (away + (j - i)).astype(jnp.float32)
                best[i] = jnp.minimum(best[i], ref[j] + far * far)
    for i in range(size_x):
        out_ref[i] = best[i]


def y_kernel(axis, hops, start, scale, *refs):
    table, out_ref = refs[-1], refs[-2]
    blocks = refs[: len(hops)]
    index = lax.axis_index(axis)
    size_x, size_y, _ = out_ref.shape
    count = size_y // 8
    s = row_of((8, LANES))
    low = -(size_y - 1)
    if start:
        accs = [refs[len(hops)][x, 8 * b : 8 * b + 8, :] for x in range(size_x) for b in range(count)]
    else:
        accs = [jnp.full((8, LANES), HUGE, jnp.float32) for _ in range(size_x * count)]
    accs = tuple(accs)
    for ref, hop in zip(blocks, hops):
        away = ((index ^ hop) - index) * size_y
        for d in range(low, size_y - 7):
            v = (s + (d - away)).astype(jnp.float32)
            table[d - low] = v * v

        def body(j, accs, ref=ref):
            accs = list(accs)
            base = pl.multiple_of(j * 8, 8)
            tiles = [ref[x, pl.ds(base, 8), :] for x in range(size_x)]
            for r in range(8):
                rows = [jnp.broadcast_to(t[r : r + 1, :], (8, LANES)) for t in tiles]
                for b in range(count):
                    square = table[8 * b - r - low - base]
                    for x in range(size_x):
                        i = x * count + b
                        accs[i] = jnp.minimum(accs[i], rows[x] + square)
            return tuple(accs)

        accs = lax.fori_loop(0, size_y // 8, body, accs)
    for x in range(size_x):
        for b in range(count):
            out_ref[x, 8 * b : 8 * b + 8, :] = accs[x * count + b] * scale


def swap(value, axis, hop):
    n = lax.axis_size(axis)
    return lax.ppermute(value, axis, [(i, i ^ hop) for i in range(n)])


def neighbours(low, high, axis):
    n, index = lax.axis_size(axis), lax.axis_index(axis)
    odd = index % 2 == 1
    even_pairs = [(i, i ^ 1) for i in range(n)]
    got_even = lax.ppermute(jnp.where(odd, low, high), axis, even_pairs)
    zero = jnp.zeros_like(got_even)
    if n == 2:
        return jnp.where(odd, got_even, zero), jnp.where(odd, zero, got_even)
    odd_pairs = [(i, (i + 1) % n if i % 2 else (i - 1) % n) for i in range(n)]
    got_odd = lax.ppermute(jnp.where(odd, high, low), axis, odd_pairs)
    from_low = jnp.where(odd, got_even, got_odd)
    from_high = jnp.where(odd, got_odd, got_even)
    return jnp.where(index == 0, zero, from_low), jnp.where(index == n - 1, zero, from_high)


def both_sides(value, axis):
    n, index = lax.axis_size(axis), lax.axis_index(axis)
    odd = index % 2 == 1
    even = lax.ppermute(value, axis, [(i, i ^ 1) for i in range(n)])
    other = lax.ppermute(value, axis, [(i, i + 1 if i % 2 else i - 1) for i in range(1, n - 1)])
    return even, other, odd


def shards(features, conv_weight, mask):
    channels, size_x, size_y, size_z = features.shape
    gx, gy, gz = lax.axis_size("gx"), lax.axis_size("gy"), lax.axis_size("gz")
    assert size_z == LANES and size_y % 16 == 0 and LANES % size_y == 0
    tiles = size_y // 16
    high = size_y + 8
    brick = (size_x, size_y, LANES)

    se, he, face = call(
        conv_kernel,
        [(size_x, high, LANES), (size_x, high, LANES), (2, 2, high, LANES)],
        [
            pltpu.VMEM(features.shape, jnp.bfloat16),
            pltpu.VMEM((9 * ROWS + 8, channels * 16), jnp.bfloat16),
            pltpu.VMEM((size_x + 2, 3, ROWS, tiles * LANES), jnp.float32),
            pltpu.SemaphoreType.DMA((size_x,)),
        ],
        mib=24,
        in_specs=[pl.BlockSpec(memory_space=pl.ANY), VMEM],
    )(features, conv_weight)

    x_low, x_high = neighbours(face[0], face[1], "gx")
    (edges,) = call(edge_kernel, [(size_x, 2, 8, LANES)])(se, he, x_low, x_high)
    y_low, y_high = neighbours(edges, edges, "gy")
    lines = size_x * size_y
    score, zm = call(turn_kernel, [brick, (LANES + 8, lines)])(
        se, he, x_low, x_high, y_low, y_high, mask
    )

    even, other, odd = both_sides(zm, "gz")
    (near,) = call(z_own_kernel, [(LANES, lines)], [pltpu.VMEM((2 * LANES - 8, 8, LANES), jnp.float32)])(zm)
    z_low, z_high = jnp.where(odd, even, other), jnp.where(odd, other, even)
    score, along_z = call(
        functools.partial(z_far_kernel, "gz"),
        [brick, brick],
        [pltpu.VMEM((2 * LANES + 6, 8, LANES), jnp.float32)],
    )(near, zm, z_low, z_high, score)

    others = [swap(along_z, "gx", k) for k in range(1, gx)]
    (along_x,) = call(functools.partial(x_kernel, "gx"), [brick])(along_z, *others)

    table = [pltpu.VMEM((2 * size_y - 8, 8, LANES), jnp.float32)]
    hops = [swap(along_x, "gy", k) for k in range(1, min(gy, 3))]
    if gy == 4:
        hops.append(swap(hops[1], "gy", 1))
    else:
        hops += [swap(along_x, "gy", k) for k in range(3, gy)]

    def y_pass(ks, blocks, start, scale):
        outs = call(functools.partial(y_kernel, "gy", ks, start is not None, scale), [brick], table)
        return outs(*blocks, *([] if start is None else [start]))[0]

    best = y_pass((0, 1), (along_x, hops[0]), None, 1.0)
    best = y_pass((2,), (hops[1],), best, 1.0)
    depth = y_pass(tuple(range(3, gy)), tuple(hops[2:]), best, 1.0 / RADIUS)
    return score, depth


def solution(mesh):
    in_specs = (P(None, "gx", "gy", "gz"), P(), P("gx", "gy", "gz"))
    out_specs = (P("gx", "gy", "gz"), P("gx", "gy", "gz"))
    return jax.shard_map(shards, mesh=mesh, in_specs=in_specs, out_specs=out_specs, check_vma=False)
```

```python
import functools

import jax
import jax.numpy as jnp
from jax import lax
from jax.experimental import pallas as pl
from jax.experimental.pallas import tpu as pltpu
from jax.sharding import PartitionSpec as P

RADIUS = 128
CEILING = float(RADIUS * RADIUS)
HUGE = 1e30
LANES = 128
ROWS = 24
VMEM = pl.BlockSpec(memory_space=pltpu.VMEM)
HBM = pl.BlockSpec(memory_space=pltpu.HBM)


def call(kernel, outs, scratch=(), mib=8, in_specs=None):
    shapes = [jax.ShapeDtypeStruct(s, jnp.float32) for s in outs]

    def run(*args):
        return pl.pallas_call(
            kernel,
            out_shape=shapes,
            in_specs=in_specs or [VMEM] * len(args),
            out_specs=[VMEM] * len(shapes),
            scratch_shapes=list(scratch),
            compiler_params=pltpu.CompilerParams(vmem_limit_bytes=mib * 1024 * 1024),
        )(*args)

    return run


def lane_of(shape):
    return lax.broadcasted_iota(jnp.int32, shape, len(shape) - 1)


def row_of(shape):
    return lax.broadcasted_iota(jnp.int32, shape, len(shape) - 2)


def cost_of(score):
    return CEILING / (1.0 + jnp.exp(-score))


def conv_kernel(planes, f_hbm, w_hbm, mask_hbm, s_ref, m_ref, e_ref, f_vmem, w_vmem, mask_vmem, w_big, acc, sems):
    channels, size_x, size_y, _ = f_vmem.shape
    tiles = size_y // 16
    depth = channels * 16
    weights = pltpu.make_async_copy(w_hbm, w_vmem, sems.at[size_x])
    weights.start()
    copies = [
        pltpu.make_async_copy(f_hbm.at[:, x], f_vmem.at[:, x], sems.at[x]) for x in range(size_x)
    ]
    for copy in copies:
        copy.start()
    masks = pltpu.make_async_copy(mask_hbm, mask_vmem, sems.at[size_x + 1])
    masks.start()

    acc[...] = jnp.zeros_like(acc)
    spread = (
        lax.broadcasted_iota(jnp.int32, (channels, depth), 1) // 16
        == lax.broadcasted_iota(jnp.int32, (channels, depth), 0)
    ).astype(jnp.bfloat16)
    row = lax.broadcasted_iota(jnp.int32, (ROWS, depth), 0)
    y_in = lax.broadcasted_iota(jnp.int32, (ROWS, depth), 1) % 16
    y_out = jnp.where(row <= 16, row, jnp.where(row == ROWS - 1, -1, 64))
    tap = y_in - y_out + 1
    weights.wait()
    wide = jnp.dot(w_vmem[...], spread, preferred_element_type=jnp.float32)
    blocks = []
    for a in range(3):
        for c in range(3):
            block = jnp.zeros((ROWS, depth), jnp.float32)
            for b in range(3):
                k = 9 * a + 3 * b + c
                block = jnp.where(tap == b, wide[k : k + 1, :], block)
            blocks.append(block)
    blocks.append(jnp.zeros((8, depth), jnp.float32))
    w_big[...] = jnp.concatenate(blocks, axis=0).astype(jnp.bfloat16)

    for x in range(size_x):
        copies[x].wait()
        right = jnp.concatenate(
            [f_vmem[:, x, 16 * t : 16 * t + 16, :].reshape(depth, LANES) for t in range(tiles)],
            axis=1,
        )
        got = jnp.dot(w_big[...], right, preferred_element_type=jnp.float32)
        for a in range(3):
            at = x + 2 - a
            for c in range(3):
                first = (3 * a + c) * ROWS
                acc[at, c] = acc[at, c] + got[first : first + ROWS, :]

    shape = (8, LANES)
    row, lane = row_of(shape), lane_of(shape)
    groups = size_y // 8
    masks.wait()
    for p, at in enumerate(planes()):
        fold = None
        for g in range(groups + 1):
            sums = []
            for c in range(3):

                def piece(tile, low, c=c):
                    return acc[at, c, low : low + 8, tile * LANES : tile * LANES + LANES]

                if g == groups:
                    part = jnp.where(row == 0, piece(tiles - 1, 16), 0.0) + jnp.where(
                        row == 7, piece(0, 16), 0.0
                    )
                else:
                    tile, low = g // 2, 8 * (g % 2)
                    part = piece(tile, low)
                    if low == 0 and tile > 0:
                        part = part + jnp.where(row == 0, piece(tile - 1, 16), 0.0)
                    if low == 8 and tile < tiles - 1:
                        part = part + jnp.where(row == 7, piece(tile + 1, 16), 0.0)
                sums.append(part)
            ahead = pltpu.roll(sums[0], 1, 1)
            behind = pltpu.roll(sums[2], LANES - 1, 1)
            inner = (
                sums[1] + jnp.where(lane == 0, 0.0, ahead) + jnp.where(lane == LANES - 1, 0.0, behind)
            )
            outer = jnp.where(lane == 0, ahead, jnp.where(lane == LANES - 1, behind, 0.0))
            if g == groups:
                e_ref[p, 0:8, :] = inner
                e_ref[p, 8:16, :] = jnp.where(row == 7, pltpu.roll(outer, 2 * (groups - 1), 1), outer)
            else:
                span = slice(8 * g, 8 * g + 8)
                if p < size_x:
                    s_ref[p, span, :] = inner
                    inner = jnp.where(mask_vmem[p, span, :] == 1, HUGE, inner)
                m_ref[p, span, :] = inner
                fold = outer if g == 0 else fold + pltpu.roll(outer, 2 * g, 1)
        m_ref[p, size_y : size_y + 8, :] = fold


def y_masks(axis, chip):
    row = row_of((8, LANES))
    index, last = lax.axis_index(axis), lax.axis_size(axis) - 1
    odd = index % 2
    if chip:
        low, high = odd == 1, odd == 0
    else:
        low, high = (odd == 0) & (index > 0), (odd == 1) & (index < last)
    return row == jnp.where(low, 0, -1), row == jnp.where(high, 7, -1)


def edge_rows(masks, part, size_y):
    low, high = masks
    return jnp.concatenate(
        [
            jnp.where(low, part, 0.0),
            jnp.zeros((size_y - 16, LANES), jnp.float32),
            jnp.where(high, part, 0.0),
        ],
        axis=0,
    )


def edge_fold(masks, part):
    low, high = masks
    return jnp.where(low, part, jnp.where(high, part, 0.0))


def turn_kernel(s_ref, own_ref, far_ref, chip_ref, cross_ref, xchip_ref, xcross_ref, score_ref, zm_ref):
    size_x, size_y, _ = s_ref.shape
    rows, fold = slice(0, size_y), slice(size_y, size_y + 8)
    chip, cross = y_masks("gy", True), y_masks("gy", False)
    first = lax.axis_index("gx") == 0
    lane = lane_of((size_y, LANES))
    border = (lane == 0) | (lane == LANES - 1)
    faces_own = {size_x - 1: jnp.where(first, 1.0, 0.0), 0: jnp.where(first, 0.0, 1.0)}
    faces_far = {0: faces_own[size_x - 1], size_x - 1: faces_own[0]}

    def complete(p, base, folded, face_ref, sides, faces):
        if p in faces:
            base = base + faces[p] * face_ref[size_x, rows]
            folded = folded + faces[p] * face_ref[size_x, fold]
        for masks, same, other in sides:
            part, part_h = same[p, 0:8], same[p, 8:16]
            if p in faces:
                part = part + faces[p] * other[size_x, 0:8]
                part_h = part_h + faces[p] * other[size_x, 8:16]
            base = base + edge_rows(masks, part, size_y)
            folded = folded + edge_fold(masks, part_h)
        return base, folded

    costs, turned = [], []
    for far in range(2):
        for p in range(size_x):
            if far:
                sides = ((chip, xchip_ref, chip_ref), (cross, xcross_ref, cross_ref))
                masked, h = complete(p, far_ref[p, rows], far_ref[p, fold], own_ref, sides, faces_far)
            else:
                sides = ((chip, chip_ref, xchip_ref), (cross, cross_ref, xcross_ref))
                full, h = complete(p, s_ref[p], own_ref[p, fold], far_ref, sides, faces_own)
                score_ref[p] = full
                masked = jnp.where(own_ref[p, rows] == HUGE, HUGE, full)
            costs.append(cost_of(masked))
            wide = jnp.concatenate(
                [pltpu.roll(h, (2 - 2 * g) % LANES, 1) for g in range(size_y // 8)], axis=0
            )
            turned.append(jnp.where(border, masked, wide))
    away = jnp.where(first, float(size_x), -float(size_x))
    lines = []
    for i in range(size_x):
        best = costs[i]
        for j in range(size_x):
            if j != i:
                best = jnp.minimum(best, costs[j] + float((i - j) ** 2))
            d = float(j - i) + away
            best = jnp.minimum(best, costs[size_x + j] + d * d)
        lines.append(best)
    zm_ref[0:LANES, :] = jnp.concatenate(lines, axis=0).T
    width = size_x * size_y
    ends = jnp.concatenate(turned, axis=0).T
    zm_ref[LANES : LANES + 8, :] = jnp.concatenate(
        [ends[r : r + 1, k * width : (k + 1) * width] for r in (0, LANES - 1, 1, 2) for k in range(2)],
        axis=0,
    )


Z_FLOOR = -(LANES + 6)


def sweep(accs, blocks, read, table, shift, low, high):
    parts = len(accs[0])

    def body(j, flat):
        flat = list(flat)
        tiles = read(j)
        squares = table.at[pl.ds(shift + 8 * blocks[0] - 8 * j, 8 * len(blocks))]
        for r in range(8):
            rows = [jnp.broadcast_to(t[r : r + 1, :], (8, LANES)) for t in tiles]
            for i in range(len(blocks)):
                square = squares[8 * i + 7 - r]
                for k in range(parts):
                    at = i * parts + k
                    flat[at] = jnp.minimum(flat[at], rows[k] + square)
        return tuple(flat)

    flat = lax.fori_loop(low, high, body, tuple(v for row in accs for v in row))
    return [list(flat[i * parts : (i + 1) * parts]) for i in range(len(blocks))]


def tiles_of(ref, j):
    rows = pl.ds(pl.multiple_of(8 * j, 8), 8)
    return [ref[rows, k * LANES : (k + 1) * LANES] for k in range(ref.shape[1] // LANES)]


def load_blocks(ref, blocks):
    return [tiles_of(ref, b) for b in blocks]


def save_blocks(ref, blocks, accs):
    for b, row in zip(blocks, accs):
        for k, v in enumerate(row):
            ref[8 * b : 8 * b + 8, k * LANES : (k + 1) * LANES] = v


def z_own_kernel(zm_ref, out_ref, table):
    count, half = LANES // 8, LANES // 16
    s = row_of((8, LANES)).astype(jnp.float32)
    for d in range(Z_FLOOR, LANES):
        v = s + float(d)
        table[d - Z_FLOOR] = v * v

    def read(j):
        at = row_of((8, LANES)) + 8 * j
        hide = (at == 0) | (at == LANES - 1)
        return [jnp.where(hide, HUGE, t) for t in tiles_of(zm_ref, j)]

    for first in (0, half):
        blocks = range(first, first + half)
        accs = [[jnp.full((8, LANES), HUGE, jnp.float32)] * (out_ref.shape[1] // LANES) for _ in blocks]
        save_blocks(out_ref, blocks, sweep(accs, blocks, read, table, -7 - Z_FLOOR, 0, count))


def border_minima(cost, size_x, size_y, partner):
    if not partner:
        return cost
    width = cost.shape[1]
    shape = (8, width)
    row, plane = row_of(shape), lane_of(shape) // size_y
    away = jnp.where(lax.axis_index("gx") == 0, size_x, -size_x)
    shift = jnp.where(row % 2 == 1, away, 0)
    best = None
    for r in range(size_x):
        source = jnp.where(plane >= r, plane - r, plane - r + size_x)
        d = (source + shift - plane).astype(jnp.float32)
        if r == 0:
            moved = cost
        else:
            cut = width - r * size_y
            moved = jnp.concatenate([cost[:, cut:], cost[:, :cut]], axis=1)
        moved = moved + d * d
        best = moved if best is None else jnp.minimum(best, moved)
    return jnp.minimum(best, pltpu.roll(best, 7, 0))


def z_far_kernel(even, partner, size_x, size_y, acc_ref, table, zm_ref, got_ref, out_ref, source, work):
    index, last = lax.axis_index("gz"), lax.axis_size("gz") - 1
    odd = index % 2 == 1
    low = odd if even else jnp.logical_not(odd)
    valid = jnp.where(low, index > 0, index < last)
    count, half = LANES // 8, LANES // 16
    out = out_ref if even else work

    own, got = zm_ref[LANES : LANES + 8, :], got_ref[LANES : LANES + 8, :]
    mine = jnp.where(low, own[0:2], own[2:4]) + jnp.where(valid, jnp.where(low, got[6:8], got[4:6]), 0.0)
    theirs = jnp.where(low, got[2:4] + own[4:6], got[0:2] + own[6:8])
    ends = border_minima(cost_of(jnp.concatenate([mine, theirs, mine, theirs], axis=0)), size_x, size_y, partner)
    source[...] = got_ref[0:LANES, :]

    squares = table.at[pl.ds(jnp.where(low, -Z_FLOOR, 1 - LANES - Z_FLOOR), LANES)]
    lanes = [slice(k * LANES, (k + 1) * LANES) for k in range(zm_ref.shape[1] // LANES)]
    rows = [jnp.broadcast_to(ends[0:1, cols], (8, LANES)) for cols in lanes]
    for b in range(count):
        for row, cols in zip(rows, lanes):
            span = slice(8 * b, 8 * b + 8)
            out[span, cols] = jnp.minimum(acc_ref[span, cols], row + squares[8 * b])

    def slanted(accs, blocks, offset, tiles, reach):
        for j in tiles:
            tile = tiles_of(source, j)
            for r in range(8):
                q = 8 * j + r
                rows = [jnp.broadcast_to(t[r : r + 1, :], (8, LANES)) for t in tile]
                for i, b in enumerate(blocks):
                    if reach(b, q):
                        square = table[8 * b - q + offset - Z_FLOOR]
                        accs[i] = [jnp.minimum(v, row + square) for v, row in zip(accs[i], rows)]
        return accs

    @pl.when(valid & low)
    def _():
        source[LANES - 1 : LANES, :] = ends[2:3]
        for first in (0, half):
            blocks = range(first, first + half)
            accs = load_blocks(out, blocks)
            accs = slanted(accs, blocks, LANES, blocks, lambda b, q: 8 * b < q)
            if blocks[-1] + 1 < count:
                read = functools.partial(tiles_of, source)
                accs = sweep(accs, blocks, read, table, LANES - 7 - Z_FLOOR, blocks[-1] + 1, count)
            save_blocks(out, blocks, accs)

    @pl.when(valid & jnp.logical_not(low))
    def _():
        source[0:1, :] = ends[2:3]
        for first in (0, half):
            blocks = range(first, first + half)
            accs = load_blocks(out, blocks)
            accs = slanted(accs, blocks, -LANES, blocks, lambda b, q: q < 8 * b + 7)
            if first:
                read = functools.partial(tiles_of, source)
                accs = sweep(accs, blocks, read, table, -LANES - 7 - Z_FLOOR, 0, first)
            save_blocks(out, blocks, accs)

    if not even:
        per = LANES // size_y
        for k, cols in enumerate(lanes):
            best = work[:, cols].T
            for i in range(per):
                out_ref[k * per + i] = best[i * size_y : (i + 1) * size_y]


def score_kernel(score_in, even_ref, odd_ref, _, score_ref):
    index, last = lax.axis_index("gz"), lax.axis_size("gz") - 1
    odd = index % 2 == 1
    size_y = score_in.shape[1]
    per = LANES // size_y
    for k in range(even_ref.shape[1] // LANES):
        cols = slice(k * LANES, (k + 1) * LANES)
        even_rows, odd_rows = even_ref[LANES : LANES + 8, cols], odd_ref[LANES : LANES + 8, cols]
        low = jnp.where(index > 0, jnp.where(odd, even_rows, odd_rows)[6:7], 0.0)
        high = jnp.where(index < last, jnp.where(odd, odd_rows, even_rows)[4:5], 0.0)
        middle = jnp.zeros((LANES - 2, LANES), jnp.float32)
        more = jnp.concatenate([low, middle, high], axis=0).T
        for i in range(per):
            x = k * per + i
            score_ref[x] = score_in[x] + more[i * size_y : (i + 1) * size_y]


def y_table(axis, hop, size_y, table):
    index = lax.axis_index(axis)
    away = (((index ^ hop) - index) * size_y).astype(jnp.float32)
    s = row_of((8, LANES)).astype(jnp.float32) - away
    for d in range(1 - size_y, size_y - 7):
        v = s + float(d)
        table[d - (1 - size_y)] = v * v


Y_BLOCKS = 4


def y_sweep(refs, tables, start, out_ref, scale):
    size_x, size_y, _ = out_ref.shape
    for first in range(0, size_y // 8, Y_BLOCKS):
        blocks = range(first, first + Y_BLOCKS)
        accs = []
        for b in blocks:
            span = slice(8 * b, 8 * b + 8)
            blank = jnp.full((8, LANES), HUGE, jnp.float32)
            accs.append([blank if start is None else start[x, span, :] for x in range(size_x)])
        for ref, table in zip(refs, tables):

            def read(j, ref=ref):
                return [ref[x, pl.ds(pl.multiple_of(8 * j, 8), 8), :] for x in range(size_x)]

            accs = sweep(accs, blocks, read, table, size_y - 8, 0, size_y // 8)
        for b, row in zip(blocks, accs):
            for x, v in enumerate(row):
                out_ref[x, 8 * b : 8 * b + 8, :] = v if scale == 1.0 else v * scale


def y_near_kernel(own_ref, chip_ref, out_ref, table_2, table_3, table_0, table_1):
    size_y = own_ref.shape[1]
    for hop, table in enumerate((table_0, table_1, table_2, table_3)):
        y_table("gy", hop, size_y, table)
    y_sweep((own_ref, chip_ref), (table_0, table_1), None, out_ref, 1.0)


def y_far_kernel(scale, start_ref, ref, table, out_ref):
    y_sweep((ref,), (table,), start_ref, out_ref, scale)


def swap(value, axis, hop):
    n = lax.axis_size(axis)
    return lax.ppermute(value, axis, [(i, i ^ hop) for i in range(n)])


def swap_xy(value, hop_x, hop_y):
    nx, ny = lax.axis_size("gx"), lax.axis_size("gy")
    pairs = [(x * ny + y, (x ^ hop_x) * ny + (y ^ hop_y)) for x in range(nx) for y in range(ny)]
    return lax.ppermute(value, ("gx", "gy"), pairs)


def neighbours(low, high, axis, beyond=0.0):
    n, index = lax.axis_size(axis), lax.axis_index(axis)
    odd = index % 2 == 1
    pairs = [(i, i + 1 if i % 2 else i - 1) for i in range(1, n - 1)]
    got_odd = lax.ppermute(jnp.where(odd, high, low), axis, pairs)
    got_even = lax.ppermute(jnp.where(odd, low, high), axis, [(i, i ^ 1) for i in range(n)])
    from_low = jnp.where(odd, got_even, got_odd)
    from_high = jnp.where(odd, got_odd, got_even)
    return jnp.where(index == 0, beyond, from_low), jnp.where(index == n - 1, beyond, from_high)


def z_swaps(value):
    n = lax.axis_size("gz")
    even = lax.ppermute(value, "gz", [(i, i ^ 1) for i in range(n)])
    return even, lax.ppermute(value, "gz", [(i, i + 1 if i % 2 else i - 1) for i in range(1, n - 1)])


def conv(features, conv_weight, mask, planes, count):
    channels, size_x, size_y, _ = features.shape
    return call(
        functools.partial(conv_kernel, planes),
        [(size_x, size_y, LANES), (count, size_y + 8, LANES), (count, 16, LANES)],
        [
            pltpu.VMEM(features.shape, jnp.bfloat16),
            pltpu.VMEM(conv_weight.shape, jnp.bfloat16),
            pltpu.VMEM(mask.shape, jnp.int32),
            pltpu.VMEM((9 * ROWS + 8, channels * 16), jnp.bfloat16),
            pltpu.VMEM((size_x + 2, 3, ROWS, size_y // 16 * LANES), jnp.float32),
            pltpu.SemaphoreType.DMA((size_x + 2,)),
        ],
        mib=24,
        in_specs=[HBM] * 3,
    )(*(pltpu.with_memory_space_constraint(v, pltpu.HBM) for v in (features, conv_weight, mask)))


def halo_with_partner(features, conv_weight, mask):
    _, size_x, size_y, _ = features.shape

    def planes():
        return [*range(1, size_x + 1), jnp.where(lax.axis_index("gx") == 0, size_x + 1, 0)]

    s, own, e = conv(features, conv_weight, mask, planes, size_x + 1)
    far = swap_xy(own, 1, 0)
    sides = [swap_xy(e, x, y) for x in range(2) for y in (1, 3)]
    return call(turn_kernel, [(size_x, size_y, LANES), (LANES + 8, size_x * size_y)])(s, own, far, *sides)


def halo_in_rounds(features, conv_weight, mask):
    _, size_x, size_y, _ = features.shape
    groups = size_y // 8
    planes = [*range(1, size_x + 1), 0, size_x + 1]
    s, rest, e = conv(features, conv_weight, mask, lambda: planes, size_x + 2)
    whole = jnp.concatenate([rest.at[:size_x, :size_y].set(s), e], axis=1)
    low, high = neighbours(whole[size_x], whole[size_x + 1], "gx")
    whole = whole[:size_x].at[0].add(low).at[size_x - 1].add(high)
    e = whole[:, size_y + 8 :]
    low, high = neighbours(e, e, "gy")
    whole = whole.at[:, 0].add(low[:, 0]).at[:, size_y - 1].add(high[:, 7])
    whole = whole.at[:, size_y].add(low[:, 8]).at[:, size_y + 7].add(high[:, 15])
    score, h = whole[:, :size_y], whole[:, size_y : size_y + 8]

    def line(value):
        return value.reshape(1, size_x * size_y)

    up = jnp.swapaxes(h[:, :, 0 : 2 * groups : 2], 1, 2)
    down = jnp.swapaxes(jnp.roll(h, 1, 2)[:, :, 0 : 2 * groups : 2], 1, 2)
    masked = jnp.where(mask == 1, HUGE, score)
    rows = jnp.transpose(cost_of(masked), (2, 0, 1)).reshape(LANES, size_x * size_y)
    ends = [line(v) for v in (masked[:, :, 0], masked[:, :, LANES - 1], down, up)]
    blank = [jnp.full_like(ends[0], HUGE)] * 2 + [jnp.zeros_like(ends[0])] * 2
    pairs = [v for pair in zip(ends, blank) for v in pair]
    return score, jnp.concatenate([rows, *pairs], axis=0)


def x_minima(value, size_x):
    n, index = lax.axis_size("gx"), lax.axis_index("gx")
    every = lax.all_gather(value, "gx", axis=0, tiled=True)
    at = index * size_x + jnp.arange(size_x)
    d = (at[:, None] - jnp.arange(n * size_x)[None, :]).astype(jnp.float32)
    return jnp.min(every[None] + (d * d)[:, :, None, None], axis=1)


def shards(features, conv_weight, mask):
    _, size_x, size_y, size_z = features.shape
    gx, gy = lax.axis_size("gx"), lax.axis_size("gy")
    assert size_z == LANES and size_y % 16 == 0 and LANES % size_y == 0 and gy == 4
    brick = (size_x, size_y, LANES)
    lines = size_x * size_y
    partner = gx == 2

    halo = halo_with_partner if partner else halo_in_rounds
    score, zm = halo(features, conv_weight, mask)

    even, odd = z_swaps(zm)
    best, table = call(z_own_kernel, [(LANES, lines), (LANES - Z_FLOOR, 8, LANES)])(zm)
    work = [pltpu.VMEM((LANES, lines), jnp.float32)] * 2
    for first, got, shape in ((True, even, (LANES, lines)), (False, odd, brick)):
        far = functools.partial(z_far_kernel, first, partner, size_x, size_y)
        (best,) = call(far, [shape], work)(best, table, zm, got)
    (score,) = call(score_kernel, [brick])(score, even, odd, best)
    if not partner:
        best = x_minima(best, size_x)

    tables = (2 * size_y - 8, 8, LANES)
    chip, across = swap(best, "gy", 1), swap(best, "gy", 2)
    near, table_2, table_3 = call(
        y_near_kernel, [brick, tables, tables], [pltpu.VMEM(tables, jnp.float32)] * 2
    )(best, chip)
    across, near = lax.optimization_barrier((across, near))
    forward = swap(across, "gy", 1)
    (near,) = call(functools.partial(y_far_kernel, 1.0), [brick])(near, across, table_2)
    (depth,) = call(functools.partial(y_far_kernel, 1.0 / RADIUS), [brick])(near, forward, table_3)
    return score, depth


def solution(mesh):
    in_specs = (P(None, "gx", "gy", "gz"), P(), P("gx", "gy", "gz"))
    out_specs = (P("gx", "gy", "gz"), P("gx", "gy", "gz"))
    return jax.shard_map(shards, mesh=mesh, in_specs=in_specs, out_specs=out_specs, check_vma=False)
```

```python
import functools

import jax
import jax.numpy as jnp
from jax import lax
from jax.experimental import pallas as pl
from jax.experimental.pallas import tpu as pltpu
from jax.sharding import PartitionSpec as P

RADIUS = 128
CEILING = float(RADIUS * RADIUS)
HUGE = 1e30
LANES = 128
ROWS = 24
VMEM = pl.BlockSpec(memory_space=pltpu.VMEM)
HBM = pl.BlockSpec(memory_space=pltpu.HBM)


def call(kernel, outs, scratch=(), mib=8, in_specs=None):
    shapes = [jax.ShapeDtypeStruct(s, jnp.float32) for s in outs]

    def run(*args):
        return pl.pallas_call(
            kernel,
            out_shape=shapes,
            in_specs=in_specs or [VMEM] * len(args),
            out_specs=[VMEM] * len(shapes),
            scratch_shapes=list(scratch),
            compiler_params=pltpu.CompilerParams(vmem_limit_bytes=mib * 1024 * 1024),
        )(*args)

    return run


def lane_of(shape):
    return lax.broadcasted_iota(jnp.int32, shape, len(shape) - 1)


def row_of(shape):
    return lax.broadcasted_iota(jnp.int32, shape, len(shape) - 2)


def cost_of(score):
    return CEILING / (1.0 + jnp.exp(-score))


def conv_kernel(
    planes, paired, f_hbm, w_hbm, mask_hbm, s_ref, m_ref, e_ref, d_ref, f_vmem, w_vmem, mask_vmem, w_big, acc, sems
):
    channels, size_x, size_y, _ = f_vmem.shape
    tiles = size_y // 16
    depth = channels * 16
    weights = pltpu.make_async_copy(w_hbm, w_vmem, sems.at[size_x])
    weights.start()
    copies = [
        pltpu.make_async_copy(f_hbm.at[:, x], f_vmem.at[:, x], sems.at[x]) for x in range(size_x)
    ]
    masks = pltpu.make_async_copy(mask_hbm, mask_vmem, sems.at[size_x + 1])
    masks.start()
    for copy in copies:
        copy.start()

    acc[...] = jnp.zeros_like(acc)
    spread = (
        lax.broadcasted_iota(jnp.int32, (channels, depth), 1) // 16
        == lax.broadcasted_iota(jnp.int32, (channels, depth), 0)
    ).astype(jnp.bfloat16)
    row = lax.broadcasted_iota(jnp.int32, (ROWS, depth), 0)
    y_in = lax.broadcasted_iota(jnp.int32, (ROWS, depth), 1) % 16
    y_out = jnp.where(row <= 16, row, jnp.where(row == ROWS - 1, -1, 64))
    tap = y_in - y_out + 1
    weights.wait()
    wide = jnp.dot(w_vmem[...], spread, preferred_element_type=jnp.float32)
    blocks = []
    for a in range(3):
        for c in range(3):
            block = jnp.zeros((ROWS, depth), jnp.float32)
            for b in range(3):
                k = 9 * a + 3 * b + c
                block = jnp.where(tap == b, wide[k : k + 1, :], block)
            blocks.append(block)
    blocks.append(jnp.zeros((8, depth), jnp.float32))
    w_big[...] = jnp.concatenate(blocks, axis=0).astype(jnp.bfloat16)

    shape = (8, LANES)
    row, lane = row_of(shape), lane_of(shape)
    groups = size_y // 8
    to_first = lax.axis_index("gy") % 2 == 1 if paired else True
    folds = []

    def finish(p, at):
        fold = None
        for g in range(groups + 1):
            sums = []
            for c in range(3):

                def piece(tile, low, c=c):
                    return acc[at, c, low : low + 8, tile * LANES : tile * LANES + LANES]

                if g == groups:
                    part = jnp.where(row == 0, piece(tiles - 1, 16), piece(0, 16))
                else:
                    tile, low = g // 2, 8 * (g % 2)
                    part = piece(tile, low)
                    if low == 0 and tile > 0:
                        part = part + jnp.where(row == 0, piece(tile - 1, 16), 0.0)
                    if low == 8 and tile < tiles - 1:
                        part = part + jnp.where(row == 7, piece(tile + 1, 16), 0.0)
                sums.append(part)
            ahead = pltpu.roll(sums[0], 1, 1)
            behind = pltpu.roll(sums[2], LANES - 1, 1)
            inner = (
                sums[1] + jnp.where(lane == 0, 0.0, ahead) + jnp.where(lane == LANES - 1, 0.0, behind)
            )
            outer = jnp.where(lane == 0, ahead, jnp.where(lane == LANES - 1, behind, 0.0))
            if g == groups:
                for up, down, at_row in (
                    (inner, inner, p),
                    (outer, pltpu.roll(outer, 2 * (groups - 1), 1), 8 + p),
                ):
                    e_ref[at_row : at_row + 1, :] = jnp.where(to_first, down[7:8], up[0:1])
                    d_ref[at_row : at_row + 1, :] = jnp.where(to_first, up[0:1], down[7:8])
            else:
                span = slice(8 * g, 8 * g + 8)
                if p < size_x:
                    s_ref[p, span, :] = inner
                    inner = jnp.where(mask_vmem[p, span, :] == 1, HUGE, inner)
                m_ref[p * size_y + 8 * g : p * size_y + 8 * g + 8, :] = inner
                shift = 16 * p + 2 * g
                outer = pltpu.roll(outer, shift, 1) if shift else outer
                fold = outer if g == 0 else fold + outer
        folds.append(fold)

    for x in range(size_x):
        copies[x].wait()
        right = jnp.concatenate(
            [f_vmem[:, x, 16 * t : 16 * t + 16, :].reshape(depth, LANES) for t in range(tiles)],
            axis=1,
        )
        got = jnp.dot(w_big[...], right, preferred_element_type=jnp.float32)
        for a in range(3):
            at = x + 2 - a
            for c in range(3):
                first = (3 * a + c) * ROWS
                acc[at, c] = acc[at, c] + got[first : first + ROWS, :]
    masks.wait()
    for p, at in enumerate(planes()):
        finish(p, at)
    m_ref[len(folds) * size_y :, :] = functools.reduce(jnp.add, folds)


def y_masks(axis, chip):
    row = row_of((8, LANES))
    index, last = lax.axis_index(axis), lax.axis_size(axis) - 1
    odd = index % 2
    if chip:
        low, high = odd == 1, odd == 0
    else:
        low, high = (odd == 0) & (index > 0), (odd == 1) & (index < last)
    return row == jnp.where(low, 0, -1), row == jnp.where(high, 7, -1)


def edge_rows(masks, part, size_y):
    low, high = masks
    return jnp.concatenate(
        [
            jnp.where(low, part, 0.0),
            jnp.zeros((size_y - 16, LANES), jnp.float32),
            jnp.where(high, part, 0.0),
        ],
        axis=0,
    )


def turn_kernel(s_ref, own_ref, far_ref, chip_ref, cross_ref, xchip_ref, xcross_ref, score_ref, zm_ref):
    size_x, size_y, _ = s_ref.shape
    chip, cross = y_masks("gy", True), y_masks("gy", False)
    first = lax.axis_index("gx") == 0
    lane = lane_of((size_y, LANES))
    border = (lane == 0) | (lane == LANES - 1)
    faces_own = {size_x - 1: jnp.where(first, 1.0, 0.0), 0: jnp.where(first, 0.0, 1.0)}
    faces_far = {0: faces_own[size_x - 1], size_x - 1: faces_own[0]}

    def plane(ref, p):
        return ref[p * size_y : (p + 1) * size_y, :]

    def fold(ref, p):
        rest = ref[(size_x + 1) * size_y :, :]
        return pltpu.roll(rest, LANES - 16 * p, 1) if p else rest

    def complete(p, base, folded, face_ref, sides, faces):
        if p in faces:
            base = base + faces[p] * plane(face_ref, size_x)
            folded = folded + faces[p] * fold(face_ref, size_x)
        for masks, same, other in sides:
            part, part_h = same[p : p + 1], same[8 + p : 9 + p]
            if p in faces:
                part = part + faces[p] * other[size_x : size_x + 1]
                part_h = part_h + faces[p] * other[8 + size_x : 9 + size_x]
            base = base + edge_rows(masks, part, size_y)
            folded = folded + jnp.where(masks[0] | masks[1], part_h, 0.0)
        return base, folded

    costs, turned = [], []
    for far in range(2):
        for p in range(size_x):
            if far:
                sides = ((chip, xchip_ref, chip_ref), (cross, xcross_ref, cross_ref))
                masked, h = complete(p, plane(far_ref, p), fold(far_ref, p), own_ref, sides, faces_far)
            else:
                sides = ((chip, chip_ref, xchip_ref), (cross, cross_ref, xcross_ref))
                full, h = complete(p, s_ref[p], fold(own_ref, p), far_ref, sides, faces_own)
                score_ref[p] = full
                masked = jnp.where(plane(own_ref, p) == HUGE, HUGE, full)
            costs.append(cost_of(masked))
            wide = jnp.concatenate(
                [pltpu.roll(h, (2 - 2 * g) % LANES, 1) for g in range(size_y // 8)], axis=0
            )
            turned.append(jnp.where(border, masked, wide))
    away = jnp.where(first, float(size_x), -float(size_x))
    lines = []
    for i in range(size_x):
        best = costs[i]
        for j in range(size_x):
            if j != i:
                best = jnp.minimum(best, costs[j] + float((i - j) ** 2))
            d = float(j - i) + away
            best = jnp.minimum(best, costs[size_x + j] + d * d)
        lines.append(best)
    zm_ref[0:LANES, :] = jnp.concatenate(lines, axis=0).T
    width = size_x * size_y
    ends = jnp.concatenate(turned, axis=0).T
    zm_ref[LANES : LANES + 8, :] = jnp.concatenate(
        [ends[r : r + 1, k * width : (k + 1) * width] for r in (0, LANES - 1, 1, 2) for k in range(2)],
        axis=0,
    )


Z_FLOOR = -(LANES + 6)


def sweep(accs, blocks, read, table, shift, low, high):
    parts = len(accs[0])

    def body(j, flat):
        flat = list(flat)
        tiles = read(j)
        squares = table.at[pl.ds(shift + 8 * blocks[0] - 8 * j, 8 * len(blocks))]
        for r in range(8):
            rows = [jnp.broadcast_to(t[r : r + 1, :], (8, LANES)) for t in tiles]
            for i in range(len(blocks)):
                square = squares[8 * i + 7 - r]
                for k in range(parts):
                    at = i * parts + k
                    flat[at] = jnp.minimum(flat[at], rows[k] + square)
        return tuple(flat)

    flat = lax.fori_loop(low, high, body, tuple(v for row in accs for v in row))
    return [list(flat[i * parts : (i + 1) * parts]) for i in range(len(blocks))]


def tiles_of(ref, j):
    rows = pl.ds(pl.multiple_of(8 * j, 8), 8)
    return [ref[rows, k * LANES : (k + 1) * LANES] for k in range(ref.shape[1] // LANES)]


def load_blocks(ref, blocks):
    return [tiles_of(ref, b) for b in blocks]


def save_blocks(ref, blocks, accs):
    for b, row in zip(blocks, accs):
        for k, v in enumerate(row):
            ref[8 * b : 8 * b + 8, k * LANES : (k + 1) * LANES] = v


def z_own_kernel(zm_ref, out_ref, table):
    count, half = LANES // 8, LANES // 16
    s = row_of((8, LANES)).astype(jnp.float32)
    for d in range(Z_FLOOR, LANES):
        v = s + float(d)
        table[d - Z_FLOOR] = v * v

    def read(j):
        at = row_of((8, LANES)) + 8 * j
        hide = (at == 0) | (at == LANES - 1)
        return [jnp.where(hide, HUGE, t) for t in tiles_of(zm_ref, j)]

    for first in (0, half):
        blocks = range(first, first + half)
        accs = [[jnp.full((8, LANES), HUGE, jnp.float32)] * (out_ref.shape[1] // LANES) for _ in blocks]
        save_blocks(out_ref, blocks, sweep(accs, blocks, read, table, -7 - Z_FLOOR, 0, count))


def border_minima(cost, size_x, size_y, partner):
    if not partner:
        return cost
    width = cost.shape[1]
    shape = (8, width)
    row, plane = row_of(shape), lane_of(shape) // size_y
    away = jnp.where(lax.axis_index("gx") == 0, size_x, -size_x)
    shift = jnp.where(row % 2 == 1, away, 0)
    best = None
    for r in range(size_x):
        source = jnp.where(plane >= r, plane - r, plane - r + size_x)
        d = (source + shift - plane).astype(jnp.float32)
        if r == 0:
            moved = cost
        else:
            cut = width - r * size_y
            moved = jnp.concatenate([cost[:, cut:], cost[:, :cut]], axis=1)
        moved = moved + d * d
        best = moved if best is None else jnp.minimum(best, moved)
    return jnp.minimum(best, pltpu.roll(best, 7, 0))


def z_far_kernel(even, partner, size_x, size_y, acc_ref, table, zm_ref, got_ref, out_ref, source, work):
    index, last = lax.axis_index("gz"), lax.axis_size("gz") - 1
    odd = index % 2 == 1
    low = odd if even else jnp.logical_not(odd)
    valid = jnp.where(low, index > 0, index < last)
    count, half = LANES // 8, LANES // 16
    out = out_ref if even else work

    own, got = zm_ref[LANES : LANES + 8, :], got_ref[LANES : LANES + 8, :]
    mine = jnp.where(low, own[0:2], own[2:4]) + jnp.where(valid, jnp.where(low, got[6:8], got[4:6]), 0.0)
    theirs = jnp.where(low, got[2:4] + own[4:6], got[0:2] + own[6:8])
    ends = border_minima(cost_of(jnp.concatenate([mine, theirs, mine, theirs], axis=0)), size_x, size_y, partner)
    source[...] = got_ref[0:LANES, :]

    squares = table.at[pl.ds(jnp.where(low, -Z_FLOOR, 1 - LANES - Z_FLOOR), LANES)]
    lanes = [slice(k * LANES, (k + 1) * LANES) for k in range(zm_ref.shape[1] // LANES)]
    rows = [jnp.broadcast_to(ends[0:1, cols], (8, LANES)) for cols in lanes]
    for b in range(count):
        for row, cols in zip(rows, lanes):
            span = slice(8 * b, 8 * b + 8)
            out[span, cols] = jnp.minimum(acc_ref[span, cols], row + squares[8 * b])

    def slanted(accs, blocks, offset, tiles, reach):
        for j in tiles:
            tile = tiles_of(source, j)
            for r in range(8):
                q = 8 * j + r
                rows = [jnp.broadcast_to(t[r : r + 1, :], (8, LANES)) for t in tile]
                for i, b in enumerate(blocks):
                    if reach(b, q):
                        square = table[8 * b - q + offset - Z_FLOOR]
                        accs[i] = [jnp.minimum(v, row + square) for v, row in zip(accs[i], rows)]
        return accs

    @pl.when(valid & low)
    def _():
        source[LANES - 1 : LANES, :] = ends[2:3]
        for first in (0, half):
            blocks = range(first, first + half)
            accs = load_blocks(out, blocks)
            accs = slanted(accs, blocks, LANES, blocks, lambda b, q: 8 * b < q)
            if blocks[-1] + 1 < count:
                read = functools.partial(tiles_of, source)
                accs = sweep(accs, blocks, read, table, LANES - 7 - Z_FLOOR, blocks[-1] + 1, count)
            save_blocks(out, blocks, accs)

    @pl.when(valid & jnp.logical_not(low))
    def _():
        source[0:1, :] = ends[2:3]
        for first in (0, half):
            blocks = range(first, first + half)
            accs = load_blocks(out, blocks)
            accs = slanted(accs, blocks, -LANES, blocks, lambda b, q: q < 8 * b + 7)
            if first:
                read = functools.partial(tiles_of, source)
                accs = sweep(accs, blocks, read, table, -LANES - 7 - Z_FLOOR, 0, first)
            save_blocks(out, blocks, accs)

    if not even:
        per = LANES // size_y
        for k, cols in enumerate(lanes):
            best = work[:, cols].T
            for i in range(per):
                out_ref[k * per + i] = best[i * size_y : (i + 1) * size_y]


def score_kernel(score_in, even_ref, odd_ref, _, score_ref):
    index, last = lax.axis_index("gz"), lax.axis_size("gz") - 1
    odd = index % 2 == 1
    size_y = score_in.shape[1]
    per = LANES // size_y
    for k in range(even_ref.shape[1] // LANES):
        cols = slice(k * LANES, (k + 1) * LANES)
        even_rows, odd_rows = even_ref[LANES : LANES + 8, cols], odd_ref[LANES : LANES + 8, cols]
        low = jnp.where(index > 0, jnp.where(odd, even_rows, odd_rows)[6:7], 0.0)
        high = jnp.where(index < last, jnp.where(odd, odd_rows, even_rows)[4:5], 0.0)
        middle = jnp.zeros((LANES - 2, LANES), jnp.float32)
        more = jnp.concatenate([low, middle, high], axis=0).T
        for i in range(per):
            x = k * per + i
            score_ref[x] = score_in[x] + more[i * size_y : (i + 1) * size_y]


def y_table(axis, hop, size_y, table):
    index = lax.axis_index(axis)
    away = (((index ^ hop) - index) * size_y).astype(jnp.float32)
    s = row_of((8, LANES)).astype(jnp.float32) - away
    for d in range(1 - size_y, size_y - 7):
        v = s + float(d)
        table[d - (1 - size_y)] = v * v


Y_BLOCKS = 4


def y_sweep(refs, tables, start, out_ref, scale):
    size_x, size_y, _ = out_ref.shape
    for first in range(0, size_y // 8, Y_BLOCKS):
        blocks = range(first, first + Y_BLOCKS)
        accs = []
        for b in blocks:
            span = slice(8 * b, 8 * b + 8)
            blank = jnp.full((8, LANES), HUGE, jnp.float32)
            accs.append([blank if start is None else start[x, span, :] for x in range(size_x)])
        for ref, table in zip(refs, tables):

            def read(j, ref=ref):
                return [ref[x, pl.ds(pl.multiple_of(8 * j, 8), 8), :] for x in range(size_x)]

            accs = sweep(accs, blocks, read, table, size_y - 8, 0, size_y // 8)
        for b, row in zip(blocks, accs):
            for x, v in enumerate(row):
                out_ref[x, 8 * b : 8 * b + 8, :] = v if scale == 1.0 else v * scale


def y_own_kernel(own_ref, out_ref, table_1, table_2, table_3, table_0):
    size_y = own_ref.shape[1]
    for hop, table in enumerate((table_0, table_1, table_2, table_3)):
        y_table("gy", hop, size_y, table)
    y_sweep((own_ref,), (table_0,), None, out_ref, 1.0)


def y_far_kernel(hop, scale, start_ref, ref, table, out_ref):
    index = lax.axis_index("gy")
    if hop < 3:
        y_sweep((ref,), (table,), start_ref, out_ref, scale)
        return
    near = jnp.abs((index ^ hop) - index) < 3

    @pl.when(near)
    def _():
        y_sweep((ref,), (table,), start_ref, out_ref, scale)

    @pl.when(jnp.logical_not(near))
    def _():
        out_ref[...] = start_ref[...] * scale


def swap(value, axis, hop):
    n = lax.axis_size(axis)
    return lax.ppermute(value, axis, [(i, i ^ hop) for i in range(n)])


def swap_xy(value, hop_x, hop_y):
    nx, ny = lax.axis_size("gx"), lax.axis_size("gy")
    pairs = [(x * ny + y, (x ^ hop_x) * ny + (y ^ hop_y)) for x in range(nx) for y in range(ny)]
    return lax.ppermute(value, ("gx", "gy"), pairs)


def neighbours(low, high, axis, beyond=0.0):
    n, index = lax.axis_size(axis), lax.axis_index(axis)
    odd = index % 2 == 1
    pairs = [(i, i + 1 if i % 2 else i - 1) for i in range(1, n - 1)]
    got_odd = lax.ppermute(jnp.where(odd, high, low), axis, pairs)
    got_even = lax.ppermute(jnp.where(odd, low, high), axis, [(i, i ^ 1) for i in range(n)])
    from_low = jnp.where(odd, got_even, got_odd)
    from_high = jnp.where(odd, got_odd, got_even)
    return jnp.where(index == 0, beyond, from_low), jnp.where(index == n - 1, beyond, from_high)


def z_swaps(value):
    n = lax.axis_size("gz")
    even = lax.ppermute(value, "gz", [(i, i ^ 1) for i in range(n)])
    return even, lax.ppermute(value, "gz", [(i, i + 1 if i % 2 else i - 1) for i in range(1, n - 1)])


def conv(features, conv_weight, mask, planes, count, paired):
    channels, size_x, size_y, _ = features.shape
    return call(
        functools.partial(conv_kernel, planes, paired),
        [(size_x, size_y, LANES), (count * size_y + 8, LANES), (16, LANES), (16, LANES)],
        [
            pltpu.VMEM(features.shape, jnp.bfloat16),
            pltpu.VMEM(conv_weight.shape, jnp.bfloat16),
            pltpu.VMEM(mask.shape, jnp.int32),
            pltpu.VMEM((9 * ROWS + 8, channels * 16), jnp.bfloat16),
            pltpu.VMEM((size_x + 2, 3, ROWS, size_y // 16 * LANES), jnp.float32),
            pltpu.SemaphoreType.DMA((size_x + 2,)),
        ],
        mib=24,
        in_specs=[HBM] * 3,
    )(*(pltpu.with_memory_space_constraint(v, pltpu.HBM) for v in (features, conv_weight, mask)))


def halo_with_partner(features, conv_weight, mask):
    _, size_x, size_y, _ = features.shape

    def planes():
        return [*range(1, size_x + 1), jnp.where(lax.axis_index("gx") == 0, size_x + 1, 0)]

    s, own, chip, cross = conv(features, conv_weight, mask, planes, size_x + 1, True)
    far = swap_xy(own, 1, 0)
    sides = [swap_xy(v, x, y) for x in range(2) for v, y in ((chip, 1), (cross, 3))]
    return call(turn_kernel, [(size_x, size_y, LANES), (LANES + 8, size_x * size_y)])(s, own, far, *sides)


def halo_in_rounds(features, conv_weight, mask):
    _, size_x, size_y, _ = features.shape
    groups = size_y // 8
    planes = [*range(1, size_x + 1), 0, size_x + 1]
    s, rest, down, up = conv(features, conv_weight, mask, lambda: planes, size_x + 2, False)

    def whole(k):
        h = jnp.roll(rest[len(planes) * size_y :], -16 * k, 1)
        part = s[k] if k < size_x else rest[k * size_y : (k + 1) * size_y]
        return jnp.concatenate([part, h, *(e[i : i + 1] for e in (down, up) for i in (k, 8 + k))], axis=0)

    low, high = neighbours(whole(size_x), whole(size_x + 1), "gx")
    own = jnp.stack([whole(k) for k in range(size_x)]).at[0].add(low).at[size_x - 1].add(high)
    e = own[:, size_y + 8 :]
    low, high = neighbours(e[:, 0:2], e[:, 2:4], "gy")
    own = own.at[:, 0].add(low[:, 0]).at[:, size_y - 1].add(high[:, 0])
    own = own.at[:, size_y].add(low[:, 1]).at[:, size_y + 7].add(high[:, 1])
    score, h = own[:, :size_y], own[:, size_y : size_y + 8]

    def line(value):
        return value.reshape(1, size_x * size_y)

    up = jnp.swapaxes(h[:, :, 0 : 2 * groups : 2], 1, 2)
    down = jnp.swapaxes(jnp.roll(h, 1, 2)[:, :, 0 : 2 * groups : 2], 1, 2)
    masked = jnp.where(mask == 1, HUGE, score)
    rows = jnp.transpose(cost_of(masked), (2, 0, 1)).reshape(LANES, size_x * size_y)
    ends = [line(v) for v in (masked[:, :, 0], masked[:, :, LANES - 1], down, up)]
    blank = [jnp.full_like(ends[0], HUGE)] * 2 + [jnp.zeros_like(ends[0])] * 2
    pairs = [v for pair in zip(ends, blank) for v in pair]
    return score, jnp.concatenate([rows, *pairs], axis=0)


def x_minima(value, size_x):
    n, index = lax.axis_size("gx"), lax.axis_index("gx")
    every = lax.all_gather(value, "gx", axis=0, tiled=True)
    at = index * size_x + jnp.arange(size_x)
    d = (at[:, None] - jnp.arange(n * size_x)[None, :]).astype(jnp.float32)
    return jnp.min(every[None] + (d * d)[:, :, None, None], axis=1)


def shards(features, conv_weight, mask):
    _, size_x, size_y, size_z = features.shape
    gx, gy = lax.axis_size("gx"), lax.axis_size("gy")
    assert size_z == LANES and size_y % 16 == 0 and LANES % size_y == 0 and gy == 4
    brick = (size_x, size_y, LANES)
    lines = size_x * size_y
    partner = gx == 2

    halo = halo_with_partner if partner else halo_in_rounds
    score, zm = halo(features, conv_weight, mask)

    even, odd = z_swaps(zm)
    best, table = call(z_own_kernel, [(LANES, lines), (LANES - Z_FLOOR, 8, LANES)])(zm)
    work = [pltpu.VMEM((LANES, lines), jnp.float32)] * 2
    for first, got, shape in ((True, even, (LANES, lines)), (False, odd, brick)):
        far = functools.partial(z_far_kernel, first, partner, size_x, size_y)
        (best,) = call(far, [shape], work)(best, table, zm, got)
    (score,) = call(score_kernel, [brick])(score, even, odd, best)
    if not partner:
        best = x_minima(best, size_x)

    tables = (2 * size_y - 8, 8, LANES)
    across, chip = swap(best, "gy", 2), swap(best, "gy", 1)
    near, *kept = call(y_own_kernel, [brick, tables, tables, tables], [pltpu.VMEM(tables, jnp.float32)])(best)
    blocks = {2: across, 1: chip, 3: lax.ppermute(best, "gy", [(1, 2), (2, 1)])}
    for hop, block in blocks.items():
        far = functools.partial(y_far_kernel, hop, 1.0 / RADIUS if hop == 3 else 1.0)
        (near,) = call(far, [brick])(near, block, kept[hop - 1])
    return score, near


def solution(mesh):
    in_specs = (P(None, "gx", "gy", "gz"), P(), P("gx", "gy", "gz"))
    out_specs = (P("gx", "gy", "gz"), P("gx", "gy", "gz"))
    return jax.shard_map(shards, mesh=mesh, in_specs=in_specs, out_specs=out_specs, check_vma=False)
```

```python
import functools

import jax
import jax.numpy as jnp
from jax import lax
from jax.experimental import pallas as pl
from jax.experimental.pallas import tpu as pltpu
from jax.sharding import PartitionSpec as P

RADIUS = 128
CEILING = float(RADIUS * RADIUS)
HUGE = 1e30
LANES = 128
ROWS = 24
VMEM = pl.BlockSpec(memory_space=pltpu.VMEM)
HBM = pl.BlockSpec(memory_space=pltpu.HBM)


def call(kernel, outs, scratch=(), mib=8, in_specs=None):
    shapes = [jax.ShapeDtypeStruct(s, jnp.float32) for s in outs]

    def run(*args):
        return pl.pallas_call(
            kernel,
            out_shape=shapes,
            in_specs=in_specs or [VMEM] * len(args),
            out_specs=[VMEM] * len(shapes),
            scratch_shapes=list(scratch),
            compiler_params=pltpu.CompilerParams(vmem_limit_bytes=mib * 1024 * 1024),
        )(*args)

    return run


def lane_of(shape):
    return lax.broadcasted_iota(jnp.int32, shape, len(shape) - 1)


def row_of(shape):
    return lax.broadcasted_iota(jnp.int32, shape, len(shape) - 2)


def cost_of(score):
    return CEILING / (1.0 + jnp.exp(-score))


def conv_kernel(
    planes, paired, f_hbm, w_hbm, mask_hbm, s_ref, m_ref, e_ref, d_ref, f_vmem, w_vmem, mask_vmem, w_big, acc, sems
):
    channels, size_x, size_y, _ = f_vmem.shape
    tiles = size_y // 16
    depth = channels * 16
    weights = pltpu.make_async_copy(w_hbm, w_vmem, sems.at[size_x])
    weights.start()
    copies = [
        pltpu.make_async_copy(f_hbm.at[:, x], f_vmem.at[:, x], sems.at[x]) for x in range(size_x)
    ]
    masks = pltpu.make_async_copy(mask_hbm, mask_vmem, sems.at[size_x + 1])
    masks.start()
    for copy in copies:
        copy.start()

    acc[...] = jnp.zeros_like(acc)
    spread = (
        lax.broadcasted_iota(jnp.int32, (channels, depth), 1) // 16
        == lax.broadcasted_iota(jnp.int32, (channels, depth), 0)
    ).astype(jnp.bfloat16)
    row = lax.broadcasted_iota(jnp.int32, (ROWS, depth), 0)
    y_in = lax.broadcasted_iota(jnp.int32, (ROWS, depth), 1) % 16
    y_out = jnp.where(row <= 16, row, jnp.where(row == ROWS - 1, -1, 64))
    tap = y_in - y_out + 1
    weights.wait()
    wide = jnp.dot(w_vmem[...], spread, preferred_element_type=jnp.float32)
    blocks = []
    for a in range(3):
        for c in range(3):
            block = jnp.zeros((ROWS, depth), jnp.float32)
            for b in range(3):
                k = 9 * a + 3 * b + c
                block = jnp.where(tap == b, wide[k : k + 1, :], block)
            blocks.append(block)
    blocks.append(jnp.zeros((8, depth), jnp.float32))
    w_big[...] = jnp.concatenate(blocks, axis=0).astype(jnp.bfloat16)

    shape = (8, LANES)
    row, lane = row_of(shape), lane_of(shape)
    groups = size_y // 8
    to_first = lax.axis_index("gy") % 2 == 1 if paired else True
    folds = []

    def finish(p, at):
        fold = None
        for g in range(groups + 1):
            sums = []
            for c in range(3):

                def piece(tile, low, c=c):
                    return acc[at, c, low : low + 8, tile * LANES : tile * LANES + LANES]

                if g == groups:
                    part = jnp.where(row == 0, piece(tiles - 1, 16), piece(0, 16))
                else:
                    tile, low = g // 2, 8 * (g % 2)
                    part = piece(tile, low)
                    if low == 0 and tile > 0:
                        part = part + jnp.where(row == 0, piece(tile - 1, 16), 0.0)
                    if low == 8 and tile < tiles - 1:
                        part = part + jnp.where(row == 7, piece(tile + 1, 16), 0.0)
                sums.append(part)
            ahead = pltpu.roll(sums[0], 1, 1)
            behind = pltpu.roll(sums[2], LANES - 1, 1)
            inner = (
                sums[1] + jnp.where(lane == 0, 0.0, ahead) + jnp.where(lane == LANES - 1, 0.0, behind)
            )
            outer = jnp.where(lane == 0, ahead, jnp.where(lane == LANES - 1, behind, 0.0))
            if g == groups:
                for up, down, at_row in (
                    (inner, inner, p),
                    (outer, pltpu.roll(outer, 2 * (groups - 1), 1), 8 + p),
                ):
                    e_ref[at_row : at_row + 1, :] = jnp.where(to_first, down[7:8], up[0:1])
                    d_ref[at_row : at_row + 1, :] = jnp.where(to_first, up[0:1], down[7:8])
            else:
                span = slice(8 * g, 8 * g + 8)
                if p < size_x:
                    s_ref[p, span, :] = inner
                    inner = jnp.where(mask_vmem[p, span, :] == 1, HUGE, inner)
                m_ref[p * size_y + 8 * g : p * size_y + 8 * g + 8, :] = inner
                shift = 16 * p + 2 * g
                outer = pltpu.roll(outer, shift, 1) if shift else outer
                fold = outer if g == 0 else fold + outer
        folds.append(fold)

    for x in range(size_x):
        copies[x].wait()
        right = jnp.concatenate(
            [f_vmem[:, x, 16 * t : 16 * t + 16, :].reshape(depth, LANES) for t in range(tiles)],
            axis=1,
        )
        got = jnp.dot(w_big[...], right, preferred_element_type=jnp.float32)
        for a in range(3):
            at = x + 2 - a
            for c in range(3):
                first = (3 * a + c) * ROWS
                acc[at, c] = acc[at, c] + got[first : first + ROWS, :]
    masks.wait()
    for p, at in enumerate(planes()):
        finish(p, at)
    m_ref[len(folds) * size_y :, :] = functools.reduce(jnp.add, folds)


def y_masks(axis, chip):
    row = row_of((8, LANES))
    index, last = lax.axis_index(axis), lax.axis_size(axis) - 1
    odd = index % 2
    if chip:
        low, high = odd == 1, odd == 0
    else:
        low, high = (odd == 0) & (index > 0), (odd == 1) & (index < last)
    return row == jnp.where(low, 0, -1), row == jnp.where(high, 7, -1)


def edge_rows(masks, part, size_y):
    low, high = masks
    return jnp.concatenate(
        [
            jnp.where(low, part, 0.0),
            jnp.zeros((size_y - 16, LANES), jnp.float32),
            jnp.where(high, part, 0.0),
        ],
        axis=0,
    )


def turn_kernel(s_ref, own_ref, far_ref, chip_ref, cross_ref, xchip_ref, xcross_ref, score_ref, zm_ref):
    size_x, size_y, _ = s_ref.shape
    chip, cross = y_masks("gy", True), y_masks("gy", False)
    first = lax.axis_index("gx") == 0
    lane = lane_of((size_y, LANES))
    border = (lane == 0) | (lane == LANES - 1)
    faces_own = {size_x - 1: jnp.where(first, 1.0, 0.0), 0: jnp.where(first, 0.0, 1.0)}
    faces_far = {0: faces_own[size_x - 1], size_x - 1: faces_own[0]}

    def plane(ref, p):
        return ref[p * size_y : (p + 1) * size_y, :]

    def fold(ref, p):
        rest = ref[(size_x + 1) * size_y :, :]
        return pltpu.roll(rest, LANES - 16 * p, 1) if p else rest

    def complete(p, base, folded, face_ref, sides, faces):
        if p in faces:
            base = base + faces[p] * plane(face_ref, size_x)
            folded = folded + faces[p] * fold(face_ref, size_x)
        for masks, same, other in sides:
            part, part_h = same[p : p + 1], same[8 + p : 9 + p]
            if p in faces:
                part = part + faces[p] * other[size_x : size_x + 1]
                part_h = part_h + faces[p] * other[8 + size_x : 9 + size_x]
            base = base + edge_rows(masks, part, size_y)
            folded = folded + jnp.where(masks[0] | masks[1], part_h, 0.0)
        return base, folded

    costs, turned = [], []
    for far in range(2):
        for p in range(size_x):
            if far:
                sides = ((chip, xchip_ref, chip_ref), (cross, xcross_ref, cross_ref))
                masked, h = complete(p, plane(far_ref, p), fold(far_ref, p), own_ref, sides, faces_far)
            else:
                sides = ((chip, chip_ref, xchip_ref), (cross, cross_ref, xcross_ref))
                full, h = complete(p, s_ref[p], fold(own_ref, p), far_ref, sides, faces_own)
                score_ref[p] = full
                masked = jnp.where(plane(own_ref, p) == HUGE, HUGE, full)
            costs.append(cost_of(masked))
            wide = jnp.concatenate(
                [pltpu.roll(h, (2 - 2 * g) % LANES, 1) for g in range(size_y // 8)], axis=0
            )
            turned.append(jnp.where(border, masked, wide))
    away = jnp.where(first, float(size_x), -float(size_x))
    lines = []
    for i in range(size_x):
        best = costs[i]
        for j in range(size_x):
            if j != i:
                best = jnp.minimum(best, costs[j] + float((i - j) ** 2))
            d = float(j - i) + away
            best = jnp.minimum(best, costs[size_x + j] + d * d)
        lines.append(best)
    zm_ref[0:LANES, :] = jnp.concatenate(lines, axis=0).T
    width = size_x * size_y
    ends = jnp.concatenate(turned, axis=0).T
    zm_ref[LANES : LANES + 8, :] = jnp.concatenate(
        [ends[r : r + 1, k * width : (k + 1) * width] for r in (0, LANES - 1, 1, 2) for k in range(2)],
        axis=0,
    )


Z_FLOOR = -(LANES + 6)


def sweep(accs, blocks, read, table, shift, low, high):
    parts = len(accs[0])

    def body(j, flat):
        flat = list(flat)
        tiles = read(j)
        squares = table.at[pl.ds(shift + 8 * blocks[0] - 8 * j, 8 * len(blocks))]
        for r in range(8):
            rows = [jnp.broadcast_to(t[r : r + 1, :], (8, LANES)) for t in tiles]
            for i in range(len(blocks)):
                square = squares[8 * i + 7 - r]
                for k in range(parts):
                    at = i * parts + k
                    flat[at] = jnp.minimum(flat[at], rows[k] + square)
        return tuple(flat)

    flat = lax.fori_loop(low, high, body, tuple(v for row in accs for v in row))
    return [list(flat[i * parts : (i + 1) * parts]) for i in range(len(blocks))]


def tiles_of(ref, j):
    rows = pl.ds(pl.multiple_of(8 * j, 8), 8)
    return [ref[rows, k * LANES : (k + 1) * LANES] for k in range(ref.shape[1] // LANES)]


def load_blocks(ref, blocks):
    return [tiles_of(ref, b) for b in blocks]


def save_blocks(ref, blocks, accs):
    for b, row in zip(blocks, accs):
        for k, v in enumerate(row):
            ref[8 * b : 8 * b + 8, k * LANES : (k + 1) * LANES] = v


def z_own_kernel(zm_ref, out_ref, table):
    count, half = LANES // 8, LANES // 16
    s = row_of((8, LANES)).astype(jnp.float32)
    for d in range(Z_FLOOR, LANES):
        v = s + float(d)
        table[d - Z_FLOOR] = v * v

    def read(j):
        at = row_of((8, LANES)) + 8 * j
        hide = (at == 0) | (at == LANES - 1)
        return [jnp.where(hide, HUGE, t) for t in tiles_of(zm_ref, j)]

    for first in (0, half):
        blocks = range(first, first + half)
        accs = [[jnp.full((8, LANES), HUGE, jnp.float32)] * (out_ref.shape[1] // LANES) for _ in blocks]
        save_blocks(out_ref, blocks, sweep(accs, blocks, read, table, -7 - Z_FLOOR, 0, count))


def border_minima(cost, size_x, size_y, partner):
    if not partner:
        return cost
    width = cost.shape[1]
    shape = (8, width)
    row, plane = row_of(shape), lane_of(shape) // size_y
    away = jnp.where(lax.axis_index("gx") == 0, size_x, -size_x)
    shift = jnp.where(row % 2 == 1, away, 0)
    best = None
    for r in range(size_x):
        source = jnp.where(plane >= r, plane - r, plane - r + size_x)
        d = (source + shift - plane).astype(jnp.float32)
        if r == 0:
            moved = cost
        else:
            cut = width - r * size_y
            moved = jnp.concatenate([cost[:, cut:], cost[:, :cut]], axis=1)
        moved = moved + d * d
        best = moved if best is None else jnp.minimum(best, moved)
    return jnp.minimum(best, pltpu.roll(best, 7, 0))


def z_far_kernel(even, partner, size_x, size_y, acc_ref, table, zm_ref, got_ref, out_ref, source, work):
    index, last = lax.axis_index("gz"), lax.axis_size("gz") - 1
    odd = index % 2 == 1
    low = odd if even else jnp.logical_not(odd)
    valid = jnp.where(low, index > 0, index < last)
    count, half = LANES // 8, LANES // 16
    out = out_ref if even else work

    own, got = zm_ref[LANES : LANES + 8, :], got_ref[LANES : LANES + 8, :]
    mine = jnp.where(low, own[0:2], own[2:4]) + jnp.where(valid, jnp.where(low, got[6:8], got[4:6]), 0.0)
    theirs = jnp.where(low, got[2:4] + own[4:6], got[0:2] + own[6:8])
    ends = border_minima(cost_of(jnp.concatenate([mine, theirs, mine, theirs], axis=0)), size_x, size_y, partner)
    source[...] = got_ref[0:LANES, :]

    squares = table.at[pl.ds(jnp.where(low, -Z_FLOOR, 1 - LANES - Z_FLOOR), LANES)]
    lanes = [slice(k * LANES, (k + 1) * LANES) for k in range(zm_ref.shape[1] // LANES)]
    rows = [jnp.broadcast_to(ends[0:1, cols], (8, LANES)) for cols in lanes]
    for b in range(count):
        for row, cols in zip(rows, lanes):
            span = slice(8 * b, 8 * b + 8)
            out[span, cols] = jnp.minimum(acc_ref[span, cols], row + squares[8 * b])

    def slanted(accs, blocks, offset, tiles, reach):
        for j in tiles:
            tile = tiles_of(source, j)
            for r in range(8):
                q = 8 * j + r
                rows = [jnp.broadcast_to(t[r : r + 1, :], (8, LANES)) for t in tile]
                for i, b in enumerate(blocks):
                    if reach(b, q):
                        square = table[8 * b - q + offset - Z_FLOOR]
                        accs[i] = [jnp.minimum(v, row + square) for v, row in zip(accs[i], rows)]
        return accs

    @pl.when(valid & low)
    def _():
        source[LANES - 1 : LANES, :] = ends[2:3]
        for first in (0, half):
            blocks = range(first, first + half)
            accs = load_blocks(out, blocks)
            accs = slanted(accs, blocks, LANES, blocks, lambda b, q: 8 * b < q)
            if blocks[-1] + 1 < count:
                read = functools.partial(tiles_of, source)
                accs = sweep(accs, blocks, read, table, LANES - 7 - Z_FLOOR, blocks[-1] + 1, count)
            save_blocks(out, blocks, accs)

    @pl.when(valid & jnp.logical_not(low))
    def _():
        source[0:1, :] = ends[2:3]
        for first in (0, half):
            blocks = range(first, first + half)
            accs = load_blocks(out, blocks)
            accs = slanted(accs, blocks, -LANES, blocks, lambda b, q: q < 8 * b + 7)
            if first:
                read = functools.partial(tiles_of, source)
                accs = sweep(accs, blocks, read, table, -LANES - 7 - Z_FLOOR, 0, first)
            save_blocks(out, blocks, accs)

    if not even:
        per = LANES // size_y
        for k, cols in enumerate(lanes):
            best = work[:, cols].T
            for i in range(per):
                out_ref[k * per + i] = best[i * size_y : (i + 1) * size_y]


def score_kernel(score_in, even_ref, odd_ref, _, score_ref):
    index, last = lax.axis_index("gz"), lax.axis_size("gz") - 1
    odd = index % 2 == 1
    size_y = score_in.shape[1]
    per = LANES // size_y
    for k in range(even_ref.shape[1] // LANES):
        cols = slice(k * LANES, (k + 1) * LANES)
        even_rows, odd_rows = even_ref[LANES : LANES + 8, cols], odd_ref[LANES : LANES + 8, cols]
        low = jnp.where(index > 0, jnp.where(odd, even_rows, odd_rows)[6:7], 0.0)
        high = jnp.where(index < last, jnp.where(odd, odd_rows, even_rows)[4:5], 0.0)
        middle = jnp.zeros((LANES - 2, LANES), jnp.float32)
        more = jnp.concatenate([low, middle, high], axis=0).T
        for i in range(per):
            x = k * per + i
            score_ref[x] = score_in[x] + more[i * size_y : (i + 1) * size_y]


def y_table(axis, hop, size_y, table):
    index = lax.axis_index(axis)
    away = (((index ^ hop) - index) * size_y).astype(jnp.float32)
    s = row_of((8, LANES)).astype(jnp.float32) - away
    for d in range(1 - size_y, size_y - 7):
        v = s + float(d)
        table[d - (1 - size_y)] = v * v


Y_BLOCKS = 4


def y_sweep(refs, tables, start, out_ref, scale):
    size_x, size_y, _ = out_ref.shape
    for first in range(0, size_y // 8, Y_BLOCKS):
        blocks = range(first, first + Y_BLOCKS)
        accs = []
        for b in blocks:
            span = slice(8 * b, 8 * b + 8)
            blank = jnp.full((8, LANES), HUGE, jnp.float32)
            accs.append([blank if start is None else start[x, span, :] for x in range(size_x)])
        for ref, table in zip(refs, tables):

            def read(j, ref=ref):
                return [ref[x, pl.ds(pl.multiple_of(8 * j, 8), 8), :] for x in range(size_x)]

            accs = sweep(accs, blocks, read, table, size_y - 8, 0, size_y // 8)
        for b, row in zip(blocks, accs):
            for x, v in enumerate(row):
                out_ref[x, 8 * b : 8 * b + 8, :] = v if scale == 1.0 else v * scale


def y_own_kernel(own_ref, out_ref, table_1, table_2, table_3, table_0):
    size_y = own_ref.shape[1]
    for hop, table in enumerate((table_0, table_1, table_2, table_3)):
        y_table("gy", hop, size_y, table)
    y_sweep((own_ref,), (table_0,), None, out_ref, 1.0)


def y_far_kernel(hop, scale, start_ref, ref, table, out_ref):
    index = lax.axis_index("gy")
    if hop < 3:
        y_sweep((ref,), (table,), start_ref, out_ref, scale)
        return
    near = jnp.abs((index ^ hop) - index) < 3

    @pl.when(near)
    def _():
        y_sweep((ref,), (table,), start_ref, out_ref, scale)

    @pl.when(jnp.logical_not(near))
    def _():
        out_ref[...] = start_ref[...] * scale


def swap(value, axis, hop):
    n = lax.axis_size(axis)
    return lax.ppermute(value, axis, [(i, i ^ hop) for i in range(n)])


def swap_xy(value, hop_x, hop_y):
    nx, ny = lax.axis_size("gx"), lax.axis_size("gy")
    pairs = [(x * ny + y, (x ^ hop_x) * ny + (y ^ hop_y)) for x in range(nx) for y in range(ny)]
    return lax.ppermute(value, ("gx", "gy"), pairs)


def neighbours(low, high, axis, beyond=0.0):
    n, index = lax.axis_size(axis), lax.axis_index(axis)
    odd = index % 2 == 1
    pairs = [(i, i + 1 if i % 2 else i - 1) for i in range(1, n - 1)]
    got_odd = lax.ppermute(jnp.where(odd, high, low), axis, pairs)
    got_even = lax.ppermute(jnp.where(odd, low, high), axis, [(i, i ^ 1) for i in range(n)])
    from_low = jnp.where(odd, got_even, got_odd)
    from_high = jnp.where(odd, got_odd, got_even)
    return jnp.where(index == 0, beyond, from_low), jnp.where(index == n - 1, beyond, from_high)


def z_swaps(value):
    nx, ny, n = (lax.axis_size(axis) for axis in ("gx", "gy", "gz"))
    even = lax.ppermute(value, "gz", [(i, i ^ 1) for i in range(n)])
    pairs = []
    for i in range(nx * ny * n):
        xy, z = i // n, i % n
        pairs.append((i, (xy ^ 1) * n + z if z in (0, n - 1) else xy * n + (z + 1 if z % 2 else z - 1)))
    return even, lax.ppermute(value, ("gx", "gy", "gz"), pairs)


def corner_swap(value):
    nx, ny = lax.axis_size("gx"), lax.axis_size("gy")
    pairs = []
    for i in range(nx * ny):
        x, y = i // ny, i % ny
        pairs.append((i, (x ^ 1) * ny + y if y in (0, ny - 1) else x * ny + (y + 1 if y % 2 else y - 1)))
    return lax.ppermute(value, ("gx", "gy"), pairs)


def conv(features, conv_weight, mask, planes, count, paired):
    channels, size_x, size_y, _ = features.shape
    return call(
        functools.partial(conv_kernel, planes, paired),
        [(size_x, size_y, LANES), (count * size_y + 8, LANES), (16, LANES), (16, LANES)],
        [
            pltpu.VMEM(features.shape, jnp.bfloat16),
            pltpu.VMEM(conv_weight.shape, jnp.bfloat16),
            pltpu.VMEM(mask.shape, jnp.int32),
            pltpu.VMEM((9 * ROWS + 8, channels * 16), jnp.bfloat16),
            pltpu.VMEM((size_x + 2, 3, ROWS, size_y // 16 * LANES), jnp.float32),
            pltpu.SemaphoreType.DMA((size_x + 2,)),
        ],
        mib=24,
        in_specs=[HBM] * 3,
    )(*(pltpu.with_memory_space_constraint(v, pltpu.HBM) for v in (features, conv_weight, mask)))


def halo_with_partner(features, conv_weight, mask):
    _, size_x, size_y, _ = features.shape

    def planes():
        return [*range(1, size_x + 1), jnp.where(lax.axis_index("gx") == 0, size_x + 1, 0)]

    s, own, chip, cross = conv(features, conv_weight, mask, planes, size_x + 1, True)
    far = swap_xy(own, 1, 0)
    sides = [swap_xy(v, x, y) for x in range(2) for v, y in ((chip, 1), (cross, 3))]
    return call(turn_kernel, [(size_x, size_y, LANES), (LANES + 8, size_x * size_y)])(s, own, far, *sides)


def halo_in_rounds(features, conv_weight, mask):
    _, size_x, size_y, _ = features.shape
    groups = size_y // 8
    planes = [*range(1, size_x + 1), 0, size_x + 1]
    s, rest, down, up = conv(features, conv_weight, mask, lambda: planes, size_x + 2, False)

    def whole(k):
        h = jnp.roll(rest[len(planes) * size_y :], -16 * k, 1)
        part = s[k] if k < size_x else rest[k * size_y : (k + 1) * size_y]
        return jnp.concatenate([part, h, *(e[i : i + 1] for e in (down, up) for i in (k, 8 + k))], axis=0)

    low, high = neighbours(whole(size_x), whole(size_x + 1), "gx")
    own = jnp.stack([whole(k) for k in range(size_x)]).at[0].add(low).at[size_x - 1].add(high)
    e = own[:, size_y + 8 :]
    low, high = neighbours(e[:, 0:2], e[:, 2:4], "gy")
    own = own.at[:, 0].add(low[:, 0]).at[:, size_y - 1].add(high[:, 0])
    own = own.at[:, size_y].add(low[:, 1]).at[:, size_y + 7].add(high[:, 1])
    score, h = own[:, :size_y], own[:, size_y : size_y + 8]

    def line(value):
        return value.reshape(1, size_x * size_y)

    up = jnp.swapaxes(h[:, :, 0 : 2 * groups : 2], 1, 2)
    down = jnp.swapaxes(jnp.roll(h, 1, 2)[:, :, 0 : 2 * groups : 2], 1, 2)
    masked = jnp.where(mask == 1, HUGE, score)
    rows = jnp.transpose(cost_of(masked), (2, 0, 1)).reshape(LANES, size_x * size_y)
    ends = [line(v) for v in (masked[:, :, 0], masked[:, :, LANES - 1], down, up)]
    blank = [jnp.full_like(ends[0], HUGE)] * 2 + [jnp.zeros_like(ends[0])] * 2
    pairs = [v for pair in zip(ends, blank) for v in pair]
    return score, jnp.concatenate([rows, *pairs], axis=0)


def x_minima(value, size_x):
    n, index = lax.axis_size("gx"), lax.axis_index("gx")
    every = lax.all_gather(value, "gx", axis=0, tiled=True)
    at = index * size_x + jnp.arange(size_x)
    d = (at[:, None] - jnp.arange(n * size_x)[None, :]).astype(jnp.float32)
    return jnp.min(every[None] + (d * d)[:, :, None, None], axis=1)


def shards(features, conv_weight, mask):
    _, size_x, size_y, size_z = features.shape
    gx, gy = lax.axis_size("gx"), lax.axis_size("gy")
    assert size_z == LANES and size_y % 16 == 0 and LANES % size_y == 0 and gy == 4
    brick = (size_x, size_y, LANES)
    lines = size_x * size_y
    partner = gx == 2

    halo = halo_with_partner if partner else halo_in_rounds
    score, zm = halo(features, conv_weight, mask)

    even, odd = z_swaps(zm)
    best, table = call(z_own_kernel, [(LANES, lines), (LANES - Z_FLOOR, 8, LANES)])(zm)
    work = [pltpu.VMEM((LANES, lines), jnp.float32)] * 2
    for first, got, shape in ((True, even, (LANES, lines)), (False, odd, brick)):
        far = functools.partial(z_far_kernel, first, partner, size_x, size_y)
        (best,) = call(far, [shape], work)(best, table, zm, got)
    (score,) = call(score_kernel, [brick])(score, even, odd, best)
    if not partner:
        best = x_minima(best, size_x)

    tables = (2 * size_y - 8, 8, LANES)
    across, chip = swap(best, "gy", 2), swap(best, "gy", 1)
    near, *kept = call(y_own_kernel, [brick, tables, tables, tables], [pltpu.VMEM(tables, jnp.float32)])(best)
    blocks = {2: across, 1: chip, 3: corner_swap(best)}
    for hop, block in blocks.items():
        far = functools.partial(y_far_kernel, hop, 1.0 / RADIUS if hop == 3 else 1.0)
        (near,) = call(far, [brick])(near, block, kept[hop - 1])
    return score, near


def solution(mesh):
    in_specs = (P(None, "gx", "gy", "gz"), P(), P("gx", "gy", "gz"))
    out_specs = (P("gx", "gy", "gz"), P("gx", "gy", "gz"))
    return jax.shard_map(shards, mesh=mesh, in_specs=in_specs, out_specs=out_specs, check_vma=False)
```

```python
import functools

import jax
import jax.numpy as jnp
from jax import lax
from jax.experimental import pallas as pl
from jax.experimental.pallas import tpu as pltpu
from jax.sharding import PartitionSpec as P

RADIUS = 128
CEILING = float(RADIUS * RADIUS)
HUGE = 1e30
LANES = 128
ROWS = 24
VMEM = pl.BlockSpec(memory_space=pltpu.VMEM)
HBM = pl.BlockSpec(memory_space=pltpu.HBM)


def call(kernel, outs, scratch=(), mib=8, in_specs=None, kind=jnp.float32):
    shapes = [jax.ShapeDtypeStruct(s, kind) for s in outs]

    def run(*args):
        return pl.pallas_call(
            kernel,
            out_shape=shapes,
            in_specs=in_specs or [VMEM] * len(args),
            out_specs=[VMEM] * len(shapes),
            scratch_shapes=list(scratch),
            compiler_params=pltpu.CompilerParams(vmem_limit_bytes=mib * 1024 * 1024),
        )(*args)

    return run


def lane_of(shape):
    return lax.broadcasted_iota(jnp.int32, shape, len(shape) - 1)


def row_of(shape):
    return lax.broadcasted_iota(jnp.int32, shape, len(shape) - 2)


def cost_of(score):
    return CEILING / (1.0 + jnp.exp(-score))


def conv_kernel(
    planes, paired, f_hbm, w_hbm, mask_hbm, s_ref, m_ref, e_ref, d_ref, f_vmem, w_vmem, mask_vmem, w_big, acc, sems
):
    channels, size_x, size_y, _ = f_vmem.shape
    tiles = size_y // 16
    depth = channels * 16
    weights = pltpu.make_async_copy(w_hbm, w_vmem, sems.at[size_x])
    weights.start()
    copies = [
        pltpu.make_async_copy(f_hbm.at[:, x], f_vmem.at[:, x], sems.at[x]) for x in range(size_x)
    ]
    masks = pltpu.make_async_copy(mask_hbm, mask_vmem, sems.at[size_x + 1])
    masks.start()
    for copy in copies:
        copy.start()

    acc[...] = jnp.zeros_like(acc)
    spread = (
        lax.broadcasted_iota(jnp.int32, (channels, depth), 1) // 16
        == lax.broadcasted_iota(jnp.int32, (channels, depth), 0)
    ).astype(jnp.bfloat16)
    row = lax.broadcasted_iota(jnp.int32, (ROWS, depth), 0)
    y_in = lax.broadcasted_iota(jnp.int32, (ROWS, depth), 1) % 16
    y_out = jnp.where(row <= 16, row, jnp.where(row == ROWS - 1, -1, 64))
    tap = y_in - y_out + 1
    weights.wait()
    wide = jnp.dot(w_vmem[...], spread, preferred_element_type=jnp.float32)
    blocks = []
    for a in range(3):
        for c in range(3):
            block = jnp.zeros((ROWS, depth), jnp.float32)
            for b in range(3):
                k = 9 * a + 3 * b + c
                block = jnp.where(tap == b, wide[k : k + 1, :], block)
            blocks.append(block)
    blocks.append(jnp.zeros((8, depth), jnp.float32))
    w_big[...] = jnp.concatenate(blocks, axis=0).astype(jnp.bfloat16)

    shape = (8, LANES)
    row, lane = row_of(shape), lane_of(shape)
    groups = size_y // 8
    to_first = lax.axis_index("gy") % 2 == 1 if paired else True
    folds = []

    def finish(p, at):
        fold = None
        for g in range(groups + 1):
            sums = []
            for c in range(3):

                def piece(tile, low, c=c):
                    return acc[at, c, low : low + 8, tile * LANES : tile * LANES + LANES]

                if g == groups:
                    part = jnp.where(row == 0, piece(tiles - 1, 16), piece(0, 16))
                else:
                    tile, low = g // 2, 8 * (g % 2)
                    part = piece(tile, low)
                    if low == 0 and tile > 0:
                        part = part + jnp.where(row == 0, piece(tile - 1, 16), 0.0)
                    if low == 8 and tile < tiles - 1:
                        part = part + jnp.where(row == 7, piece(tile + 1, 16), 0.0)
                sums.append(part)
            ahead = pltpu.roll(sums[0], 1, 1)
            behind = pltpu.roll(sums[2], LANES - 1, 1)
            inner = (
                sums[1] + jnp.where(lane == 0, 0.0, ahead) + jnp.where(lane == LANES - 1, 0.0, behind)
            )
            outer = jnp.where(lane == 0, ahead, jnp.where(lane == LANES - 1, behind, 0.0))
            if g == groups:
                for up, down, at_row in (
                    (inner, inner, p),
                    (outer, pltpu.roll(outer, 2 * (groups - 1), 1), 8 + p),
                ):
                    e_ref[at_row : at_row + 1, :] = jnp.where(to_first, down[7:8], up[0:1])
                    d_ref[at_row : at_row + 1, :] = jnp.where(to_first, up[0:1], down[7:8])
            else:
                span = slice(8 * g, 8 * g + 8)
                if p < size_x:
                    s_ref[p, span, :] = inner
                    inner = jnp.where(mask_vmem[p, span, :] == 1, HUGE, inner)
                m_ref[p * size_y + 8 * g : p * size_y + 8 * g + 8, :] = inner
                shift = 16 * p + 2 * g
                outer = pltpu.roll(outer, shift, 1) if shift else outer
                fold = outer if g == 0 else fold + outer
        folds.append(fold)

    for x in range(size_x):
        copies[x].wait()
        right = jnp.concatenate(
            [f_vmem[:, x, 16 * t : 16 * t + 16, :].reshape(depth, LANES) for t in range(tiles)],
            axis=1,
        )
        got = jnp.dot(w_big[...], right, preferred_element_type=jnp.float32)
        for a in range(3):
            at = x + 2 - a
            for c in range(3):
                first = (3 * a + c) * ROWS
                acc[at, c] = acc[at, c] + got[first : first + ROWS, :]
    masks.wait()
    for p, at in enumerate(planes()):
        finish(p, at)
    m_ref[len(folds) * size_y :, :] = functools.reduce(jnp.add, folds)


def y_masks(axis, chip):
    row = row_of((8, LANES))
    index, last = lax.axis_index(axis), lax.axis_size(axis) - 1
    odd = index % 2
    if chip:
        low, high = odd == 1, odd == 0
    else:
        low, high = (odd == 0) & (index > 0), (odd == 1) & (index < last)
    return row == jnp.where(low, 0, -1), row == jnp.where(high, 7, -1)


def edge_rows(masks, part, size_y):
    low, high = masks
    return jnp.concatenate(
        [
            jnp.where(low, part, 0.0),
            jnp.zeros((size_y - 16, LANES), jnp.float32),
            jnp.where(high, part, 0.0),
        ],
        axis=0,
    )


def turn_kernel(s_ref, own_ref, far_ref, cross_ref, xcross_ref, chip_ref, xchip_ref, score_ref, zm_ref):
    size_x, size_y, _ = s_ref.shape
    chip, cross = y_masks("gy", True), y_masks("gy", False)
    first = lax.axis_index("gx") == 0
    lane = lane_of((size_y, LANES))
    border = (lane == 0) | (lane == LANES - 1)
    faces_own = {size_x - 1: jnp.where(first, 1.0, 0.0), 0: jnp.where(first, 0.0, 1.0)}
    faces_far = {0: faces_own[size_x - 1], size_x - 1: faces_own[0]}

    def plane(ref, p):
        return ref[p * size_y : (p + 1) * size_y, :]

    def fold(ref, p):
        rest = ref[(size_x + 1) * size_y :, :]
        return pltpu.roll(rest, LANES - 16 * p, 1) if p else rest

    def complete(p, base, folded, face_ref, sides, faces):
        if p in faces:
            base = base + faces[p] * plane(face_ref, size_x)
            folded = folded + faces[p] * fold(face_ref, size_x)
        for masks, same, other in sides:
            part, part_h = same[p : p + 1], same[8 + p : 9 + p]
            if p in faces:
                part = part + faces[p] * other[size_x : size_x + 1]
                part_h = part_h + faces[p] * other[8 + size_x : 9 + size_x]
            base = base + edge_rows(masks, part, size_y)
            folded = folded + jnp.where(masks[0] | masks[1], part_h, 0.0)
        return base, folded

    costs, turned = [], []
    for far in range(2):
        for p in range(size_x):
            if far:
                sides = ((chip, xchip_ref, chip_ref), (cross, xcross_ref, cross_ref))
                masked, h = complete(p, plane(far_ref, p), fold(far_ref, p), own_ref, sides, faces_far)
            else:
                sides = ((chip, chip_ref, xchip_ref), (cross, cross_ref, xcross_ref))
                full, h = complete(p, s_ref[p], fold(own_ref, p), far_ref, sides, faces_own)
                score_ref[p] = full
                masked = jnp.where(plane(own_ref, p) == HUGE, HUGE, full)
            costs.append(cost_of(masked))
            wide = jnp.concatenate(
                [pltpu.roll(h, (2 - 2 * g) % LANES, 1) for g in range(size_y // 8)], axis=0
            )
            turned.append(jnp.where(border, masked, wide))
    away = jnp.where(first, float(size_x), -float(size_x))
    lines = []
    for i in range(size_x):
        best = costs[i]
        for j in range(size_x):
            if j != i:
                best = jnp.minimum(best, costs[j] + float((i - j) ** 2))
            d = float(j - i) + away
            best = jnp.minimum(best, costs[size_x + j] + d * d)
        lines.append(best)
    zm_ref[0:LANES, :] = jnp.concatenate(lines, axis=0).T
    width = size_x * size_y
    ends = jnp.concatenate(turned, axis=0).T
    zm_ref[LANES : LANES + 8, :] = jnp.concatenate(
        [ends[r : r + 1, k * width : (k + 1) * width] for r in (0, LANES - 1, 1, 2) for k in range(2)],
        axis=0,
    )


Z_FLOOR = -(LANES + 6)


def sweep(accs, blocks, read, table, shift, low, high):
    parts = len(accs[0])

    def body(j, flat):
        flat = list(flat)
        tiles = read(j)
        squares = table.at[pl.ds(shift + 8 * blocks[0] - 8 * j, 8 * len(blocks))]
        for r in range(8):
            rows = [jnp.broadcast_to(t[r : r + 1, :], (8, LANES)) for t in tiles]
            for i in range(len(blocks)):
                square = squares[8 * i + 7 - r]
                for k in range(parts):
                    at = i * parts + k
                    flat[at] = jnp.minimum(flat[at], rows[k] + square)
        return tuple(flat)

    flat = lax.fori_loop(low, high, body, tuple(v for row in accs for v in row))
    return [list(flat[i * parts : (i + 1) * parts]) for i in range(len(blocks))]


def tiles_of(ref, j):
    rows = pl.ds(pl.multiple_of(8 * j, 8), 8)
    return [ref[rows, k * LANES : (k + 1) * LANES] for k in range(ref.shape[1] // LANES)]


def load_blocks(ref, blocks):
    return [tiles_of(ref, b) for b in blocks]


def save_blocks(ref, blocks, accs):
    for b, row in zip(blocks, accs):
        for k, v in enumerate(row):
            ref[8 * b : 8 * b + 8, k * LANES : (k + 1) * LANES] = v


def y_table(axis, hop, size_y, table):
    index = lax.axis_index(axis)
    away = (((index ^ hop) - index) * size_y).astype(jnp.float32)
    s = row_of((8, LANES)).astype(jnp.float32) - away
    for d in range(1 - size_y, size_y - 7):
        v = s + float(d)
        table[d - (1 - size_y)] = v * v


def z_own_kernel(size_y, zm_ref, out_ref, table, *y_tables):
    count, half = LANES // 8, LANES // 16
    for hop, y_one in enumerate(y_tables):
        y_table("gy", hop, size_y, y_one)
    s = row_of((8, LANES)).astype(jnp.float32)
    for d in range(Z_FLOOR, LANES):
        v = s + float(d)
        table[d - Z_FLOOR] = v * v

    def read(j):
        at = row_of((8, LANES)) + 8 * j
        hide = (at == 0) | (at == LANES - 1)
        return [jnp.where(hide, HUGE, t) for t in tiles_of(zm_ref, j)]

    for first in (0, half):
        blocks = range(first, first + half)
        accs = [[jnp.full((8, LANES), HUGE, jnp.float32)] * (out_ref.shape[1] // LANES) for _ in blocks]
        save_blocks(out_ref, blocks, sweep(accs, blocks, read, table, -7 - Z_FLOOR, 0, count))


def border_minima(cost, size_x, size_y, partner):
    if not partner:
        return cost
    width = cost.shape[1]
    shape = (8, width)
    row, plane = row_of(shape), lane_of(shape) // size_y
    away = jnp.where(lax.axis_index("gx") == 0, size_x, -size_x)
    shift = jnp.where(row % 2 == 1, away, 0)
    best = None
    for r in range(size_x):
        source = jnp.where(plane >= r, plane - r, plane - r + size_x)
        d = (source + shift - plane).astype(jnp.float32)
        if r == 0:
            moved = cost
        else:
            cut = width - r * size_y
            moved = jnp.concatenate([cost[:, cut:], cost[:, :cut]], axis=1)
        moved = moved + d * d
        best = moved if best is None else jnp.minimum(best, moved)
    return jnp.minimum(best, pltpu.roll(best, 7, 0))


def z_far_kernel(even, partner, size_x, size_y, acc_ref, table, zm_ref, got_ref, out_ref, source, work):
    index, last = lax.axis_index("gz"), lax.axis_size("gz") - 1
    odd = index % 2 == 1
    low = odd if even else jnp.logical_not(odd)
    valid = jnp.where(low, index > 0, index < last)
    count, half = LANES // 8, LANES // 16
    out = out_ref if even else work

    own, got = zm_ref[LANES : LANES + 8, :], got_ref[LANES : LANES + 8, :]
    mine = jnp.where(low, own[0:2], own[2:4]) + jnp.where(valid, jnp.where(low, got[6:8], got[4:6]), 0.0)
    theirs = jnp.where(low, got[2:4] + own[4:6], got[0:2] + own[6:8])
    ends = border_minima(cost_of(jnp.concatenate([mine, theirs, mine, theirs], axis=0)), size_x, size_y, partner)
    source[...] = got_ref[0:LANES, :]

    squares = table.at[pl.ds(jnp.where(low, -Z_FLOOR, 1 - LANES - Z_FLOOR), LANES)]
    lanes = [slice(k * LANES, (k + 1) * LANES) for k in range(zm_ref.shape[1] // LANES)]
    rows = [jnp.broadcast_to(ends[0:1, cols], (8, LANES)) for cols in lanes]
    for b in range(count):
        for row, cols in zip(rows, lanes):
            span = slice(8 * b, 8 * b + 8)
            out[span, cols] = jnp.minimum(acc_ref[span, cols], row + squares[8 * b])

    def slanted(accs, blocks, offset, tiles, reach):
        for j in tiles:
            tile = tiles_of(source, j)
            for r in range(8):
                q = 8 * j + r
                rows = [jnp.broadcast_to(t[r : r + 1, :], (8, LANES)) for t in tile]
                for i, b in enumerate(blocks):
                    if reach(b, q):
                        square = table[8 * b - q + offset - Z_FLOOR]
                        accs[i] = [jnp.minimum(v, row + square) for v, row in zip(accs[i], rows)]
        return accs

    @pl.when(valid & low)
    def _():
        source[LANES - 1 : LANES, :] = ends[2:3]
        for first in (0, half):
            blocks = range(first, first + half)
            accs = load_blocks(out, blocks)
            accs = slanted(accs, blocks, LANES, blocks, lambda b, q: 8 * b < q)
            if blocks[-1] + 1 < count:
                read = functools.partial(tiles_of, source)
                accs = sweep(accs, blocks, read, table, LANES - 7 - Z_FLOOR, blocks[-1] + 1, count)
            save_blocks(out, blocks, accs)

    @pl.when(valid & jnp.logical_not(low))
    def _():
        source[0:1, :] = ends[2:3]
        for first in (0, half):
            blocks = range(first, first + half)
            accs = load_blocks(out, blocks)
            accs = slanted(accs, blocks, -LANES, blocks, lambda b, q: q < 8 * b + 7)
            if first:
                read = functools.partial(tiles_of, source)
                accs = sweep(accs, blocks, read, table, -LANES - 7 - Z_FLOOR, 0, first)
            save_blocks(out, blocks, accs)

    if not even:
        per = LANES // size_y
        for k, cols in enumerate(lanes):
            best = work[:, cols].T
            for i in range(per):
                out_ref[k * per + i] = best[i * size_y : (i + 1) * size_y]


def score_kernel(score_in, even_ref, odd_ref, _, score_ref):
    index, last = lax.axis_index("gz"), lax.axis_size("gz") - 1
    odd = index % 2 == 1
    size_y = score_in.shape[1]
    per = LANES // size_y
    for k in range(even_ref.shape[1] // LANES):
        cols = slice(k * LANES, (k + 1) * LANES)
        even_rows, odd_rows = even_ref[LANES : LANES + 8, cols], odd_ref[LANES : LANES + 8, cols]
        low = jnp.where(index > 0, jnp.where(odd, even_rows, odd_rows)[6:7], 0.0)
        high = jnp.where(index < last, jnp.where(odd, odd_rows, even_rows)[4:5], 0.0)
        middle = jnp.zeros((LANES - 2, LANES), jnp.float32)
        more = jnp.concatenate([low, middle, high], axis=0).T
        for i in range(per):
            x = k * per + i
            score_ref[x] = score_in[x] + more[i * size_y : (i + 1) * size_y]


Y_BLOCKS = 4


def y_sweep(refs, tables, start, out_ref, scale):
    size_x, size_y, _ = out_ref.shape
    for first in range(0, size_y // 8, Y_BLOCKS):
        blocks = range(first, first + Y_BLOCKS)
        accs = []
        for b in blocks:
            span = slice(8 * b, 8 * b + 8)
            blank = jnp.full((8, LANES), HUGE, jnp.float32)
            accs.append([blank if start is None else start[x, span, :] for x in range(size_x)])
        for ref, table in zip(refs, tables):

            def read(j, ref=ref):
                return [ref[x, pl.ds(pl.multiple_of(8 * j, 8), 8), :] for x in range(size_x)]

            accs = sweep(accs, blocks, read, table, size_y - 8, 0, size_y // 8)
        for b, row in zip(blocks, accs):
            for x, v in enumerate(row):
                out_ref[x, 8 * b : 8 * b + 8, :] = v if scale == 1.0 else v * scale


CODES = 4681.0
LN2 = 0.6931471805599453


def encode_kernel(value_ref, code_ref):
    code = jnp.round(jnp.log(value_ref[...] + 1.0) * (CODES / LN2)) - 32768.0
    code_ref[...] = jnp.clip(code, -32768.0, 32767.0).astype(jnp.int32).astype(jnp.int16)


def decode(code):
    level = code.astype(jnp.int32).astype(jnp.float32) + 32768.0
    return jnp.exp(level * (LN2 / CODES)) - 1.0


def y_own_kernel(own_ref, table, out_ref):
    y_sweep((own_ref,), (table,), None, out_ref, 1.0)


def y_far_kernel(start_ref, code_ref, table, out_ref, block):
    block[...] = decode(code_ref[...])
    y_sweep((block,), (table,), start_ref, out_ref, 1.0)


def y_last_kernel(start_ref, code_ref, table, score_in, out_ref, score_ref, block):
    index = lax.axis_index("gy")
    near = jnp.abs((index ^ 3) - index) < 3
    score_ref[...] = score_in[...]

    @pl.when(near)
    def _():
        block[...] = decode(code_ref[...])
        y_sweep((block,), (table,), start_ref, out_ref, 1.0 / RADIUS)

    @pl.when(jnp.logical_not(near))
    def _():
        out_ref[...] = start_ref[...] * (1.0 / RADIUS)


def swap(value, axis, hop):
    n = lax.axis_size(axis)
    return lax.ppermute(value, axis, [(i, i ^ hop) for i in range(n)])


def swap_xy(value, hop_x, hop_y):
    nx, ny = lax.axis_size("gx"), lax.axis_size("gy")
    pairs = [(x * ny + y, (x ^ hop_x) * ny + (y ^ hop_y)) for x in range(nx) for y in range(ny)]
    return lax.ppermute(value, ("gx", "gy"), pairs)


def neighbours(low, high, axis, beyond=0.0):
    n, index = lax.axis_size(axis), lax.axis_index(axis)
    odd = index % 2 == 1
    pairs = [(i, i + 1 if i % 2 else i - 1) for i in range(1, n - 1)]
    got_odd = lax.ppermute(jnp.where(odd, high, low), axis, pairs)
    got_even = lax.ppermute(jnp.where(odd, low, high), axis, [(i, i ^ 1) for i in range(n)])
    from_low = jnp.where(odd, got_even, got_odd)
    from_high = jnp.where(odd, got_odd, got_even)
    return jnp.where(index == 0, beyond, from_low), jnp.where(index == n - 1, beyond, from_high)


def z_swaps(value):
    nx, ny, n = (lax.axis_size(axis) for axis in ("gx", "gy", "gz"))
    even = lax.ppermute(value, "gz", [(i, i ^ 1) for i in range(n)])
    pairs = []
    for i in range(nx * ny * n):
        xy, z = i // n, i % n
        pairs.append((i, (xy ^ 1) * n + z if z in (0, n - 1) else xy * n + (z + 1 if z % 2 else z - 1)))
    return even, lax.ppermute(value, ("gx", "gy", "gz"), pairs)


def corner_swap(value):
    nx, ny = lax.axis_size("gx"), lax.axis_size("gy")
    pairs = []
    for i in range(nx * ny):
        x, y = i // ny, i % ny
        pairs.append((i, (x ^ 1) * ny + y if y in (0, ny - 1) else x * ny + (y + 1 if y % 2 else y - 1)))
    return lax.ppermute(value, ("gx", "gy"), pairs)


def conv(features, conv_weight, mask, planes, count, paired):
    channels, size_x, size_y, _ = features.shape
    return call(
        functools.partial(conv_kernel, planes, paired),
        [(size_x, size_y, LANES), (count * size_y + 8, LANES), (16, LANES), (16, LANES)],
        [
            pltpu.VMEM(features.shape, jnp.bfloat16),
            pltpu.VMEM(conv_weight.shape, jnp.bfloat16),
            pltpu.VMEM(mask.shape, jnp.int32),
            pltpu.VMEM((9 * ROWS + 8, channels * 16), jnp.bfloat16),
            pltpu.VMEM((size_x + 2, 3, ROWS, size_y // 16 * LANES), jnp.float32),
            pltpu.SemaphoreType.DMA((size_x + 2,)),
        ],
        mib=24,
        in_specs=[HBM] * 3,
    )(*(pltpu.with_memory_space_constraint(v, pltpu.HBM) for v in (features, conv_weight, mask)))


def halo_with_partner(features, conv_weight, mask):
    _, size_x, size_y, _ = features.shape

    def planes():
        return [*range(1, size_x + 1), jnp.where(lax.axis_index("gx") == 0, size_x + 1, 0)]

    s, own, chip, cross = conv(features, conv_weight, mask, planes, size_x + 1, True)
    far = swap_xy(own, 1, 0)
    sides = [swap_xy(cross, 0, 3), swap_xy(cross, 1, 3), swap_xy(chip, 0, 1), swap_xy(chip, 1, 1)]
    return call(turn_kernel, [(size_x, size_y, LANES), (LANES + 8, size_x * size_y)])(s, own, far, *sides)


def halo_in_rounds(features, conv_weight, mask):
    _, size_x, size_y, _ = features.shape
    groups = size_y // 8
    planes = [*range(1, size_x + 1), 0, size_x + 1]
    s, rest, down, up = conv(features, conv_weight, mask, lambda: planes, size_x + 2, False)

    def whole(k):
        h = jnp.roll(rest[len(planes) * size_y :], -16 * k, 1)
        part = s[k] if k < size_x else rest[k * size_y : (k + 1) * size_y]
        return jnp.concatenate([part, h, *(e[i : i + 1] for e in (down, up) for i in (k, 8 + k))], axis=0)

    low, high = neighbours(whole(size_x), whole(size_x + 1), "gx")
    own = jnp.stack([whole(k) for k in range(size_x)]).at[0].add(low).at[size_x - 1].add(high)
    e = own[:, size_y + 8 :]
    low, high = neighbours(e[:, 0:2], e[:, 2:4], "gy")
    own = own.at[:, 0].add(low[:, 0]).at[:, size_y - 1].add(high[:, 0])
    own = own.at[:, size_y].add(low[:, 1]).at[:, size_y + 7].add(high[:, 1])
    score, h = own[:, :size_y], own[:, size_y : size_y + 8]

    def line(value):
        return value.reshape(1, size_x * size_y)

    up = jnp.swapaxes(h[:, :, 0 : 2 * groups : 2], 1, 2)
    down = jnp.swapaxes(jnp.roll(h, 1, 2)[:, :, 0 : 2 * groups : 2], 1, 2)
    masked = jnp.where(mask == 1, HUGE, score)
    rows = jnp.transpose(cost_of(masked), (2, 0, 1)).reshape(LANES, size_x * size_y)
    ends = [line(v) for v in (masked[:, :, 0], masked[:, :, LANES - 1], down, up)]
    blank = [jnp.full_like(ends[0], HUGE)] * 2 + [jnp.zeros_like(ends[0])] * 2
    pairs = [v for pair in zip(ends, blank) for v in pair]
    return score, jnp.concatenate([rows, *pairs], axis=0)


def x_minima(value, size_x):
    n, index = lax.axis_size("gx"), lax.axis_index("gx")
    every = lax.all_gather(value, "gx", axis=0, tiled=True)
    at = index * size_x + jnp.arange(size_x)
    d = (at[:, None] - jnp.arange(n * size_x)[None, :]).astype(jnp.float32)
    return jnp.min(every[None] + (d * d)[:, :, None, None], axis=1)


def shards(features, conv_weight, mask):
    _, size_x, size_y, size_z = features.shape
    gx, gy = lax.axis_size("gx"), lax.axis_size("gy")
    assert size_z == LANES and size_y % 16 == 0 and LANES % size_y == 0 and gy == 4
    brick = (size_x, size_y, LANES)
    lines = size_x * size_y
    partner = gx == 2

    halo = halo_with_partner if partner else halo_in_rounds
    score, zm = halo(features, conv_weight, mask)

    even, odd = z_swaps(zm)
    tables = (2 * size_y - 8, 8, LANES)
    own = functools.partial(z_own_kernel, size_y)
    best, table, *kept = call(own, [(LANES, lines), (LANES - Z_FLOOR, 8, LANES)] + [tables] * 4)(zm)
    work = [pltpu.VMEM((LANES, lines), jnp.float32)] * 2
    for first, got, shape in ((True, even, (LANES, lines)), (False, odd, brick)):
        far = functools.partial(z_far_kernel, first, partner, size_x, size_y)
        (best,) = call(far, [shape], work)(best, table, zm, got)
    (score,) = call(score_kernel, [brick])(score, even, odd, best)
    if not partner:
        best = x_minima(best, size_x)

    (code,) = call(encode_kernel, [brick], kind=jnp.int16)(best)
    blocks = {2: swap(code, "gy", 2), 1: swap(code, "gy", 1), 3: corner_swap(code)}
    (near,) = call(y_own_kernel, [brick])(best, kept[0])
    block = [pltpu.VMEM(brick, jnp.float32)]
    for hop in (2, 1):
        (near,) = call(y_far_kernel, [brick], block)(near, blocks[hop], kept[hop])
    depth, score = call(y_last_kernel, [brick, brick], block)(near, blocks[3], kept[3], score)
    return score, depth


def solution(mesh):
    in_specs = (P(None, "gx", "gy", "gz"), P(), P("gx", "gy", "gz"))
    out_specs = (P("gx", "gy", "gz"), P("gx", "gy", "gz"))
    return jax.shard_map(shards, mesh=mesh, in_specs=in_specs, out_specs=out_specs, check_vma=False)
```

```python
import functools

import jax
import jax.numpy as jnp
from jax import lax
from jax.experimental import pallas as pl
from jax.experimental.pallas import tpu as pltpu
from jax.sharding import PartitionSpec as P

RADIUS = 128
CEILING = float(RADIUS * RADIUS)
HUGE = 1e30
LANES = 128
ROWS = 24
VMEM = pl.BlockSpec(memory_space=pltpu.VMEM)
HBM = pl.BlockSpec(memory_space=pltpu.HBM)


def call(kernel, outs, scratch=(), mib=8, in_specs=None, kind=jnp.float32, out_spec=VMEM):
    shapes = [s if isinstance(s, jax.ShapeDtypeStruct) else jax.ShapeDtypeStruct(s, kind) for s in outs]

    def run(*args):
        return pl.pallas_call(
            kernel,
            out_shape=shapes,
            in_specs=in_specs or [VMEM] * len(args),
            out_specs=[out_spec] * len(shapes),
            scratch_shapes=list(scratch),
            compiler_params=pltpu.CompilerParams(vmem_limit_bytes=mib * 1024 * 1024),
        )(*args)

    return run


def lane_of(shape):
    return lax.broadcasted_iota(jnp.int32, shape, len(shape) - 1)


def row_of(shape):
    return lax.broadcasted_iota(jnp.int32, shape, len(shape) - 2)


def cost_of(score):
    return CEILING / (1.0 + jnp.exp(-score))


def conv_kernel(
    planes, paired, f_hbm, w_hbm, mask_hbm, s_ref, m_ref, e_ref, d_ref, f_vmem, w_vmem, mask_vmem, w_big, acc, sems
):
    channels, size_x, size_y, _ = f_vmem.shape
    tiles = size_y // 16
    depth = channels * 16
    weights = pltpu.make_async_copy(w_hbm, w_vmem, sems.at[size_x])
    weights.start()
    copies = [
        pltpu.make_async_copy(f_hbm.at[:, x], f_vmem.at[:, x], sems.at[x]) for x in range(size_x)
    ]
    masks = pltpu.make_async_copy(mask_hbm, mask_vmem, sems.at[size_x + 1])
    masks.start()
    for copy in copies:
        copy.start()

    spread = (
        lax.broadcasted_iota(jnp.int32, (channels, depth), 1) // 16
        == lax.broadcasted_iota(jnp.int32, (channels, depth), 0)
    ).astype(jnp.bfloat16)
    row = lax.broadcasted_iota(jnp.int32, (ROWS, depth), 0)
    y_in = lax.broadcasted_iota(jnp.int32, (ROWS, depth), 1) % 16
    y_out = jnp.where(row <= 16, row, jnp.where(row == ROWS - 1, -1, 64))
    tap = y_in - y_out + 1
    weights.wait()
    wide = jnp.dot(w_vmem[...], spread, preferred_element_type=jnp.float32)
    blocks = []
    for a in range(3):
        for c in range(3):
            block = jnp.zeros((ROWS, depth), jnp.float32)
            for b in range(3):
                k = 9 * a + 3 * b + c
                block = jnp.where(tap == b, wide[k : k + 1, :], block)
            blocks.append(block)
    blocks.append(jnp.zeros((8, depth), jnp.float32))
    w_big[...] = jnp.concatenate(blocks, axis=0).astype(jnp.bfloat16)

    shape = (8, LANES)
    row, lane = row_of(shape), lane_of(shape)
    groups = size_y // 8
    to_first = lax.axis_index("gy") % 2 == 1 if paired else True
    folds = []

    def finish(p, at):
        fold = None
        for g in range(groups + 1):
            sums = []
            for c in range(3):

                def piece(tile, low, c=c):
                    return acc[at, c, low : low + 8, tile * LANES : tile * LANES + LANES]

                if g == groups:
                    part = jnp.where(row == 0, piece(tiles - 1, 16), piece(0, 16))
                else:
                    tile, low = g // 2, 8 * (g % 2)
                    part = piece(tile, low)
                    if low == 0 and tile > 0:
                        part = part + jnp.where(row == 0, piece(tile - 1, 16), 0.0)
                    if low == 8 and tile < tiles - 1:
                        part = part + jnp.where(row == 7, piece(tile + 1, 16), 0.0)
                sums.append(part)
            ahead = pltpu.roll(sums[0], 1, 1)
            behind = pltpu.roll(sums[2], LANES - 1, 1)
            inner = (
                sums[1] + jnp.where(lane == 0, 0.0, ahead) + jnp.where(lane == LANES - 1, 0.0, behind)
            )
            outer = jnp.where(lane == 0, ahead, jnp.where(lane == LANES - 1, behind, 0.0))
            if g == groups:
                for up, down, at_row in (
                    (inner, inner, p),
                    (outer, pltpu.roll(outer, 2 * (groups - 1), 1), 8 + p),
                ):
                    e_ref[at_row : at_row + 1, :] = jnp.where(to_first, down[7:8], up[0:1])
                    d_ref[at_row : at_row + 1, :] = jnp.where(to_first, up[0:1], down[7:8])
            else:
                span = slice(8 * g, 8 * g + 8)
                if p < size_x:
                    s_ref[p, span, :] = inner
                    inner = jnp.where(mask_vmem[p, span, :] == 1, HUGE, inner)
                m_ref[p * size_y + 8 * g : p * size_y + 8 * g + 8, :] = inner
                shift = 16 * p + 2 * g
                outer = pltpu.roll(outer, shift, 1) if shift else outer
                fold = outer if g == 0 else fold + outer
        folds.append(fold)

    at_plane = planes()
    half = size_x // 2
    for x in range(size_x):
        if x % half == 0:
            for copy in copies[x : x + half]:
                copy.wait()
            if x:
                masks.wait()
                for p in range(x - 1):
                    finish(p, at_plane[p])
        right = jnp.concatenate(
            [f_vmem[:, x, 16 * t : 16 * t + 16, :].reshape(depth, LANES) for t in range(tiles)],
            axis=1,
        )
        got = jnp.dot(w_big[...], right, preferred_element_type=jnp.float32)
        for a in range(3):
            at = x + 2 - a
            for c in range(3):
                first = (3 * a + c) * ROWS
                part = got[first : first + ROWS, :]
                acc[at, c] = part if a == 0 or x == 0 else acc[at, c] + part
    for p in range(half - 1, len(at_plane)):
        finish(p, at_plane[p])
    m_ref[len(folds) * size_y :, :] = functools.reduce(jnp.add, folds)


CODES = 4681.0
LN2 = 0.6931471805599453
TOP = 2.0**30


def encode(value):
    code = jnp.round(jnp.log(value + 1.0) * (CODES / LN2)) - 32768.0
    return jnp.clip(code, -32768.0, 32767.0).astype(jnp.int32)


def decode(code):
    level = code.astype(jnp.int32).astype(jnp.float32) + 32768.0
    return jnp.exp(level * (LN2 / CODES)) - 1.0


def pack_z(rows, ends):
    half = LANES // 2
    code = encode(rows)
    masked = ends >= 0.5 * HUGE
    most = jnp.max(jnp.where(masked, 0.0, jnp.abs(ends)), axis=1, keepdims=True)
    most = jnp.max(most, axis=0, keepdims=True)
    power = jnp.ceil(jnp.log(jnp.maximum(most, 1e-18)) * (1.0 / LN2)) + 1.0
    scores = jnp.round(jnp.where(masked, TOP, ends * (jnp.exp(power * -LN2) * TOP))).astype(jnp.int32)
    first = jnp.where(row_of((half, rows.shape[1])) == 0, power.astype(jnp.int32), code[:half])
    return jnp.concatenate([(first << 16) | (code[half:] & 0xFFFF), scores], axis=0)


def unpack_rows(words):
    return decode(words >> 16), decode((words << 16) >> 16)


def unpack_ends(ref):
    half = LANES // 2
    power = (ref[0:8, :] >> 16)[0:1].astype(jnp.float32)
    scores = ref[half : half + 8, :].astype(jnp.float32)
    return jnp.where(scores >= 0.75 * TOP, HUGE, scores * (jnp.exp(power * LN2) * (1.0 / TOP)))


def y_masks(axis, chip):
    row = row_of((8, LANES))
    index, last = lax.axis_index(axis), lax.axis_size(axis) - 1
    odd = index % 2
    if chip:
        low, high = odd == 1, odd == 0
    else:
        low, high = (odd == 0) & (index > 0), (odd == 1) & (index < last)
    return row == jnp.where(low, 0, -1), row == jnp.where(high, 7, -1)


def edge_rows(masks, part, size_y):
    low, high = masks
    return jnp.concatenate(
        [
            jnp.where(low, part, 0.0),
            jnp.zeros((size_y - 16, LANES), jnp.float32),
            jnp.where(high, part, 0.0),
        ],
        axis=0,
    )


def turn_kernel(s_ref, own_ref, far_ref, cross_ref, xcross_ref, chip_ref, xchip_ref, score_ref, zm_ref, words_ref):
    size_x, size_y, _ = s_ref.shape
    chip, cross = y_masks("gy", True), y_masks("gy", False)
    first = lax.axis_index("gx") == 0
    lane = lane_of((size_y, LANES))
    border = (lane == 0) | (lane == LANES - 1)
    faces_own = {size_x - 1: jnp.where(first, 1.0, 0.0), 0: jnp.where(first, 0.0, 1.0)}
    faces_far = {0: faces_own[size_x - 1], size_x - 1: faces_own[0]}

    def plane(ref, p):
        return ref[p * size_y : (p + 1) * size_y, :]

    def fold(ref, p):
        rest = ref[(size_x + 1) * size_y :, :]
        return pltpu.roll(rest, LANES - 16 * p, 1) if p else rest

    def complete(p, base, folded, face_ref, sides, faces):
        if p in faces:
            base = base + faces[p] * plane(face_ref, size_x)
            folded = folded + faces[p] * fold(face_ref, size_x)
        for masks, same, other in sides:
            part, part_h = same[p : p + 1], same[8 + p : 9 + p]
            if p in faces:
                part = part + faces[p] * other[size_x : size_x + 1]
                part_h = part_h + faces[p] * other[8 + size_x : 9 + size_x]
            base = base + edge_rows(masks, part, size_y)
            folded = folded + jnp.where(masks[0] | masks[1], part_h, 0.0)
        return base, folded

    costs, turned = [], []
    for far in range(2):
        for p in range(size_x):
            if far:
                sides = ((chip, xchip_ref, chip_ref), (cross, xcross_ref, cross_ref))
                masked, h = complete(p, plane(far_ref, p), fold(far_ref, p), own_ref, sides, faces_far)
            else:
                sides = ((chip, chip_ref, xchip_ref), (cross, cross_ref, xcross_ref))
                full, h = complete(p, s_ref[p], fold(own_ref, p), far_ref, sides, faces_own)
                score_ref[p] = full
                masked = jnp.where(plane(own_ref, p) == HUGE, HUGE, full)
            costs.append(cost_of(masked))
            wide = jnp.concatenate(
                [pltpu.roll(h, (2 - 2 * g) % LANES, 1) for g in range(size_y // 8)], axis=0
            )
            turned.append(jnp.where(border, masked, wide))
    away = jnp.where(first, float(size_x), -float(size_x))
    lines = []
    for i in range(size_x):
        best = costs[i]
        for j in range(size_x):
            if j != i:
                best = jnp.minimum(best, costs[j] + float((i - j) ** 2))
            d = float(j - i) + away
            best = jnp.minimum(best, costs[size_x + j] + d * d)
        lines.append(best)
    width = size_x * size_y
    rows = jnp.concatenate(lines, axis=0).T
    ends = jnp.concatenate(turned, axis=0).T
    ends = jnp.concatenate(
        [ends[r : r + 1, k * width : (k + 1) * width] for r in (0, LANES - 1, 1, 2) for k in range(2)],
        axis=0,
    )
    zm_ref[0:LANES, :] = rows
    zm_ref[LANES : LANES + 8, :] = ends
    words_ref[...] = pack_z(rows, ends)


Z_FLOOR = -(LANES + 6)


def sweep(accs, blocks, read, table, shift, low, high):
    parts = len(accs[0])

    def body(j, flat):
        flat = list(flat)
        tiles = read(j)
        squares = table.at[pl.ds(shift + 8 * blocks[0] - 8 * j, 8 * len(blocks))]
        for r in range(8):
            rows = [jnp.broadcast_to(t[r : r + 1, :], (8, LANES)) for t in tiles]
            for i in range(len(blocks)):
                square = squares[8 * i + 7 - r]
                for k in range(parts):
                    at = i * parts + k
                    flat[at] = jnp.minimum(flat[at], rows[k] + square)
        return tuple(flat)

    flat = lax.fori_loop(low, high, body, tuple(v for row in accs for v in row))
    return [list(flat[i * parts : (i + 1) * parts]) for i in range(len(blocks))]


def tiles_of(ref, j):
    rows = pl.ds(pl.multiple_of(8 * j, 8), 8)
    return [ref[rows, k * LANES : (k + 1) * LANES] for k in range(ref.shape[1] // LANES)]


def load_blocks(ref, blocks):
    return [tiles_of(ref, b) for b in blocks]


def save_blocks(ref, blocks, accs):
    for b, row in zip(blocks, accs):
        for k, v in enumerate(row):
            ref[8 * b : 8 * b + 8, k * LANES : (k + 1) * LANES] = v


def y_table(axis, hop, size_y, table):
    index = lax.axis_index(axis)
    away = (((index ^ hop) - index) * size_y).astype(jnp.float32)
    s = row_of((8, LANES)).astype(jnp.float32) - away
    for d in range(1 - size_y, size_y - 7):
        v = s + float(d)
        table[d - (1 - size_y)] = v * v


def z_own_kernel(size_y, zm_ref, out_ref, table, *y_tables):
    count, half = LANES // 8, LANES // 16
    for hop, y_one in enumerate(y_tables):
        y_table("gy", hop, size_y, y_one)
    s = row_of((8, LANES)).astype(jnp.float32)
    for d in range(Z_FLOOR, LANES):
        v = s + float(d)
        table[d - Z_FLOOR] = v * v

    def read(j):
        at = row_of((8, LANES)) + 8 * j
        hide = (at == 0) | (at == LANES - 1)
        return [jnp.where(hide, HUGE, t) for t in tiles_of(zm_ref, j)]

    for first in (0, half):
        blocks = range(first, first + half)
        accs = [[jnp.full((8, LANES), HUGE, jnp.float32)] * (out_ref.shape[1] // LANES) for _ in blocks]
        save_blocks(out_ref, blocks, sweep(accs, blocks, read, table, -7 - Z_FLOOR, 0, count))


def border_minima(cost, size_x, size_y, partner):
    if not partner:
        return cost
    width = cost.shape[1]
    shape = (8, width)
    row, plane = row_of(shape), lane_of(shape) // size_y
    away = jnp.where(lax.axis_index("gx") == 0, size_x, -size_x)
    shift = jnp.where(row % 2 == 1, away, 0)
    best = None
    for r in range(size_x):
        source = jnp.where(plane >= r, plane - r, plane - r + size_x)
        d = (source + shift - plane).astype(jnp.float32)
        if r == 0:
            moved = cost
        else:
            cut = width - r * size_y
            moved = jnp.concatenate([cost[:, cut:], cost[:, :cut]], axis=1)
        moved = moved + d * d
        best = moved if best is None else jnp.minimum(best, moved)
    return jnp.minimum(best, pltpu.roll(best, 7, 0))


def z_far_kernel(even, partner, size_x, size_y, acc_ref, table, zm_ref, got_ref, out_ref, source, work):
    index, last = lax.axis_index("gz"), lax.axis_size("gz") - 1
    odd = index % 2 == 1
    low = odd if even else jnp.logical_not(odd)
    valid = jnp.where(low, index > 0, index < last)
    count, half = LANES // 8, LANES // 16
    out = out_ref if even else work

    own, got = zm_ref[LANES : LANES + 8, :], unpack_ends(got_ref)
    mine = jnp.where(low, own[0:2], own[2:4]) + jnp.where(valid, jnp.where(low, got[6:8], got[4:6]), 0.0)
    theirs = jnp.where(low, got[2:4] + own[4:6], got[0:2] + own[6:8])
    ends = border_minima(cost_of(jnp.concatenate([mine, theirs, mine, theirs], axis=0)), size_x, size_y, partner)
    source[0 : LANES // 2, :], source[LANES // 2 :, :] = unpack_rows(got_ref[0 : LANES // 2, :])

    squares = table.at[pl.ds(jnp.where(low, -Z_FLOOR, 1 - LANES - Z_FLOOR), LANES)]
    lanes = [slice(k * LANES, (k + 1) * LANES) for k in range(zm_ref.shape[1] // LANES)]
    rows = [jnp.broadcast_to(ends[0:1, cols], (8, LANES)) for cols in lanes]
    for b in range(count):
        for row, cols in zip(rows, lanes):
            span = slice(8 * b, 8 * b + 8)
            out[span, cols] = jnp.minimum(acc_ref[span, cols], row + squares[8 * b])

    def slanted(accs, blocks, offset, tiles, reach):
        for j in tiles:
            tile = tiles_of(source, j)
            for r in range(8):
                q = 8 * j + r
                rows = [jnp.broadcast_to(t[r : r + 1, :], (8, LANES)) for t in tile]
                for i, b in enumerate(blocks):
                    if reach(b, q):
                        square = table[8 * b - q + offset - Z_FLOOR]
                        accs[i] = [jnp.minimum(v, row + square) for v, row in zip(accs[i], rows)]
        return accs

    @pl.when(valid & low)
    def _():
        source[LANES - 1 : LANES, :] = ends[2:3]
        for first in (0, half):
            blocks = range(first, first + half)
            accs = load_blocks(out, blocks)
            accs = slanted(accs, blocks, LANES, blocks, lambda b, q: 8 * b < q)
            if blocks[-1] + 1 < count:
                read = functools.partial(tiles_of, source)
                accs = sweep(accs, blocks, read, table, LANES - 7 - Z_FLOOR, blocks[-1] + 1, count)
            save_blocks(out, blocks, accs)

    @pl.when(valid & jnp.logical_not(low))
    def _():
        source[0:1, :] = ends[2:3]
        for first in (0, half):
            blocks = range(first, first + half)
            accs = load_blocks(out, blocks)
            accs = slanted(accs, blocks, -LANES, blocks, lambda b, q: q < 8 * b + 7)
            if first:
                read = functools.partial(tiles_of, source)
                accs = sweep(accs, blocks, read, table, -LANES - 7 - Z_FLOOR, 0, first)
            save_blocks(out, blocks, accs)

    if not even:
        per = LANES // size_y
        for k, cols in enumerate(lanes):
            best = work[:, cols].T
            for i in range(per):
                out_ref[k * per + i] = best[i * size_y : (i + 1) * size_y]


def score_kernel(score_in, even_ref, odd_ref, _, score_ref):
    index, last = lax.axis_index("gz"), lax.axis_size("gz") - 1
    odd = index % 2 == 1
    size_y = score_in.shape[1]
    per = LANES // size_y
    even_ends, odd_ends = unpack_ends(even_ref), unpack_ends(odd_ref)
    for k in range(even_ref.shape[1] // LANES):
        cols = slice(k * LANES, (k + 1) * LANES)
        even_rows, odd_rows = even_ends[:, cols], odd_ends[:, cols]
        low = jnp.where(index > 0, jnp.where(odd, even_rows, odd_rows)[6:7], 0.0)
        high = jnp.where(index < last, jnp.where(odd, odd_rows, even_rows)[4:5], 0.0)
        middle = jnp.zeros((LANES - 2, LANES), jnp.float32)
        more = jnp.concatenate([low, middle, high], axis=0).T
        for i in range(per):
            x = k * per + i
            score_ref[x] = score_in[x] + more[i * size_y : (i + 1) * size_y]


Y_BLOCKS = 4


def y_sweep(refs, tables, start, out_ref, scale, span=None):
    size_x, size_y, _ = out_ref.shape
    span = span or range(size_y // 8)
    for first in range(span[0], span[-1] + 1, Y_BLOCKS):
        blocks = range(first, first + Y_BLOCKS)
        accs = []
        for b in blocks:
            span = slice(8 * b, 8 * b + 8)
            blank = jnp.full((8, LANES), HUGE, jnp.float32)
            accs.append([blank if start is None else start[x, span, :] for x in range(size_x)])
        for ref, table in zip(refs, tables):

            def read(j, ref=ref):
                return [ref[x, pl.ds(pl.multiple_of(8 * j, 8), 8), :] for x in range(size_x)]

            accs = sweep(accs, blocks, read, table, size_y - 8, 0, size_y // 8)
        for b, row in zip(blocks, accs):
            for x, v in enumerate(row):
                out_ref[x, 8 * b : 8 * b + 8, :] = v if scale == 1.0 else v * scale


def encode_kernel(value_ref, code_ref):
    code_ref[...] = encode(value_ref[...]).astype(jnp.int16)


def y_own_kernel(own_ref, table, out_ref):
    y_sweep((own_ref,), (table,), None, out_ref, 1.0)


def in_reach(hop):
    index = lax.axis_index("gy")
    return jnp.abs((index ^ hop) - index) < 3


def y_far_kernel(hop, start_ref, code_ref, table, out_ref, block):
    near = in_reach(hop)

    @pl.when(near)
    def _():
        block[...] = decode(code_ref[...])
        y_sweep((block,), (table,), start_ref, out_ref, 1.0)

    @pl.when(jnp.logical_not(near))
    def _():
        out_ref[...] = start_ref[...]


def y_last_kernel(hop, start_ref, code_ref, table, score_ref, depth_hbm, score_hbm, block, depth, sems):
    near = in_reach(hop)
    size_y = depth.shape[1]
    scores = pltpu.make_async_copy(score_ref, score_hbm, sems.at[0])
    scores.start()
    parts = [
        pltpu.make_async_copy(depth.at[:, rows], depth_hbm.at[:, rows], sems.at[1 + i])
        for i, rows in enumerate(pl.ds(f, size_y // 2) for f in (0, size_y // 2))
    ]

    @pl.when(near)
    def _():
        block[...] = decode(code_ref[...])
        half = size_y // 16
        for i, part in enumerate(parts):
            y_sweep((block,), (table,), start_ref, depth, 1.0 / RADIUS, range(i * half, (i + 1) * half))
            part.start()

    @pl.when(jnp.logical_not(near))
    def _():
        depth[...] = start_ref[...] * (1.0 / RADIUS)
        for part in parts:
            part.start()

    for copy in (scores, *parts):
        copy.wait()


def swap(value, axis, hop):
    n = lax.axis_size(axis)
    return lax.ppermute(value, axis, [(i, i ^ hop) for i in range(n)])


def swap_xy(value, hop_x, hop_y):
    nx, ny = lax.axis_size("gx"), lax.axis_size("gy")
    pairs = [(x * ny + y, (x ^ hop_x) * ny + (y ^ hop_y)) for x in range(nx) for y in range(ny)]
    return lax.ppermute(value, ("gx", "gy"), pairs)


def neighbours(low, high, axis, beyond=0.0):
    n, index = lax.axis_size(axis), lax.axis_index(axis)
    odd = index % 2 == 1
    pairs = [(i, i + 1 if i % 2 else i - 1) for i in range(1, n - 1)]
    got_odd = lax.ppermute(jnp.where(odd, high, low), axis, pairs)
    got_even = lax.ppermute(jnp.where(odd, low, high), axis, [(i, i ^ 1) for i in range(n)])
    from_low = jnp.where(odd, got_even, got_odd)
    from_high = jnp.where(odd, got_odd, got_even)
    return jnp.where(index == 0, beyond, from_low), jnp.where(index == n - 1, beyond, from_high)


def z_swaps(value):
    nx, ny, n = (lax.axis_size(axis) for axis in ("gx", "gy", "gz"))
    even = lax.ppermute(value, "gz", [(i, i ^ 1) for i in range(n)])
    pairs = []
    for i in range(nx * ny * n):
        xy, z = i // n, i % n
        pairs.append((i, (xy ^ 1) * n + z if z in (0, n - 1) else xy * n + (z + 1 if z % 2 else z - 1)))
    return even, lax.ppermute(value, ("gx", "gy", "gz"), pairs)


def corner_swap(value):
    nx, ny = lax.axis_size("gx"), lax.axis_size("gy")
    pairs = []
    for i in range(nx * ny):
        x, y = i // ny, i % ny
        pairs.append((i, (x ^ 1) * ny + y if y in (0, ny - 1) else x * ny + (y + 1 if y % 2 else y - 1)))
    return lax.ppermute(value, ("gx", "gy"), pairs)


def conv(features, conv_weight, mask, planes, count, paired):
    channels, size_x, size_y, _ = features.shape
    return call(
        functools.partial(conv_kernel, planes, paired),
        [(size_x, size_y, LANES), (count * size_y + 8, LANES), (16, LANES), (16, LANES)],
        [
            pltpu.VMEM(features.shape, jnp.bfloat16),
            pltpu.VMEM(conv_weight.shape, jnp.bfloat16),
            pltpu.VMEM(mask.shape, jnp.int32),
            pltpu.VMEM((9 * ROWS + 8, channels * 16), jnp.bfloat16),
            pltpu.VMEM((size_x + 2, 3, ROWS, size_y // 16 * LANES), jnp.float32),
            pltpu.SemaphoreType.DMA((size_x + 2,)),
        ],
        mib=24,
        in_specs=[HBM] * 3,
    )(*(pltpu.with_memory_space_constraint(v, pltpu.HBM) for v in (features, conv_weight, mask)))


def halo_with_partner(features, conv_weight, mask):
    _, size_x, size_y, _ = features.shape

    def planes():
        return [*range(1, size_x + 1), jnp.where(lax.axis_index("gx") == 0, size_x + 1, 0)]

    s, own, chip, cross = conv(features, conv_weight, mask, planes, size_x + 1, True)
    far = swap_xy(own, 1, 0)
    sides = [swap_xy(cross, 0, 3), swap_xy(cross, 1, 3), swap_xy(chip, 0, 1), swap_xy(chip, 1, 1)]
    lines = size_x * size_y
    words = jax.ShapeDtypeStruct((LANES // 2 + 8, lines), jnp.int32)
    return call(turn_kernel, [(size_x, size_y, LANES), (LANES + 8, lines), words])(s, own, far, *sides)


def halo_in_rounds(features, conv_weight, mask):
    _, size_x, size_y, _ = features.shape
    groups = size_y // 8
    planes = [*range(1, size_x + 1), 0, size_x + 1]
    s, rest, down, up = conv(features, conv_weight, mask, lambda: planes, size_x + 2, False)

    def whole(k):
        h = jnp.roll(rest[len(planes) * size_y :], -16 * k, 1)
        part = s[k] if k < size_x else rest[k * size_y : (k + 1) * size_y]
        return jnp.concatenate([part, h, *(e[i : i + 1] for e in (down, up) for i in (k, 8 + k))], axis=0)

    low, high = neighbours(whole(size_x), whole(size_x + 1), "gx")
    own = jnp.stack([whole(k) for k in range(size_x)]).at[0].add(low).at[size_x - 1].add(high)
    e = own[:, size_y + 8 :]
    low, high = neighbours(e[:, 0:2], e[:, 2:4], "gy")
    own = own.at[:, 0].add(low[:, 0]).at[:, size_y - 1].add(high[:, 0])
    own = own.at[:, size_y].add(low[:, 1]).at[:, size_y + 7].add(high[:, 1])
    score, h = own[:, :size_y], own[:, size_y : size_y + 8]

    def line(value):
        return value.reshape(1, size_x * size_y)

    up = jnp.swapaxes(h[:, :, 0 : 2 * groups : 2], 1, 2)
    down = jnp.swapaxes(jnp.roll(h, 1, 2)[:, :, 0 : 2 * groups : 2], 1, 2)
    masked = jnp.where(mask == 1, HUGE, score)
    rows = jnp.transpose(cost_of(masked), (2, 0, 1)).reshape(LANES, size_x * size_y)
    ends = [line(v) for v in (masked[:, :, 0], masked[:, :, LANES - 1], down, up)]
    blank = [jnp.full_like(ends[0], HUGE)] * 2 + [jnp.zeros_like(ends[0])] * 2
    pairs = [v for pair in zip(ends, blank) for v in pair]
    ends = jnp.concatenate(pairs, axis=0)
    return score, jnp.concatenate([rows, ends], axis=0), pack_z(rows, ends)


def x_minima(value, size_x):
    n, index = lax.axis_size("gx"), lax.axis_index("gx")
    every = lax.all_gather(value, "gx", axis=0, tiled=True)
    at = index * size_x + jnp.arange(size_x)
    d = (at[:, None] - jnp.arange(n * size_x)[None, :]).astype(jnp.float32)
    return jnp.min(every[None] + (d * d)[:, :, None, None], axis=1)


def shards(features, conv_weight, mask):
    _, size_x, size_y, size_z = features.shape
    gx, gy = lax.axis_size("gx"), lax.axis_size("gy")
    assert size_z == LANES and size_y % 16 == 0 and LANES % size_y == 0 and gy == 4
    brick = (size_x, size_y, LANES)
    lines = size_x * size_y
    partner = gx == 2

    halo = halo_with_partner if partner else halo_in_rounds
    score, zm, words = halo(features, conv_weight, mask)

    even, odd = z_swaps(words)
    tables = (2 * size_y - 8, 8, LANES)
    own = functools.partial(z_own_kernel, size_y)
    best, table, *kept = call(own, [(LANES, lines), (LANES - Z_FLOOR, 8, LANES)] + [tables] * 4)(zm)
    work = [pltpu.VMEM((LANES, lines), jnp.float32)] * 2
    for first, got, shape in ((True, even, (LANES, lines)), (False, odd, brick)):
        far = functools.partial(z_far_kernel, first, partner, size_x, size_y)
        (best,) = call(far, [shape], work)(best, table, zm, got)
    (score,) = call(score_kernel, [brick])(score, even, odd, best)
    if not partner:
        best = x_minima(best, size_x)

    (code,) = call(encode_kernel, [brick], kind=jnp.int16)(best)
    blocks = {1: swap(code, "gy", 1), 2: swap(code, "gy", 2), 3: corner_swap(code)}
    (near,) = call(y_own_kernel, [brick])(best, kept[0])
    block = [pltpu.VMEM(brick, jnp.float32)]
    *hops, final = blocks
    for hop in hops:
        far = functools.partial(y_far_kernel, hop)
        (near,) = call(far, [brick], block)(near, blocks[hop], kept[hop])
    last = [*block, *block, pltpu.SemaphoreType.DMA((3,))]
    depth, score = call(
        functools.partial(y_last_kernel, final), [brick, brick], last, out_spec=HBM
    )(near, blocks[final], kept[final], score)
    return score, depth


def solution(mesh):
    in_specs = (P(None, "gx", "gy", "gz"), P(), P("gx", "gy", "gz"))
    out_specs = (P("gx", "gy", "gz"), P("gx", "gy", "gz"))
    return jax.shard_map(shards, mesh=mesh, in_specs=in_specs, out_specs=out_specs, check_vma=False)
```

```python
import functools

import jax
import jax.numpy as jnp
from jax import lax
from jax.experimental import pallas as pl
from jax.experimental.pallas import tpu as pltpu
from jax.sharding import PartitionSpec as P

RADIUS = 128
CEILING = float(RADIUS * RADIUS)
HUGE = 1e30
LANES = 128
ROWS = 24
VMEM = pl.BlockSpec(memory_space=pltpu.VMEM)
HBM = pl.BlockSpec(memory_space=pltpu.HBM)


def call(kernel, outs, scratch=(), mib=8, in_specs=None, kind=jnp.float32, out_spec=VMEM):
    shapes = [s if isinstance(s, jax.ShapeDtypeStruct) else jax.ShapeDtypeStruct(s, kind) for s in outs]

    def run(*args):
        return pl.pallas_call(
            kernel,
            out_shape=shapes,
            in_specs=in_specs or [VMEM] * len(args),
            out_specs=[out_spec] * len(shapes),
            scratch_shapes=list(scratch),
            compiler_params=pltpu.CompilerParams(vmem_limit_bytes=mib * 1024 * 1024),
        )(*args)

    return run


def lane_of(shape):
    return lax.broadcasted_iota(jnp.int32, shape, len(shape) - 1)


def row_of(shape):
    return lax.broadcasted_iota(jnp.int32, shape, len(shape) - 2)


def cost_of(score):
    return CEILING / (1.0 + jnp.exp(-score))


def conv_kernel(
    planes, paired, f_hbm, w_hbm, mask_hbm, s_ref, m_ref, e_ref, d_ref, f_vmem, w_vmem, mask_vmem, w_big, acc, sems
):
    channels, size_x, size_y, _ = f_vmem.shape
    tiles = size_y // 16
    depth = channels * 16
    weights = pltpu.make_async_copy(w_hbm, w_vmem, sems.at[size_x])
    weights.start()
    copies = [
        pltpu.make_async_copy(f_hbm.at[:, x], f_vmem.at[:, x], sems.at[x]) for x in range(size_x)
    ]
    masks = pltpu.make_async_copy(mask_hbm, mask_vmem, sems.at[size_x + 1])
    masks.start()
    for copy in copies:
        copy.start()

    spread = (
        lax.broadcasted_iota(jnp.int32, (channels, depth), 1) // 16
        == lax.broadcasted_iota(jnp.int32, (channels, depth), 0)
    ).astype(jnp.bfloat16)
    row = lax.broadcasted_iota(jnp.int32, (ROWS, depth), 0)
    y_in = lax.broadcasted_iota(jnp.int32, (ROWS, depth), 1) % 16
    y_out = jnp.where(row <= 16, row, jnp.where(row == ROWS - 1, -1, 64))
    tap = y_in - y_out + 1
    weights.wait()
    wide = jnp.dot(w_vmem[...], spread, preferred_element_type=jnp.float32)
    blocks = []
    for a in range(3):
        for c in range(3):
            block = jnp.zeros((ROWS, depth), jnp.float32)
            for b in range(3):
                k = 9 * a + 3 * b + c
                block = jnp.where(tap == b, wide[k : k + 1, :], block)
            blocks.append(block)
    blocks.append(jnp.zeros((8, depth), jnp.float32))
    w_big[...] = jnp.concatenate(blocks, axis=0).astype(jnp.bfloat16)

    shape = (8, LANES)
    row, lane = row_of(shape), lane_of(shape)
    groups = size_y // 8
    to_first = lax.axis_index("gy") % 2 == 1 if paired else True
    folds = []

    def finish(p, at):
        fold = None
        for g in range(groups + 1):
            sums = []
            for c in range(3):

                def piece(tile, low, c=c):
                    return acc[at, c, low : low + 8, tile * LANES : tile * LANES + LANES]

                if g == groups:
                    part = jnp.where(row == 0, piece(tiles - 1, 16), piece(0, 16))
                else:
                    tile, low = g // 2, 8 * (g % 2)
                    part = piece(tile, low)
                    if low == 0 and tile > 0:
                        part = part + jnp.where(row == 0, piece(tile - 1, 16), 0.0)
                    if low == 8 and tile < tiles - 1:
                        part = part + jnp.where(row == 7, piece(tile + 1, 16), 0.0)
                sums.append(part)
            ahead = pltpu.roll(sums[0], 1, 1)
            behind = pltpu.roll(sums[2], LANES - 1, 1)
            inner = (
                sums[1] + jnp.where(lane == 0, 0.0, ahead) + jnp.where(lane == LANES - 1, 0.0, behind)
            )
            outer = jnp.where(lane == 0, ahead, jnp.where(lane == LANES - 1, behind, 0.0))
            if g == groups:
                for up, down, at_row in (
                    (inner, inner, p),
                    (outer, pltpu.roll(outer, 2 * (groups - 1), 1), 8 + p),
                ):
                    e_ref[at_row : at_row + 1, :] = jnp.where(to_first, down[7:8], up[0:1])
                    d_ref[at_row : at_row + 1, :] = jnp.where(to_first, up[0:1], down[7:8])
            else:
                span = slice(8 * g, 8 * g + 8)
                if p < size_x:
                    s_ref[p, span, :] = inner
                    inner = jnp.where(mask_vmem[p, span, :] == 1, HUGE, inner)
                m_ref[p * size_y + 8 * g : p * size_y + 8 * g + 8, :] = inner
                shift = 16 * p + 2 * g
                outer = pltpu.roll(outer, shift, 1) if shift else outer
                fold = outer if g == 0 else fold + outer
        folds.append(fold)

    at_plane = planes()
    half = size_x // 2
    for x in range(size_x):
        if x % half == 0:
            for copy in copies[x : x + half]:
                copy.wait()
            if x:
                masks.wait()
                for p in range(x - 1):
                    finish(p, at_plane[p])
        right = jnp.concatenate(
            [f_vmem[:, x, 16 * t : 16 * t + 16, :].reshape(depth, LANES) for t in range(tiles)],
            axis=1,
        )
        got = jnp.dot(w_big[...], right, preferred_element_type=jnp.float32)
        for a in range(3):
            at = x + 2 - a
            for c in range(3):
                first = (3 * a + c) * ROWS
                part = got[first : first + ROWS, :]
                acc[at, c] = part if a == 0 or x == 0 else acc[at, c] + part
    for p in range(half - 1, len(at_plane)):
        finish(p, at_plane[p])
    m_ref[len(folds) * size_y :, :] = functools.reduce(jnp.add, folds)


CODES = 4681.0
LN2 = 0.6931471805599453
TOP = 2.0**30


def encode(value):
    code = jnp.round(jnp.log(value + 1.0) * (CODES / LN2)) - 32768.0
    return jnp.clip(code, -32768.0, 32767.0).astype(jnp.int32)


def decode(code):
    level = code.astype(jnp.int32).astype(jnp.float32) + 32768.0
    return jnp.exp(level * (LN2 / CODES)) - 1.0


def pack_z(rows, ends):
    half = LANES // 2
    code = encode(rows)
    masked = ends >= 0.5 * HUGE
    most = jnp.max(jnp.where(masked, 0.0, jnp.abs(ends)), axis=1, keepdims=True)
    most = jnp.max(most, axis=0, keepdims=True)
    power = jnp.ceil(jnp.log(jnp.maximum(most, 1e-18)) * (1.0 / LN2)) + 1.0
    scores = jnp.round(jnp.where(masked, TOP, ends * (jnp.exp(power * -LN2) * TOP))).astype(jnp.int32)
    first = jnp.where(row_of((half, rows.shape[1])) == 0, power.astype(jnp.int32), code[:half])
    return jnp.concatenate([(first << 16) | (code[half:] & 0xFFFF), scores], axis=0)


def unpack_rows(words):
    return decode(words >> 16), decode((words << 16) >> 16)


def unpack_ends(ref):
    half = LANES // 2
    power = (ref[0:8, :] >> 16)[0:1].astype(jnp.float32)
    scores = ref[half : half + 8, :].astype(jnp.float32)
    return jnp.where(scores >= 0.75 * TOP, HUGE, scores * (jnp.exp(power * LN2) * (1.0 / TOP)))


def y_masks(axis, chip):
    row = row_of((8, LANES))
    index, last = lax.axis_index(axis), lax.axis_size(axis) - 1
    odd = index % 2
    if chip:
        low, high = odd == 1, odd == 0
    else:
        low, high = (odd == 0) & (index > 0), (odd == 1) & (index < last)
    return row == jnp.where(low, 0, -1), row == jnp.where(high, 7, -1)


def edge_rows(masks, part, size_y):
    low, high = masks
    return jnp.concatenate(
        [
            jnp.where(low, part, 0.0),
            jnp.zeros((size_y - 16, LANES), jnp.float32),
            jnp.where(high, part, 0.0),
        ],
        axis=0,
    )


def turn_kernel(s_ref, own_ref, far_ref, cross_ref, xcross_ref, chip_ref, xchip_ref, score_ref, zm_ref, words_ref):
    size_x, size_y, _ = s_ref.shape
    chip, cross = y_masks("gy", True), y_masks("gy", False)
    first = lax.axis_index("gx") == 0
    lane = lane_of((size_y, LANES))
    border = (lane == 0) | (lane == LANES - 1)
    faces_own = {size_x - 1: jnp.where(first, 1.0, 0.0), 0: jnp.where(first, 0.0, 1.0)}
    faces_far = {0: faces_own[size_x - 1], size_x - 1: faces_own[0]}

    def plane(ref, p):
        return ref[p * size_y : (p + 1) * size_y, :]

    def fold(ref, p):
        rest = ref[(size_x + 1) * size_y :, :]
        return pltpu.roll(rest, LANES - 16 * p, 1) if p else rest

    def complete(p, base, folded, face_ref, sides, faces):
        if p in faces:
            base = base + faces[p] * plane(face_ref, size_x)
            folded = folded + faces[p] * fold(face_ref, size_x)
        for masks, same, other in sides:
            part, part_h = same[p : p + 1], same[8 + p : 9 + p]
            if p in faces:
                part = part + faces[p] * other[size_x : size_x + 1]
                part_h = part_h + faces[p] * other[8 + size_x : 9 + size_x]
            base = base + edge_rows(masks, part, size_y)
            folded = folded + jnp.where(masks[0] | masks[1], part_h, 0.0)
        return base, folded

    costs, turned = [], []
    for far in range(2):
        for p in range(size_x):
            if far:
                sides = ((chip, xchip_ref, chip_ref), (cross, xcross_ref, cross_ref))
                masked, h = complete(p, plane(far_ref, p), fold(far_ref, p), own_ref, sides, faces_far)
            else:
                sides = ((chip, chip_ref, xchip_ref), (cross, cross_ref, xcross_ref))
                full, h = complete(p, s_ref[p], fold(own_ref, p), far_ref, sides, faces_own)
                score_ref[p] = full
                masked = jnp.where(plane(own_ref, p) == HUGE, HUGE, full)
            costs.append(cost_of(masked))
            wide = jnp.concatenate(
                [pltpu.roll(h, (2 - 2 * g) % LANES, 1) for g in range(size_y // 8)], axis=0
            )
            turned.append(jnp.where(border, masked, wide))
    away = jnp.where(first, float(size_x), -float(size_x))
    lines = []
    for i in range(size_x):
        best = costs[i]
        for j in range(size_x):
            if j != i:
                best = jnp.minimum(best, costs[j] + float((i - j) ** 2))
            d = float(j - i) + away
            best = jnp.minimum(best, costs[size_x + j] + d * d)
        lines.append(best)
    width = size_x * size_y
    rows = jnp.concatenate(lines, axis=0).T
    ends = jnp.concatenate(turned, axis=0).T
    ends = jnp.concatenate(
        [ends[r : r + 1, k * width : (k + 1) * width] for r in (0, LANES - 1, 1, 2) for k in range(2)],
        axis=0,
    )
    zm_ref[0:LANES, :] = rows
    zm_ref[LANES : LANES + 8, :] = ends
    words_ref[...] = pack_z(rows, ends)


Z_FLOOR = -(LANES + 6)


def sweep(accs, blocks, read, table, shift, low, high):
    parts = len(accs[0])

    def body(j, flat):
        flat = list(flat)
        tiles = read(j)
        squares = table.at[pl.ds(shift + 8 * blocks[0] - 8 * j, 8 * len(blocks))]
        for r in range(8):
            rows = [jnp.broadcast_to(t[r : r + 1, :], (8, LANES)) for t in tiles]
            for i in range(len(blocks)):
                square = squares[8 * i + 7 - r]
                for k in range(parts):
                    at = i * parts + k
                    flat[at] = jnp.minimum(flat[at], rows[k] + square)
        return tuple(flat)

    flat = lax.fori_loop(low, high, body, tuple(v for row in accs for v in row))
    return [list(flat[i * parts : (i + 1) * parts]) for i in range(len(blocks))]


def tiles_of(ref, j):
    rows = pl.ds(pl.multiple_of(8 * j, 8), 8)
    return [ref[rows, k * LANES : (k + 1) * LANES] for k in range(ref.shape[1] // LANES)]


def load_blocks(ref, blocks):
    return [tiles_of(ref, b) for b in blocks]


def save_blocks(ref, blocks, accs):
    for b, row in zip(blocks, accs):
        for k, v in enumerate(row):
            ref[8 * b : 8 * b + 8, k * LANES : (k + 1) * LANES] = v


def y_table(axis, hop, size_y, table):
    index = lax.axis_index(axis)
    away = (((index ^ hop) - index) * size_y).astype(jnp.float32)
    s = row_of((8, LANES)).astype(jnp.float32) - away
    for d in range(1 - size_y, size_y - 7):
        v = s + float(d)
        table[d - (1 - size_y)] = v * v


def z_own_kernel(size_y, zm_ref, out_ref, table, *y_tables):
    count, half = LANES // 8, LANES // 16
    for hop, y_one in enumerate(y_tables):
        y_table("gy", hop, size_y, y_one)
    s = row_of((8, LANES)).astype(jnp.float32)
    for d in range(Z_FLOOR, LANES):
        v = s + float(d)
        table[d - Z_FLOOR] = v * v

    def read(j):
        at = row_of((8, LANES)) + 8 * j
        hide = (at == 0) | (at == LANES - 1)
        return [jnp.where(hide, HUGE, t) for t in tiles_of(zm_ref, j)]

    for first in (0, half):
        blocks = range(first, first + half)
        accs = [[jnp.full((8, LANES), HUGE, jnp.float32)] * (out_ref.shape[1] // LANES) for _ in blocks]
        save_blocks(out_ref, blocks, sweep(accs, blocks, read, table, -7 - Z_FLOOR, 0, count))


def border_minima(cost, size_x, size_y, partner):
    if not partner:
        return cost
    width = cost.shape[1]
    shape = (8, width)
    row, plane = row_of(shape), lane_of(shape) // size_y
    away = jnp.where(lax.axis_index("gx") == 0, size_x, -size_x)
    shift = jnp.where(row % 2 == 1, away, 0)
    best = None
    for r in range(size_x):
        source = jnp.where(plane >= r, plane - r, plane - r + size_x)
        d = (source + shift - plane).astype(jnp.float32)
        if r == 0:
            moved = cost
        else:
            cut = width - r * size_y
            moved = jnp.concatenate([cost[:, cut:], cost[:, :cut]], axis=1)
        moved = moved + d * d
        best = moved if best is None else jnp.minimum(best, moved)
    return jnp.minimum(best, pltpu.roll(best, 7, 0))


def z_far_kernel(even, partner, size_x, size_y, acc_ref, table, zm_ref, got_ref, out_ref, *refs):
    *code_ref, source, work = refs
    index, last = lax.axis_index("gz"), lax.axis_size("gz") - 1
    odd = index % 2 == 1
    low = odd if even else jnp.logical_not(odd)
    valid = jnp.where(low, index > 0, index < last)
    count, half = LANES // 8, LANES // 16
    out = out_ref if even else work

    own, got = zm_ref[LANES : LANES + 8, :], unpack_ends(got_ref)
    mine = jnp.where(low, own[0:2], own[2:4]) + jnp.where(valid, jnp.where(low, got[6:8], got[4:6]), 0.0)
    theirs = jnp.where(low, got[2:4] + own[4:6], got[0:2] + own[6:8])
    ends = border_minima(cost_of(jnp.concatenate([mine, theirs, mine, theirs], axis=0)), size_x, size_y, partner)
    source[0 : LANES // 2, :], source[LANES // 2 :, :] = unpack_rows(got_ref[0 : LANES // 2, :])

    squares = table.at[pl.ds(jnp.where(low, -Z_FLOOR, 1 - LANES - Z_FLOOR), LANES)]
    lanes = [slice(k * LANES, (k + 1) * LANES) for k in range(zm_ref.shape[1] // LANES)]
    rows = [jnp.broadcast_to(ends[0:1, cols], (8, LANES)) for cols in lanes]
    for b in range(count):
        for row, cols in zip(rows, lanes):
            span = slice(8 * b, 8 * b + 8)
            out[span, cols] = jnp.minimum(acc_ref[span, cols], row + squares[8 * b])

    def slanted(accs, blocks, offset, tiles, reach):
        for j in tiles:
            tile = tiles_of(source, j)
            for r in range(8):
                q = 8 * j + r
                rows = [jnp.broadcast_to(t[r : r + 1, :], (8, LANES)) for t in tile]
                for i, b in enumerate(blocks):
                    if reach(b, q):
                        square = table[8 * b - q + offset - Z_FLOOR]
                        accs[i] = [jnp.minimum(v, row + square) for v, row in zip(accs[i], rows)]
        return accs

    @pl.when(valid & low)
    def _():
        source[LANES - 1 : LANES, :] = ends[2:3]
        for first in (0, half):
            blocks = range(first, first + half)
            accs = load_blocks(out, blocks)
            accs = slanted(accs, blocks, LANES, blocks, lambda b, q: 8 * b < q)
            if blocks[-1] + 1 < count:
                read = functools.partial(tiles_of, source)
                accs = sweep(accs, blocks, read, table, LANES - 7 - Z_FLOOR, blocks[-1] + 1, count)
            save_blocks(out, blocks, accs)

    @pl.when(valid & jnp.logical_not(low))
    def _():
        source[0:1, :] = ends[2:3]
        for first in (0, half):
            blocks = range(first, first + half)
            accs = load_blocks(out, blocks)
            accs = slanted(accs, blocks, -LANES, blocks, lambda b, q: q < 8 * b + 7)
            if first:
                read = functools.partial(tiles_of, source)
                accs = sweep(accs, blocks, read, table, -LANES - 7 - Z_FLOOR, 0, first)
            save_blocks(out, blocks, accs)

    if not even:
        per = LANES // size_y
        for k, cols in enumerate(lanes):
            best = work[:, cols].T
            code = encode(best).astype(jnp.int16)
            for i in range(per):
                out_ref[k * per + i] = best[i * size_y : (i + 1) * size_y]
                code_ref[0][k * per + i] = code[i * size_y : (i + 1) * size_y]


def score_kernel(score_in, even_ref, odd_ref, _, score_ref):
    index, last = lax.axis_index("gz"), lax.axis_size("gz") - 1
    odd = index % 2 == 1
    size_y = score_in.shape[1]
    per = LANES // size_y
    even_ends, odd_ends = unpack_ends(even_ref), unpack_ends(odd_ref)
    for k in range(even_ref.shape[1] // LANES):
        cols = slice(k * LANES, (k + 1) * LANES)
        even_rows, odd_rows = even_ends[:, cols], odd_ends[:, cols]
        low = jnp.where(index > 0, jnp.where(odd, even_rows, odd_rows)[6:7], 0.0)
        high = jnp.where(index < last, jnp.where(odd, odd_rows, even_rows)[4:5], 0.0)
        middle = jnp.zeros((LANES - 2, LANES), jnp.float32)
        more = jnp.concatenate([low, middle, high], axis=0).T
        for i in range(per):
            x = k * per + i
            score_ref[x] = score_in[x] + more[i * size_y : (i + 1) * size_y]


Y_BLOCKS = 4


def y_sweep(refs, tables, start, out_ref, scale, span=None):
    size_x, size_y, _ = out_ref.shape
    span = span or range(size_y // 8)
    for first in range(span[0], span[-1] + 1, Y_BLOCKS):
        blocks = range(first, first + Y_BLOCKS)
        accs = []
        for b in blocks:
            span = slice(8 * b, 8 * b + 8)
            blank = jnp.full((8, LANES), HUGE, jnp.float32)
            accs.append([blank if start is None else start[x, span, :] for x in range(size_x)])
        for ref, table in zip(refs, tables):

            def read(j, ref=ref):
                return [ref[x, pl.ds(pl.multiple_of(8 * j, 8), 8), :] for x in range(size_x)]

            accs = sweep(accs, blocks, read, table, size_y - 8, 0, size_y // 8)
        for b, row in zip(blocks, accs):
            for x, v in enumerate(row):
                out_ref[x, 8 * b : 8 * b + 8, :] = v if scale == 1.0 else v * scale


def y_near_kernel(own_ref, code_ref, table_0, table_1, out_ref, block):
    block[...] = decode(code_ref[...])
    y_sweep((own_ref, block), (table_0, table_1), None, out_ref, 1.0)


def y_across_kernel(start_ref, code_ref, table, out_ref, block):
    block[...] = decode(code_ref[...])
    y_sweep((block,), (table,), start_ref, out_ref, 1.0)


def y_last_kernel(start_ref, code_ref, table, score_ref, depth_hbm, score_hbm, block, depth, sems):
    index = lax.axis_index("gy")
    near = jnp.abs((index ^ 3) - index) < 3
    size_y = depth.shape[1]
    scores = pltpu.make_async_copy(score_ref, score_hbm, sems.at[0])
    scores.start()
    parts = [
        pltpu.make_async_copy(depth.at[:, rows], depth_hbm.at[:, rows], sems.at[1 + i])
        for i, rows in enumerate(pl.ds(f, size_y // 2) for f in (0, size_y // 2))
    ]

    @pl.when(near)
    def _():
        block[...] = decode(code_ref[...])
        half = size_y // 16
        for i, part in enumerate(parts):
            y_sweep((block,), (table,), start_ref, depth, 1.0 / RADIUS, range(i * half, (i + 1) * half))
            part.start()

    @pl.when(jnp.logical_not(near))
    def _():
        depth[...] = start_ref[...] * (1.0 / RADIUS)
        for part in parts:
            part.start()

    for copy in (scores, *parts):
        copy.wait()


def swap(value, axis, hop):
    n = lax.axis_size(axis)
    return lax.ppermute(value, axis, [(i, i ^ hop) for i in range(n)])


def swap_xy(value, hop_x, hop_y):
    nx, ny = lax.axis_size("gx"), lax.axis_size("gy")
    pairs = [(x * ny + y, (x ^ hop_x) * ny + (y ^ hop_y)) for x in range(nx) for y in range(ny)]
    return lax.ppermute(value, ("gx", "gy"), pairs)


def neighbours(low, high, axis, beyond=0.0):
    n, index = lax.axis_size(axis), lax.axis_index(axis)
    odd = index % 2 == 1
    pairs = [(i, i + 1 if i % 2 else i - 1) for i in range(1, n - 1)]
    got_odd = lax.ppermute(jnp.where(odd, high, low), axis, pairs)
    got_even = lax.ppermute(jnp.where(odd, low, high), axis, [(i, i ^ 1) for i in range(n)])
    from_low = jnp.where(odd, got_even, got_odd)
    from_high = jnp.where(odd, got_odd, got_even)
    return jnp.where(index == 0, beyond, from_low), jnp.where(index == n - 1, beyond, from_high)


def z_swaps(value):
    nx, ny, n = (lax.axis_size(axis) for axis in ("gx", "gy", "gz"))
    even = lax.ppermute(value, "gz", [(i, i ^ 1) for i in range(n)])
    pairs = []
    for i in range(nx * ny * n):
        xy, z = i // n, i % n
        pairs.append((i, (xy ^ 1) * n + z if z in (0, n - 1) else xy * n + (z + 1 if z % 2 else z - 1)))
    return even, lax.ppermute(value, ("gx", "gy", "gz"), pairs)


def corner_swap(value):
    nx, ny = lax.axis_size("gx"), lax.axis_size("gy")
    pairs = []
    for i in range(nx * ny):
        x, y = i // ny, i % ny
        pairs.append((i, (x ^ 1) * ny + y if y in (0, ny - 1) else x * ny + (y + 1 if y % 2 else y - 1)))
    return lax.ppermute(value, ("gx", "gy"), pairs)


def conv(features, conv_weight, mask, planes, count, paired):
    channels, size_x, size_y, _ = features.shape
    return call(
        functools.partial(conv_kernel, planes, paired),
        [(size_x, size_y, LANES), (count * size_y + 8, LANES), (16, LANES), (16, LANES)],
        [
            pltpu.VMEM(features.shape, jnp.bfloat16),
            pltpu.VMEM(conv_weight.shape, jnp.bfloat16),
            pltpu.VMEM(mask.shape, jnp.int32),
            pltpu.VMEM((9 * ROWS + 8, channels * 16), jnp.bfloat16),
            pltpu.VMEM((size_x + 2, 3, ROWS, size_y // 16 * LANES), jnp.float32),
            pltpu.SemaphoreType.DMA((size_x + 2,)),
        ],
        mib=24,
        in_specs=[HBM] * 3,
    )(*(pltpu.with_memory_space_constraint(v, pltpu.HBM) for v in (features, conv_weight, mask)))


def halo_with_partner(features, conv_weight, mask):
    _, size_x, size_y, _ = features.shape

    def planes():
        return [*range(1, size_x + 1), jnp.where(lax.axis_index("gx") == 0, size_x + 1, 0)]

    s, own, chip, cross = conv(features, conv_weight, mask, planes, size_x + 1, True)
    far = swap_xy(own, 1, 0)
    sides = [swap_xy(cross, 0, 3), swap_xy(cross, 1, 3), swap_xy(chip, 0, 1), swap_xy(chip, 1, 1)]
    lines = size_x * size_y
    words = jax.ShapeDtypeStruct((LANES // 2 + 8, lines), jnp.int32)
    return call(turn_kernel, [(size_x, size_y, LANES), (LANES + 8, lines), words])(s, own, far, *sides)


def halo_in_rounds(features, conv_weight, mask):
    _, size_x, size_y, _ = features.shape
    groups = size_y // 8
    planes = [*range(1, size_x + 1), 0, size_x + 1]
    s, rest, down, up = conv(features, conv_weight, mask, lambda: planes, size_x + 2, False)

    def whole(k):
        h = jnp.roll(rest[len(planes) * size_y :], -16 * k, 1)
        part = s[k] if k < size_x else rest[k * size_y : (k + 1) * size_y]
        return jnp.concatenate([part, h, *(e[i : i + 1] for e in (down, up) for i in (k, 8 + k))], axis=0)

    low, high = neighbours(whole(size_x), whole(size_x + 1), "gx")
    own = jnp.stack([whole(k) for k in range(size_x)]).at[0].add(low).at[size_x - 1].add(high)
    e = own[:, size_y + 8 :]
    low, high = neighbours(e[:, 0:2], e[:, 2:4], "gy")
    own = own.at[:, 0].add(low[:, 0]).at[:, size_y - 1].add(high[:, 0])
    own = own.at[:, size_y].add(low[:, 1]).at[:, size_y + 7].add(high[:, 1])
    score, h = own[:, :size_y], own[:, size_y : size_y + 8]

    def line(value):
        return value.reshape(1, size_x * size_y)

    up = jnp.swapaxes(h[:, :, 0 : 2 * groups : 2], 1, 2)
    down = jnp.swapaxes(jnp.roll(h, 1, 2)[:, :, 0 : 2 * groups : 2], 1, 2)
    masked = jnp.where(mask == 1, HUGE, score)
    rows = jnp.transpose(cost_of(masked), (2, 0, 1)).reshape(LANES, size_x * size_y)
    ends = [line(v) for v in (masked[:, :, 0], masked[:, :, LANES - 1], down, up)]
    blank = [jnp.full_like(ends[0], HUGE)] * 2 + [jnp.zeros_like(ends[0])] * 2
    pairs = [v for pair in zip(ends, blank) for v in pair]
    ends = jnp.concatenate(pairs, axis=0)
    return score, jnp.concatenate([rows, ends], axis=0), pack_z(rows, ends)


def x_minima(value, size_x):
    n, index = lax.axis_size("gx"), lax.axis_index("gx")
    every = lax.all_gather(value, "gx", axis=0, tiled=True)
    at = index * size_x + jnp.arange(size_x)
    d = (at[:, None] - jnp.arange(n * size_x)[None, :]).astype(jnp.float32)
    return jnp.min(every[None] + (d * d)[:, :, None, None], axis=1)


def shards(features, conv_weight, mask):
    _, size_x, size_y, size_z = features.shape
    gx, gy = lax.axis_size("gx"), lax.axis_size("gy")
    assert size_z == LANES and size_y % 16 == 0 and LANES % size_y == 0 and gy == 4
    brick = (size_x, size_y, LANES)
    lines = size_x * size_y
    partner = gx == 2

    halo = halo_with_partner if partner else halo_in_rounds
    score, zm, words = halo(features, conv_weight, mask)

    even, odd = z_swaps(words)
    tables = (2 * size_y - 8, 8, LANES)
    own = functools.partial(z_own_kernel, size_y)
    best, table, *kept = call(own, [(LANES, lines), (LANES - Z_FLOOR, 8, LANES)] + [tables] * 4)(zm)
    work = [pltpu.VMEM((LANES, lines), jnp.float32)] * 2
    coded = jax.ShapeDtypeStruct(brick, jnp.int16)
    for first, got, shapes in ((True, even, [(LANES, lines)]), (False, odd, [brick, coded])):
        far = functools.partial(z_far_kernel, first, partner, size_x, size_y)
        best, *code = call(far, shapes, work)(best, table, zm, got)
    if not partner:
        best = x_minima(best, size_x)
        code = [encode(best).astype(jnp.int16)]

    code = code[0]
    chip, across, corner = swap(code, "gy", 1), swap(code, "gy", 2), corner_swap(code)
    block = [pltpu.VMEM(brick, jnp.float32)]
    (near,) = call(y_near_kernel, [brick], block)(best, chip, kept[0], kept[1])
    (near,) = call(y_across_kernel, [brick], block)(near, across, kept[2])
    (score,) = call(score_kernel, [brick])(score, even, odd, near)
    last = [*block, *block, pltpu.SemaphoreType.DMA((3,))]
    depth, score = call(y_last_kernel, [brick, brick], last, out_spec=HBM)(near, corner, kept[3], score)
    return score, depth


def solution(mesh):
    in_specs = (P(None, "gx", "gy", "gz"), P(), P("gx", "gy", "gz"))
    out_specs = (P("gx", "gy", "gz"), P("gx", "gy", "gz"))
    return jax.shard_map(shards, mesh=mesh, in_specs=in_specs, out_specs=out_specs, check_vma=False)
```

```python
import functools

import jax
import jax.numpy as jnp
from jax import lax
from jax.experimental import pallas as pl
from jax.experimental.pallas import tpu as pltpu
from jax.sharding import PartitionSpec as P

RADIUS = 128
CEILING = float(RADIUS * RADIUS)
HUGE = 1e30
LANES = 128
ROWS = 24
VMEM = pl.BlockSpec(memory_space=pltpu.VMEM)
HBM = pl.BlockSpec(memory_space=pltpu.HBM)


def call(kernel, outs, scratch=(), mib=8, in_specs=None, kind=jnp.float32, out_spec=VMEM):
    shapes = [s if isinstance(s, jax.ShapeDtypeStruct) else jax.ShapeDtypeStruct(s, kind) for s in outs]

    def run(*args):
        return pl.pallas_call(
            kernel,
            out_shape=shapes,
            in_specs=in_specs or [VMEM] * len(args),
            out_specs=[out_spec] * len(shapes),
            scratch_shapes=list(scratch),
            compiler_params=pltpu.CompilerParams(vmem_limit_bytes=mib * 1024 * 1024),
        )(*args)

    return run


def lane_of(shape):
    return lax.broadcasted_iota(jnp.int32, shape, len(shape) - 1)


def row_of(shape):
    return lax.broadcasted_iota(jnp.int32, shape, len(shape) - 2)


def cost_of(score):
    return CEILING / (1.0 + jnp.exp(-score))


def conv_kernel(
    planes, paired, f_hbm, w_hbm, mask_hbm, s_ref, m_ref, e_ref, d_ref, f_vmem, w_vmem, mask_vmem, w_big, acc, sems
):
    channels, size_x, size_y, _ = f_vmem.shape
    tiles = size_y // 16
    depth = channels * 16
    weights = pltpu.make_async_copy(w_hbm, w_vmem, sems.at[size_x])
    weights.start()
    copies = [
        pltpu.make_async_copy(f_hbm.at[:, x], f_vmem.at[:, x], sems.at[x]) for x in range(size_x)
    ]
    masks = pltpu.make_async_copy(mask_hbm, mask_vmem, sems.at[size_x + 1])
    masks.start()
    for copy in copies:
        copy.start()

    spread = (
        lax.broadcasted_iota(jnp.int32, (channels, depth), 1) // 16
        == lax.broadcasted_iota(jnp.int32, (channels, depth), 0)
    ).astype(jnp.bfloat16)
    row = lax.broadcasted_iota(jnp.int32, (ROWS, depth), 0)
    y_in = lax.broadcasted_iota(jnp.int32, (ROWS, depth), 1) % 16
    y_out = jnp.where(row <= 16, row, jnp.where(row == ROWS - 1, -1, 64))
    tap = y_in - y_out + 1
    weights.wait()
    wide = jnp.dot(w_vmem[...], spread, preferred_element_type=jnp.float32)
    blocks = []
    for a in range(3):
        for c in range(3):
            block = jnp.zeros((ROWS, depth), jnp.float32)
            for b in range(3):
                k = 9 * a + 3 * b + c
                block = jnp.where(tap == b, wide[k : k + 1, :], block)
            blocks.append(block)
    blocks.append(jnp.zeros((8, depth), jnp.float32))
    w_big[...] = jnp.concatenate(blocks, axis=0).astype(jnp.bfloat16)

    shape = (8, LANES)
    row, lane = row_of(shape), lane_of(shape)
    groups = size_y // 8
    to_first = lax.axis_index("gy") % 2 == 1 if paired else True
    folds = []

    def finish(p, at):
        fold = None
        for g in range(groups + 1):
            sums = []
            for c in range(3):

                def piece(tile, low, c=c):
                    return acc[at, c, low : low + 8, tile * LANES : tile * LANES + LANES]

                if g == groups:
                    part = jnp.where(row == 0, piece(tiles - 1, 16), piece(0, 16))
                else:
                    tile, low = g // 2, 8 * (g % 2)
                    part = piece(tile, low)
                    if low == 0 and tile > 0:
                        part = part + jnp.where(row == 0, piece(tile - 1, 16), 0.0)
                    if low == 8 and tile < tiles - 1:
                        part = part + jnp.where(row == 7, piece(tile + 1, 16), 0.0)
                sums.append(part)
            ahead = pltpu.roll(sums[0], 1, 1)
            behind = pltpu.roll(sums[2], LANES - 1, 1)
            inner = (
                sums[1] + jnp.where(lane == 0, 0.0, ahead) + jnp.where(lane == LANES - 1, 0.0, behind)
            )
            outer = jnp.where(lane == 0, ahead, jnp.where(lane == LANES - 1, behind, 0.0))
            if g == groups:
                for up, down, at_row in (
                    (inner, inner, p),
                    (outer, pltpu.roll(outer, 2 * (groups - 1), 1), 8 + p),
                ):
                    e_ref[at_row : at_row + 1, :] = jnp.where(to_first, down[7:8], up[0:1])
                    d_ref[at_row : at_row + 1, :] = jnp.where(to_first, up[0:1], down[7:8])
            else:
                span = slice(8 * g, 8 * g + 8)
                if p < size_x:
                    s_ref[p, span, :] = inner
                    inner = jnp.where(mask_vmem[p, span, :] == 1, HUGE, inner)
                m_ref[p * size_y + 8 * g : p * size_y + 8 * g + 8, :] = inner
                shift = 16 * p + 2 * g
                outer = pltpu.roll(outer, shift, 1) if shift else outer
                fold = outer if g == 0 else fold + outer
        folds.append(fold)

    at_plane = planes()
    half = size_x // 2
    for x in range(size_x):
        if x % half == 0:
            for copy in copies[x : x + half]:
                copy.wait()
            if x:
                masks.wait()
                finish(x - half, at_plane[x - half])
        right = jnp.concatenate(
            [f_vmem[:, x, 16 * t : 16 * t + 16, :].reshape(depth, LANES) for t in range(tiles)],
            axis=1,
        )
        if x == size_x - 1:
            finish(x - 2, at_plane[x - 2])
        got = jnp.dot(w_big[...], right, preferred_element_type=jnp.float32)
        for a in range(3):
            at = x + 2 - a
            for c in range(3):
                first = (3 * a + c) * ROWS
                part = got[first : first + ROWS, :]
                acc[at, c] = part if a == 0 or x == 0 else acc[at, c] + part
    for p in range(size_x - 2, len(at_plane)):
        finish(p, at_plane[p])
    m_ref[len(folds) * size_y :, :] = functools.reduce(jnp.add, folds)


CODES = 4681.0
LN2 = 0.6931471805599453
TOP = 2.0**30


def encode(value):
    code = jnp.round(jnp.log(value + 1.0) * (CODES / LN2)) - 32768.0
    return jnp.clip(code, -32768.0, 32767.0).astype(jnp.int32)


def decode(code):
    level = code.astype(jnp.int32).astype(jnp.float32) + 32768.0
    return jnp.exp(level * (LN2 / CODES)) - 1.0


def pack_z(rows, ends):
    half = LANES // 2
    code = encode(rows)
    masked = ends >= 0.5 * HUGE
    most = jnp.max(jnp.where(masked, 0.0, jnp.abs(ends)), axis=1, keepdims=True)
    most = jnp.max(most, axis=0, keepdims=True)
    power = jnp.ceil(jnp.log(jnp.maximum(most, 1e-18)) * (1.0 / LN2)) + 1.0
    scores = jnp.round(jnp.where(masked, TOP, ends * (jnp.exp(power * -LN2) * TOP))).astype(jnp.int32)
    first = jnp.where(row_of((half, rows.shape[1])) == 0, power.astype(jnp.int32), code[:half])
    return jnp.concatenate([(first << 16) | (code[half:] & 0xFFFF), scores], axis=0)


def unpack_rows(words):
    return decode(words >> 16), decode((words << 16) >> 16)


def unpack_ends(ref):
    half = LANES // 2
    power = (ref[0:8, :] >> 16)[0:1].astype(jnp.float32)
    scores = ref[half : half + 8, :].astype(jnp.float32)
    return jnp.where(scores >= 0.75 * TOP, HUGE, scores * (jnp.exp(power * LN2) * (1.0 / TOP)))


def y_masks(axis, chip):
    row = row_of((8, LANES))
    index, last = lax.axis_index(axis), lax.axis_size(axis) - 1
    odd = index % 2
    if chip:
        low, high = odd == 1, odd == 0
    else:
        low, high = (odd == 0) & (index > 0), (odd == 1) & (index < last)
    return row == jnp.where(low, 0, -1), row == jnp.where(high, 7, -1)


def edge_rows(masks, part, size_y):
    low, high = masks
    return jnp.concatenate(
        [
            jnp.where(low, part, 0.0),
            jnp.zeros((size_y - 16, LANES), jnp.float32),
            jnp.where(high, part, 0.0),
        ],
        axis=0,
    )


def turn_kernel(s_ref, own_ref, far_ref, cross_ref, xcross_ref, chip_ref, xchip_ref, score_ref, zm_ref, words_ref):
    size_x, size_y, _ = s_ref.shape
    chip, cross = y_masks("gy", True), y_masks("gy", False)
    first = lax.axis_index("gx") == 0
    lane = lane_of((size_y, LANES))
    border = (lane == 0) | (lane == LANES - 1)
    faces_own = {size_x - 1: jnp.where(first, 1.0, 0.0), 0: jnp.where(first, 0.0, 1.0)}
    faces_far = {0: faces_own[size_x - 1], size_x - 1: faces_own[0]}

    def plane(ref, p):
        return ref[p * size_y : (p + 1) * size_y, :]

    def fold(ref, p):
        rest = ref[(size_x + 1) * size_y :, :]
        return pltpu.roll(rest, LANES - 16 * p, 1) if p else rest

    def complete(p, base, folded, face_ref, sides, faces):
        if p in faces:
            base = base + faces[p] * plane(face_ref, size_x)
            folded = folded + faces[p] * fold(face_ref, size_x)
        for masks, same, other in sides:
            part, part_h = same[p : p + 1], same[8 + p : 9 + p]
            if p in faces:
                part = part + faces[p] * other[size_x : size_x + 1]
                part_h = part_h + faces[p] * other[8 + size_x : 9 + size_x]
            base = base + edge_rows(masks, part, size_y)
            folded = folded + jnp.where(masks[0] | masks[1], part_h, 0.0)
        return base, folded

    costs, turned = [], []
    for far in range(2):
        for p in range(size_x):
            if far:
                sides = ((chip, xchip_ref, chip_ref), (cross, xcross_ref, cross_ref))
                masked, h = complete(p, plane(far_ref, p), fold(far_ref, p), own_ref, sides, faces_far)
            else:
                sides = ((chip, chip_ref, xchip_ref), (cross, cross_ref, xcross_ref))
                full, h = complete(p, s_ref[p], fold(own_ref, p), far_ref, sides, faces_own)
                score_ref[p] = full
                masked = jnp.where(plane(own_ref, p) == HUGE, HUGE, full)
            costs.append(cost_of(masked))
            wide = jnp.concatenate(
                [pltpu.roll(h, (2 - 2 * g) % LANES, 1) for g in range(size_y // 8)], axis=0
            )
            turned.append(jnp.where(border, masked, wide))
    away = jnp.where(first, float(size_x), -float(size_x))
    lines = []
    for i in range(size_x):
        best = costs[i]
        for j in range(size_x):
            if j != i:
                best = jnp.minimum(best, costs[j] + float((i - j) ** 2))
            d = float(j - i) + away
            best = jnp.minimum(best, costs[size_x + j] + d * d)
        lines.append(best)
    width = size_x * size_y
    rows = jnp.concatenate(lines, axis=0).T
    ends = jnp.concatenate(turned, axis=0).T
    ends = jnp.concatenate(
        [ends[r : r + 1, k * width : (k + 1) * width] for r in (0, LANES - 1, 1, 2) for k in range(2)],
        axis=0,
    )
    zm_ref[0:LANES, :] = rows
    zm_ref[LANES : LANES + 8, :] = ends
    words_ref[...] = pack_z(rows, ends)


Z_FLOOR = -(LANES + 6)


def sweep(accs, blocks, read, table, shift, low, high):
    parts = len(accs[0])

    def body(j, flat):
        flat = list(flat)
        tiles = read(j)
        squares = table.at[pl.ds(shift + 8 * blocks[0] - 8 * j, 8 * len(blocks))]
        for r in range(8):
            rows = [jnp.broadcast_to(t[r : r + 1, :], (8, LANES)) for t in tiles]
            for i in range(len(blocks)):
                square = squares[8 * i + 7 - r]
                for k in range(parts):
                    at = i * parts + k
                    flat[at] = jnp.minimum(flat[at], rows[k] + square)
        return tuple(flat)

    flat = lax.fori_loop(low, high, body, tuple(v for row in accs for v in row))
    return [list(flat[i * parts : (i + 1) * parts]) for i in range(len(blocks))]


def tiles_of(ref, j):
    rows = pl.ds(pl.multiple_of(8 * j, 8), 8)
    return [ref[rows, k * LANES : (k + 1) * LANES] for k in range(ref.shape[1] // LANES)]


def load_blocks(ref, blocks):
    return [tiles_of(ref, b) for b in blocks]


def save_blocks(ref, blocks, accs):
    for b, row in zip(blocks, accs):
        for k, v in enumerate(row):
            ref[8 * b : 8 * b + 8, k * LANES : (k + 1) * LANES] = v


def y_table(axis, hop, size_y, table):
    index = lax.axis_index(axis)
    away = (((index ^ hop) - index) * size_y).astype(jnp.float32)
    s = row_of((8, LANES)).astype(jnp.float32) - away
    for d in range(1 - size_y, size_y - 7):
        v = s + float(d)
        table[d - (1 - size_y)] = v * v


def z_own_kernel(size_y, zm_ref, out_ref, table, *y_tables):
    count, half = LANES // 8, LANES // 16
    for hop, y_one in enumerate(y_tables):
        y_table("gy", hop, size_y, y_one)
    s = row_of((8, LANES)).astype(jnp.float32)
    for d in range(Z_FLOOR, LANES):
        v = s + float(d)
        table[d - Z_FLOOR] = v * v

    def read(j):
        at = row_of((8, LANES)) + 8 * j
        hide = (at == 0) | (at == LANES - 1)
        return [jnp.where(hide, HUGE, t) for t in tiles_of(zm_ref, j)]

    for first in (0, half):
        blocks = range(first, first + half)
        accs = [[jnp.full((8, LANES), HUGE, jnp.float32)] * (out_ref.shape[1] // LANES) for _ in blocks]
        save_blocks(out_ref, blocks, sweep(accs, blocks, read, table, -7 - Z_FLOOR, 0, count))


def border_minima(cost, size_x, size_y, partner):
    if not partner:
        return cost
    width = cost.shape[1]
    shape = (8, width)
    row, plane = row_of(shape), lane_of(shape) // size_y
    away = jnp.where(lax.axis_index("gx") == 0, size_x, -size_x)
    shift = jnp.where(row % 2 == 1, away, 0)
    best = None
    for r in range(size_x):
        source = jnp.where(plane >= r, plane - r, plane - r + size_x)
        d = (source + shift - plane).astype(jnp.float32)
        if r == 0:
            moved = cost
        else:
            cut = width - r * size_y
            moved = jnp.concatenate([cost[:, cut:], cost[:, :cut]], axis=1)
        moved = moved + d * d
        best = moved if best is None else jnp.minimum(best, moved)
    return jnp.minimum(best, pltpu.roll(best, 7, 0))


def z_far_kernel(even, partner, size_x, size_y, acc_ref, table, zm_ref, got_ref, out_ref, *refs):
    *code_ref, source, work = refs
    index, last = lax.axis_index("gz"), lax.axis_size("gz") - 1
    odd = index % 2 == 1
    low = odd if even else jnp.logical_not(odd)
    valid = jnp.where(low, index > 0, index < last)
    count, half = LANES // 8, LANES // 16
    out = out_ref if even else work
    own, got = zm_ref[LANES : LANES + 8, :], unpack_ends(got_ref)
    lanes = [slice(k * LANES, (k + 1) * LANES) for k in range(zm_ref.shape[1] // LANES)]
    source[0 : LANES // 2, :], source[LANES // 2 :, :] = unpack_rows(got_ref[0 : LANES // 2, :])

    def minima(mine, theirs):
        ends = cost_of(jnp.concatenate([mine, theirs, mine, theirs], axis=0))
        return border_minima(ends, size_x, size_y, partner)

    def add_ends(ends, start, places):
        for b in range(count):
            span = slice(8 * b, 8 * b + 8)
            for cols in lanes:
                best = start[span, cols]
                for i, place in enumerate(places):
                    row = jnp.broadcast_to(ends[2 * i : 2 * i + 1, cols], (8, LANES))
                    best = jnp.minimum(best, row + table[8 * b - place - Z_FLOOR])
                out[span, cols] = best

    def slanted(accs, blocks, offset, skip, reach):
        for j in blocks:
            tile = tiles_of(source, j)
            for r in range(8):
                q = 8 * j + r
                rows = [jnp.broadcast_to(t[r : r + 1, :], (8, LANES)) for t in tile]
                for i, b in enumerate(blocks):
                    if reach(b, q) and q != skip:
                        square = table[8 * b - q + offset - Z_FLOOR]
                        accs[i] = [jnp.minimum(v, row + square) for v, row in zip(accs[i], rows)]
        return accs

    def far(offset, skip, reach, more):
        source[skip : skip + 1, :] = jnp.full((1, zm_ref.shape[1]), HUGE, jnp.float32)
        for first in (0, half):
            blocks = range(first, first + half)
            accs = slanted(load_blocks(acc_ref, blocks), blocks, offset, skip, reach)
            if more(first):
                read = functools.partial(tiles_of, source)
                accs = sweep(accs, blocks, read, table, offset - 7 - Z_FLOOR, *more(first))
            save_blocks(out, blocks, accs)

    @pl.when(valid & low)
    def _():
        ends = minima(own[0:2] + got[6:8], got[2:4] + own[4:6])
        far(LANES, LANES - 1, lambda b, q: 8 * b < q, lambda first: None if first else (half, count))
        add_ends(ends, out, (0, -1))

    @pl.when(valid & jnp.logical_not(low))
    def _():
        ends = minima(own[2:4] + got[4:6], got[0:2] + own[6:8])
        far(-LANES, 0, lambda b, q: q < 8 * b + 7, lambda first: (0, first) if first else None)
        add_ends(ends, out, (LANES - 1, LANES))

    @pl.when(jnp.logical_not(valid) & low)
    def _():
        add_ends(minima(own[0:2], own[0:2]), acc_ref, (0,))

    @pl.when(jnp.logical_not(valid) & jnp.logical_not(low))
    def _():
        add_ends(minima(own[2:4], own[2:4]), acc_ref, (LANES - 1,))

    if not even:
        per = LANES // size_y
        for k, cols in enumerate(lanes):
            best = work[:, cols].T
            code = encode(best).astype(jnp.int16)
            for i in range(per):
                out_ref[k * per + i] = best[i * size_y : (i + 1) * size_y]
                code_ref[0][k * per + i] = code[i * size_y : (i + 1) * size_y]


def score_kernel(score_in, even_ref, odd_ref, _, score_ref):
    index, last = lax.axis_index("gz"), lax.axis_size("gz") - 1
    odd = index % 2 == 1
    size_y = score_in.shape[1]
    per = LANES // size_y
    even_ends, odd_ends = unpack_ends(even_ref), unpack_ends(odd_ref)
    for k in range(even_ref.shape[1] // LANES):
        cols = slice(k * LANES, (k + 1) * LANES)
        even_rows, odd_rows = even_ends[:, cols], odd_ends[:, cols]
        low = jnp.where(index > 0, jnp.where(odd, even_rows, odd_rows)[6:7], 0.0)
        high = jnp.where(index < last, jnp.where(odd, odd_rows, even_rows)[4:5], 0.0)
        middle = jnp.zeros((LANES - 2, LANES), jnp.float32)
        more = jnp.concatenate([low, middle, high], axis=0).T
        for i in range(per):
            x = k * per + i
            score_ref[x] = score_in[x] + more[i * size_y : (i + 1) * size_y]


Y_BLOCKS = 4


def y_sweep(refs, tables, start, out_ref, scale, span=None):
    size_x, size_y, _ = out_ref.shape
    span = span or range(size_y // 8)
    for first in range(span[0], span[-1] + 1, Y_BLOCKS):
        blocks = range(first, first + Y_BLOCKS)
        accs = []
        for b in blocks:
            span = slice(8 * b, 8 * b + 8)
            blank = jnp.full((8, LANES), HUGE, jnp.float32)
            accs.append([blank if start is None else start[x, span, :] for x in range(size_x)])
        for ref, table in zip(refs, tables):

            def read(j, ref=ref):
                return [ref[x, pl.ds(pl.multiple_of(8 * j, 8), 8), :] for x in range(size_x)]

            accs = sweep(accs, blocks, read, table, size_y - 8, 0, size_y // 8)
        for b, row in zip(blocks, accs):
            for x, v in enumerate(row):
                out_ref[x, 8 * b : 8 * b + 8, :] = v if scale == 1.0 else v * scale


def y_near_kernel(own_ref, code_ref, table_0, table_1, out_ref, block):
    block[...] = decode(code_ref[...])
    y_sweep((own_ref, block), (table_0, table_1), None, out_ref, 1.0)


def y_across_kernel(start_ref, code_ref, table, out_ref, block):
    block[...] = decode(code_ref[...])
    y_sweep((block,), (table,), start_ref, out_ref, 1.0)


def y_last_kernel(start_ref, code_ref, table, score_ref, depth_hbm, score_hbm, block, depth, sems):
    index = lax.axis_index("gy")
    near = jnp.abs((index ^ 3) - index) < 3
    size_y = depth.shape[1]
    scores = pltpu.make_async_copy(score_ref, score_hbm, sems.at[0])
    scores.start()
    parts = [
        pltpu.make_async_copy(depth.at[:, rows], depth_hbm.at[:, rows], sems.at[1 + i])
        for i, rows in enumerate(pl.ds(f, size_y // 2) for f in (0, size_y // 2))
    ]

    @pl.when(near)
    def _():
        block[...] = decode(code_ref[...])
        half = size_y // 16
        for i, part in enumerate(parts):
            y_sweep((block,), (table,), start_ref, depth, 1.0 / RADIUS, range(i * half, (i + 1) * half))
            part.start()

    @pl.when(jnp.logical_not(near))
    def _():
        depth[...] = start_ref[...] * (1.0 / RADIUS)
        for part in parts:
            part.start()

    for copy in (scores, *parts):
        copy.wait()


def swap(value, axis, hop):
    n = lax.axis_size(axis)
    return lax.ppermute(value, axis, [(i, i ^ hop) for i in range(n)])


def swap_xy(value, hop_x, hop_y):
    nx, ny = lax.axis_size("gx"), lax.axis_size("gy")
    pairs = [(x * ny + y, (x ^ hop_x) * ny + (y ^ hop_y)) for x in range(nx) for y in range(ny)]
    return lax.ppermute(value, ("gx", "gy"), pairs)


def neighbours(low, high, axis, beyond=0.0):
    n, index = lax.axis_size(axis), lax.axis_index(axis)
    odd = index % 2 == 1
    pairs = [(i, i + 1 if i % 2 else i - 1) for i in range(1, n - 1)]
    got_odd = lax.ppermute(jnp.where(odd, high, low), axis, pairs)
    got_even = lax.ppermute(jnp.where(odd, low, high), axis, [(i, i ^ 1) for i in range(n)])
    from_low = jnp.where(odd, got_even, got_odd)
    from_high = jnp.where(odd, got_odd, got_even)
    return jnp.where(index == 0, beyond, from_low), jnp.where(index == n - 1, beyond, from_high)


def z_swaps(value):
    nx, ny, n = (lax.axis_size(axis) for axis in ("gx", "gy", "gz"))
    even = lax.ppermute(value, "gz", [(i, i ^ 1) for i in range(n)])
    pairs = []
    for i in range(nx * ny * n):
        xy, z = i // n, i % n
        pairs.append((i, (xy ^ 1) * n + z if z in (0, n - 1) else xy * n + (z + 1 if z % 2 else z - 1)))
    return even, lax.ppermute(value, ("gx", "gy", "gz"), pairs)


def corner_swap(value):
    nx, ny = lax.axis_size("gx"), lax.axis_size("gy")
    pairs = []
    for i in range(nx * ny):
        x, y = i // ny, i % ny
        pairs.append((i, (x ^ 1) * ny + y if y in (0, ny - 1) else x * ny + (y + 1 if y % 2 else y - 1)))
    return lax.ppermute(value, ("gx", "gy"), pairs)


def conv(features, conv_weight, mask, planes, count, paired):
    channels, size_x, size_y, _ = features.shape
    return call(
        functools.partial(conv_kernel, planes, paired),
        [(size_x, size_y, LANES), (count * size_y + 8, LANES), (16, LANES), (16, LANES)],
        [
            pltpu.VMEM(features.shape, jnp.bfloat16),
            pltpu.VMEM(conv_weight.shape, jnp.bfloat16),
            pltpu.VMEM(mask.shape, jnp.int32),
            pltpu.VMEM((9 * ROWS + 8, channels * 16), jnp.bfloat16),
            pltpu.VMEM((size_x + 2, 3, ROWS, size_y // 16 * LANES), jnp.float32),
            pltpu.SemaphoreType.DMA((size_x + 2,)),
        ],
        mib=24,
        in_specs=[HBM] * 3,
    )(*(pltpu.with_memory_space_constraint(v, pltpu.HBM) for v in (features, conv_weight, mask)))


def halo_with_partner(features, conv_weight, mask):
    _, size_x, size_y, _ = features.shape

    def planes():
        return [*range(1, size_x + 1), jnp.where(lax.axis_index("gx") == 0, size_x + 1, 0)]

    s, own, chip, cross = conv(features, conv_weight, mask, planes, size_x + 1, True)
    far = swap_xy(own, 1, 0)
    sides = [swap_xy(cross, 0, 3), swap_xy(cross, 1, 3), swap_xy(chip, 0, 1), swap_xy(chip, 1, 1)]
    lines = size_x * size_y
    words = jax.ShapeDtypeStruct((LANES // 2 + 8, lines), jnp.int32)
    return call(turn_kernel, [(size_x, size_y, LANES), (LANES + 8, lines), words])(s, own, far, *sides)


def halo_in_rounds(features, conv_weight, mask):
    _, size_x, size_y, _ = features.shape
    groups = size_y // 8
    planes = [*range(1, size_x + 1), 0, size_x + 1]
    s, rest, down, up = conv(features, conv_weight, mask, lambda: planes, size_x + 2, False)

    def whole(k):
        h = jnp.roll(rest[len(planes) * size_y :], -16 * k, 1)
        part = s[k] if k < size_x else rest[k * size_y : (k + 1) * size_y]
        return jnp.concatenate([part, h, *(e[i : i + 1] for e in (down, up) for i in (k, 8 + k))], axis=0)

    low, high = neighbours(whole(size_x), whole(size_x + 1), "gx")
    own = jnp.stack([whole(k) for k in range(size_x)]).at[0].add(low).at[size_x - 1].add(high)
    e = own[:, size_y + 8 :]
    low, high = neighbours(e[:, 0:2], e[:, 2:4], "gy")
    own = own.at[:, 0].add(low[:, 0]).at[:, size_y - 1].add(high[:, 0])
    own = own.at[:, size_y].add(low[:, 1]).at[:, size_y + 7].add(high[:, 1])
    score, h = own[:, :size_y], own[:, size_y : size_y + 8]

    def line(value):
        return value.reshape(1, size_x * size_y)

    up = jnp.swapaxes(h[:, :, 0 : 2 * groups : 2], 1, 2)
    down = jnp.swapaxes(jnp.roll(h, 1, 2)[:, :, 0 : 2 * groups : 2], 1, 2)
    masked = jnp.where(mask == 1, HUGE, score)
    rows = jnp.transpose(cost_of(masked), (2, 0, 1)).reshape(LANES, size_x * size_y)
    ends = [line(v) for v in (masked[:, :, 0], masked[:, :, LANES - 1], down, up)]
    blank = [jnp.full_like(ends[0], HUGE)] * 2 + [jnp.zeros_like(ends[0])] * 2
    pairs = [v for pair in zip(ends, blank) for v in pair]
    ends = jnp.concatenate(pairs, axis=0)
    return score, jnp.concatenate([rows, ends], axis=0), pack_z(rows, ends)


def x_minima(value, size_x):
    n, index = lax.axis_size("gx"), lax.axis_index("gx")
    every = lax.all_gather(value, "gx", axis=0, tiled=True)
    at = index * size_x + jnp.arange(size_x)
    d = (at[:, None] - jnp.arange(n * size_x)[None, :]).astype(jnp.float32)
    return jnp.min(every[None] + (d * d)[:, :, None, None], axis=1)


def shards(features, conv_weight, mask):
    _, size_x, size_y, size_z = features.shape
    gx, gy = lax.axis_size("gx"), lax.axis_size("gy")
    assert size_x == 4 and size_z == LANES and size_y % 16 == 0 and LANES % size_y == 0 and gy == 4
    brick = (size_x, size_y, LANES)
    lines = size_x * size_y
    partner = gx == 2

    halo = halo_with_partner if partner else halo_in_rounds
    score, zm, words = halo(features, conv_weight, mask)

    even, odd = z_swaps(words)
    tables = (2 * size_y - 8, 8, LANES)
    own = functools.partial(z_own_kernel, size_y)
    best, table, *kept = call(own, [(LANES, lines), (LANES - Z_FLOOR, 8, LANES)] + [tables] * 4)(zm)
    work = [pltpu.VMEM((LANES, lines), jnp.float32)] * 2
    coded = jax.ShapeDtypeStruct(brick, jnp.int16)
    for first, got, shapes in ((True, even, [(LANES, lines)]), (False, odd, [brick, coded])):
        far = functools.partial(z_far_kernel, first, partner, size_x, size_y)
        best, *code = call(far, shapes, work)(best, table, zm, got)
    if not partner:
        best = x_minima(best, size_x)
        code = [encode(best).astype(jnp.int16)]

    code = code[0]
    chip, across, corner = swap(code, "gy", 1), swap(code, "gy", 2), corner_swap(code)
    block = [pltpu.VMEM(brick, jnp.float32)]
    (near,) = call(y_near_kernel, [brick], block)(best, chip, kept[0], kept[1])
    (near,) = call(y_across_kernel, [brick], block)(near, across, kept[2])
    (score,) = call(score_kernel, [brick])(score, even, odd, near)
    last = [*block, *block, pltpu.SemaphoreType.DMA((3,))]
    depth, score = call(y_last_kernel, [brick, brick], last, out_spec=HBM)(near, corner, kept[3], score)
    return score, depth


def solution(mesh):
    in_specs = (P(None, "gx", "gy", "gz"), P(), P("gx", "gy", "gz"))
    out_specs = (P("gx", "gy", "gz"), P("gx", "gy", "gz"))
    return jax.shard_map(shards, mesh=mesh, in_specs=in_specs, out_specs=out_specs, check_vma=False)
```

```python
import functools

import jax
import jax.numpy as jnp
from jax import lax
from jax.experimental import pallas as pl
from jax.experimental.pallas import tpu as pltpu
from jax.sharding import PartitionSpec as P

RADIUS = 128
CEILING = float(RADIUS * RADIUS)
HUGE = 1e30
LANES = 128
ROWS = 24
VMEM = pl.BlockSpec(memory_space=pltpu.VMEM)
HBM = pl.BlockSpec(memory_space=pltpu.HBM)


def call(kernel, outs, scratch=(), mib=8, in_specs=None, kind=jnp.float32, out_spec=VMEM):
    shapes = [s if isinstance(s, jax.ShapeDtypeStruct) else jax.ShapeDtypeStruct(s, kind) for s in outs]

    def run(*args):
        return pl.pallas_call(
            kernel,
            out_shape=shapes,
            in_specs=in_specs or [VMEM] * len(args),
            out_specs=[out_spec] * len(shapes),
            scratch_shapes=list(scratch),
            compiler_params=pltpu.CompilerParams(vmem_limit_bytes=mib * 1024 * 1024),
        )(*args)

    return run


def lane_of(shape):
    return lax.broadcasted_iota(jnp.int32, shape, len(shape) - 1)


def row_of(shape):
    return lax.broadcasted_iota(jnp.int32, shape, len(shape) - 2)


def cost_of(score):
    return CEILING / (1.0 + jnp.exp(-score))


def conv_kernel(
    planes, paired, f_hbm, w_hbm, mask_hbm, s_ref, m_ref, e_ref, d_ref, f_vmem, w_vmem, mask_vmem, w_big, acc, sems
):
    channels, size_x, size_y, _ = f_vmem.shape
    tiles = size_y // 16
    depth = channels * 16
    weights = pltpu.make_async_copy(w_hbm, w_vmem, sems.at[size_x])
    weights.start()
    copies = [
        pltpu.make_async_copy(f_hbm.at[:, x], f_vmem.at[:, x], sems.at[x]) for x in range(size_x)
    ]
    masks = pltpu.make_async_copy(mask_hbm, mask_vmem, sems.at[size_x + 1])
    masks.start()
    for copy in copies:
        copy.start()

    spread = (
        lax.broadcasted_iota(jnp.int32, (channels, depth), 1) // 16
        == lax.broadcasted_iota(jnp.int32, (channels, depth), 0)
    ).astype(jnp.bfloat16)
    row = lax.broadcasted_iota(jnp.int32, (ROWS, depth), 0)
    y_in = lax.broadcasted_iota(jnp.int32, (ROWS, depth), 1) % 16
    y_out = jnp.where(row <= 16, row, jnp.where(row == ROWS - 1, -1, 64))
    tap = y_in - y_out + 1
    weights.wait()
    wide = jnp.dot(w_vmem[...], spread, preferred_element_type=jnp.float32)
    blocks = []
    for a in range(3):
        for c in range(3):
            block = jnp.zeros((ROWS, depth), jnp.float32)
            for b in range(3):
                k = 9 * a + 3 * b + c
                block = jnp.where(tap == b, wide[k : k + 1, :], block)
            blocks.append(block)
    blocks.append(jnp.zeros((8, depth), jnp.float32))
    w_big[...] = jnp.concatenate(blocks, axis=0).astype(jnp.bfloat16)

    shape = (8, LANES)
    row, lane = row_of(shape), lane_of(shape)
    groups = size_y // 8
    to_first = lax.axis_index("gy") % 2 == 1 if paired else True
    folds = []

    def finish(p, at):
        fold = None
        for g in range(groups + 1):
            sums = []
            for c in range(3):

                def piece(tile, low, c=c):
                    return acc[at, c, low : low + 8, tile * LANES : tile * LANES + LANES]

                if g == groups:
                    part = jnp.where(row == 0, piece(tiles - 1, 16), piece(0, 16))
                else:
                    tile, low = g // 2, 8 * (g % 2)
                    part = piece(tile, low)
                    if low == 0 and tile > 0:
                        part = part + jnp.where(row == 0, piece(tile - 1, 16), 0.0)
                    if low == 8 and tile < tiles - 1:
                        part = part + jnp.where(row == 7, piece(tile + 1, 16), 0.0)
                sums.append(part)
            ahead = pltpu.roll(sums[0], 1, 1)
            behind = pltpu.roll(sums[2], LANES - 1, 1)
            inner = (
                sums[1] + jnp.where(lane == 0, 0.0, ahead) + jnp.where(lane == LANES - 1, 0.0, behind)
            )
            outer = jnp.where(lane == 0, ahead, jnp.where(lane == LANES - 1, behind, 0.0))
            if g == groups:
                for up, down, at_row in (
                    (inner, inner, p),
                    (outer, pltpu.roll(outer, 2 * (groups - 1), 1), 8 + p),
                ):
                    e_ref[at_row : at_row + 1, :] = jnp.where(to_first, down[7:8], up[0:1])
                    d_ref[at_row : at_row + 1, :] = jnp.where(to_first, up[0:1], down[7:8])
            else:
                span = slice(8 * g, 8 * g + 8)
                if p < size_x:
                    s_ref[p, span, :] = inner
                    inner = jnp.where(mask_vmem[p, span, :] == 1, HUGE, inner)
                m_ref[p * size_y + 8 * g : p * size_y + 8 * g + 8, :] = inner
                shift = 16 * p + 2 * g
                outer = pltpu.roll(outer, shift, 1) if shift else outer
                fold = outer if g == 0 else fold + outer
        folds.append(fold)

    at_plane = planes()
    half = size_x // 2
    for x in range(size_x):
        if x % half == 0:
            for copy in copies[x : x + half]:
                copy.wait()
            if x:
                masks.wait()
                finish(x - half, at_plane[x - half])
        right = jnp.concatenate(
            [f_vmem[:, x, 16 * t : 16 * t + 16, :].reshape(depth, LANES) for t in range(tiles)],
            axis=1,
        )
        if x == size_x - 1:
            finish(x - 2, at_plane[x - 2])
        got = jnp.dot(w_big[...], right, preferred_element_type=jnp.float32)
        for a in range(3):
            at = x + 2 - a
            for c in range(3):
                first = (3 * a + c) * ROWS
                part = got[first : first + ROWS, :]
                acc[at, c] = part if a == 0 or x == 0 else acc[at, c] + part
    for p in range(size_x - 2, len(at_plane)):
        finish(p, at_plane[p])
    m_ref[len(folds) * size_y :, :] = functools.reduce(jnp.add, folds)


CODES = 4681.0
LN2 = 0.6931471805599453
TOP = 2.0**30


def encode(value):
    code = jnp.round(jnp.log(value + 1.0) * (CODES / LN2)) - 32768.0
    return jnp.clip(code, -32768.0, 32767.0).astype(jnp.int32)


def decode(code):
    level = code.astype(jnp.int32).astype(jnp.float32) + 32768.0
    return jnp.exp(level * (LN2 / CODES)) - 1.0


def pack_z(rows, ends):
    half = LANES // 2
    code = encode(rows)
    masked = ends >= 0.5 * HUGE
    most = jnp.max(jnp.where(masked, 0.0, jnp.abs(ends)), axis=1, keepdims=True)
    most = jnp.max(most, axis=0, keepdims=True)
    power = jnp.ceil(jnp.log(jnp.maximum(most, 1e-18)) * (1.0 / LN2)) + 1.0
    scores = jnp.round(jnp.where(masked, TOP, ends * (jnp.exp(power * -LN2) * TOP))).astype(jnp.int32)
    first = jnp.where(row_of((half, rows.shape[1])) == 0, power.astype(jnp.int32), code[:half])
    return jnp.concatenate([(first << 16) | (code[half:] & 0xFFFF), scores], axis=0)


def unpack_rows(words):
    return decode(words >> 16), decode((words << 16) >> 16)


def unpack_ends(ref):
    half = LANES // 2
    power = (ref[0:8, :] >> 16)[0:1].astype(jnp.float32)
    scores = ref[half : half + 8, :].astype(jnp.float32)
    return jnp.where(scores >= 0.75 * TOP, HUGE, scores * (jnp.exp(power * LN2) * (1.0 / TOP)))


def y_masks(axis, chip):
    row = row_of((8, LANES))
    index, last = lax.axis_index(axis), lax.axis_size(axis) - 1
    odd = index % 2
    if chip:
        low, high = odd == 1, odd == 0
    else:
        low, high = (odd == 0) & (index > 0), (odd == 1) & (index < last)
    return row == jnp.where(low, 0, -1), row == jnp.where(high, 7, -1)


def edge_rows(masks, part, size_y):
    low, high = masks
    return jnp.concatenate(
        [
            jnp.where(low, part, 0.0),
            jnp.zeros((size_y - 16, LANES), jnp.float32),
            jnp.where(high, part, 0.0),
        ],
        axis=0,
    )


def turn_kernel(s_ref, own_ref, far_ref, cross_ref, xcross_ref, chip_ref, xchip_ref, score_ref, zm_ref, words_ref):
    size_x, size_y, _ = s_ref.shape
    chip, cross = y_masks("gy", True), y_masks("gy", False)
    first = lax.axis_index("gx") == 0
    lane = lane_of((size_y, LANES))
    border = (lane == 0) | (lane == LANES - 1)
    faces_own = {size_x - 1: jnp.where(first, 1.0, 0.0), 0: jnp.where(first, 0.0, 1.0)}
    faces_far = {0: faces_own[size_x - 1], size_x - 1: faces_own[0]}

    def plane(ref, p):
        return ref[p * size_y : (p + 1) * size_y, :]

    def fold(ref, p):
        rest = ref[(size_x + 1) * size_y :, :]
        return pltpu.roll(rest, LANES - 16 * p, 1) if p else rest

    def complete(p, base, folded, face_ref, sides, faces):
        if p in faces:
            base = base + faces[p] * plane(face_ref, size_x)
            folded = folded + faces[p] * fold(face_ref, size_x)
        for masks, same, other in sides:
            part, part_h = same[p : p + 1], same[8 + p : 9 + p]
            if p in faces:
                part = part + faces[p] * other[size_x : size_x + 1]
                part_h = part_h + faces[p] * other[8 + size_x : 9 + size_x]
            base = base + edge_rows(masks, part, size_y)
            folded = folded + jnp.where(masks[0] | masks[1], part_h, 0.0)
        return base, folded

    costs, turned = [], []
    for far in range(2):
        for p in range(size_x):
            if far:
                sides = ((chip, xchip_ref, chip_ref), (cross, xcross_ref, cross_ref))
                masked, h = complete(p, plane(far_ref, p), fold(far_ref, p), own_ref, sides, faces_far)
            else:
                sides = ((chip, chip_ref, xchip_ref), (cross, cross_ref, xcross_ref))
                full, h = complete(p, s_ref[p], fold(own_ref, p), far_ref, sides, faces_own)
                score_ref[p] = full
                masked = jnp.where(plane(own_ref, p) == HUGE, HUGE, full)
            costs.append(cost_of(masked))
            wide = jnp.concatenate(
                [pltpu.roll(h, (2 - 2 * g) % LANES, 1) for g in range(size_y // 8)], axis=0
            )
            turned.append(jnp.where(border, masked, wide))
    away = jnp.where(first, float(size_x), -float(size_x))
    lines = []
    for i in range(size_x):
        best = costs[i]
        for j in range(size_x):
            if j != i:
                best = jnp.minimum(best, costs[j] + float((i - j) ** 2))
            d = float(j - i) + away
            best = jnp.minimum(best, costs[size_x + j] + d * d)
        lines.append(best)
    width = size_x * size_y
    rows = jnp.concatenate(lines, axis=0).T
    ends = jnp.concatenate(turned, axis=0).T
    ends = jnp.concatenate(
        [ends[r : r + 1, k * width : (k + 1) * width] for r in (0, LANES - 1, 1, 2) for k in range(2)],
        axis=0,
    )
    zm_ref[0:LANES, :] = rows
    zm_ref[LANES : LANES + 8, :] = ends
    words_ref[...] = pack_z(rows, ends)


Z_FLOOR = -(LANES + 6)


def sweep(accs, blocks, read, table, shift, low, high):
    parts = len(accs[0])

    def body(j, flat):
        flat = list(flat)
        tiles = read(j)
        squares = table.at[pl.ds(shift + 8 * blocks[0] - 8 * j, 8 * len(blocks))]
        for r in range(8):
            rows = [jnp.broadcast_to(t[r : r + 1, :], (8, LANES)) for t in tiles]
            for i in range(len(blocks)):
                square = squares[8 * i + 7 - r]
                for k in range(parts):
                    at = i * parts + k
                    flat[at] = jnp.minimum(flat[at], rows[k] + square)
        return tuple(flat)

    flat = lax.fori_loop(low, high, body, tuple(v for row in accs for v in row))
    return [list(flat[i * parts : (i + 1) * parts]) for i in range(len(blocks))]


def tiles_of(ref, j):
    rows = pl.ds(pl.multiple_of(8 * j, 8), 8)
    return [ref[rows, k * LANES : (k + 1) * LANES] for k in range(ref.shape[1] // LANES)]


def load_blocks(ref, blocks):
    return [tiles_of(ref, b) for b in blocks]


def save_blocks(ref, blocks, accs):
    for b, row in zip(blocks, accs):
        for k, v in enumerate(row):
            ref[8 * b : 8 * b + 8, k * LANES : (k + 1) * LANES] = v


def y_table(axis, hop, size_y, table):
    index = lax.axis_index(axis)
    away = (((index ^ hop) - index) * size_y).astype(jnp.float32)
    s = row_of((8, LANES)).astype(jnp.float32) - away
    for d in range(1 - size_y, size_y - 7):
        v = s + float(d)
        table[d - (1 - size_y)] = v * v


def z_own_kernel(zm_ref, out_ref, table):
    count, half = LANES // 8, LANES // 16
    s = row_of((8, LANES)).astype(jnp.float32)
    for d in range(Z_FLOOR, LANES):
        v = s + float(d)
        table[d - Z_FLOOR] = v * v

    def read(j):
        at = row_of((8, LANES)) + 8 * j
        hide = (at == 0) | (at == LANES - 1)
        return [jnp.where(hide, HUGE, t) for t in tiles_of(zm_ref, j)]

    for first in (0, half):
        blocks = range(first, first + half)
        accs = [[jnp.full((8, LANES), HUGE, jnp.float32)] * (out_ref.shape[1] // LANES) for _ in blocks]
        save_blocks(out_ref, blocks, sweep(accs, blocks, read, table, -7 - Z_FLOOR, 0, count))


def border_minima(cost, size_x, size_y, partner):
    if not partner:
        return cost
    width = cost.shape[1]
    shape = (8, width)
    row, plane = row_of(shape), lane_of(shape) // size_y
    away = jnp.where(lax.axis_index("gx") == 0, size_x, -size_x)
    shift = jnp.where(row % 2 == 1, away, 0)
    best = None
    for r in range(size_x):
        source = jnp.where(plane >= r, plane - r, plane - r + size_x)
        d = (source + shift - plane).astype(jnp.float32)
        if r == 0:
            moved = cost
        else:
            cut = width - r * size_y
            moved = jnp.concatenate([cost[:, cut:], cost[:, :cut]], axis=1)
        moved = moved + d * d
        best = moved if best is None else jnp.minimum(best, moved)
    return jnp.minimum(best, pltpu.roll(best, 7, 0))


def z_far_kernel(even, partner, size_x, size_y, acc_ref, table, zm_ref, got_ref, out_ref, *refs):
    *code_ref, source, work = refs
    index, last = lax.axis_index("gz"), lax.axis_size("gz") - 1
    odd = index % 2 == 1
    low = odd if even else jnp.logical_not(odd)
    valid = jnp.where(low, index > 0, index < last)
    count, half = LANES // 8, LANES // 16
    out = out_ref if even else work
    own, got = zm_ref[LANES : LANES + 8, :], unpack_ends(got_ref)
    lanes = [slice(k * LANES, (k + 1) * LANES) for k in range(zm_ref.shape[1] // LANES)]
    source[0 : LANES // 2, :], source[LANES // 2 :, :] = unpack_rows(got_ref[0 : LANES // 2, :])

    def minima(mine, theirs):
        ends = cost_of(jnp.concatenate([mine, theirs, mine, theirs], axis=0))
        return border_minima(ends, size_x, size_y, partner)

    def add_ends(ends, start, places):
        for b in range(count):
            span = slice(8 * b, 8 * b + 8)
            for cols in lanes:
                best = start[span, cols]
                for i, place in enumerate(places):
                    row = jnp.broadcast_to(ends[2 * i : 2 * i + 1, cols], (8, LANES))
                    best = jnp.minimum(best, row + table[8 * b - place - Z_FLOOR])
                out[span, cols] = best

    def slanted(accs, blocks, offset, skip, reach):
        for j in blocks:
            tile = tiles_of(source, j)
            for r in range(8):
                q = 8 * j + r
                rows = [jnp.broadcast_to(t[r : r + 1, :], (8, LANES)) for t in tile]
                for i, b in enumerate(blocks):
                    if reach(b, q) and q != skip:
                        square = table[8 * b - q + offset - Z_FLOOR]
                        accs[i] = [jnp.minimum(v, row + square) for v, row in zip(accs[i], rows)]
        return accs

    def far(offset, skip, reach, more):
        source[skip : skip + 1, :] = jnp.full((1, zm_ref.shape[1]), HUGE, jnp.float32)
        for first in (0, half):
            blocks = range(first, first + half)
            accs = slanted(load_blocks(acc_ref, blocks), blocks, offset, skip, reach)
            if more(first):
                read = functools.partial(tiles_of, source)
                accs = sweep(accs, blocks, read, table, offset - 7 - Z_FLOOR, *more(first))
            save_blocks(out, blocks, accs)

    @pl.when(valid & low)
    def _():
        ends = minima(own[0:2] + got[6:8], got[2:4] + own[4:6])
        far(LANES, LANES - 1, lambda b, q: 8 * b < q, lambda first: None if first else (half, count))
        add_ends(ends, out, (0, -1))

    @pl.when(valid & jnp.logical_not(low))
    def _():
        ends = minima(own[2:4] + got[4:6], got[0:2] + own[6:8])
        far(-LANES, 0, lambda b, q: q < 8 * b + 7, lambda first: (0, first) if first else None)
        add_ends(ends, out, (LANES - 1, LANES))

    @pl.when(jnp.logical_not(valid) & low)
    def _():
        add_ends(minima(own[0:2], own[0:2]), acc_ref, (0,))

    @pl.when(jnp.logical_not(valid) & jnp.logical_not(low))
    def _():
        add_ends(minima(own[2:4], own[2:4]), acc_ref, (LANES - 1,))

    if not even:
        per = LANES // size_y
        for k, cols in enumerate(lanes):
            best = work[:, cols].T
            code = encode(best).astype(jnp.int16)
            for i in range(per):
                out_ref[k * per + i] = best[i * size_y : (i + 1) * size_y]
                code_ref[0][k * per + i] = code[i * size_y : (i + 1) * size_y]


def score_kernel(score_in, even_ref, odd_ref, _, score_ref):
    index, last = lax.axis_index("gz"), lax.axis_size("gz") - 1
    odd = index % 2 == 1
    size_y = score_in.shape[1]
    per = LANES // size_y
    even_ends, odd_ends = unpack_ends(even_ref), unpack_ends(odd_ref)
    for k in range(even_ref.shape[1] // LANES):
        cols = slice(k * LANES, (k + 1) * LANES)
        even_rows, odd_rows = even_ends[:, cols], odd_ends[:, cols]
        low = jnp.where(index > 0, jnp.where(odd, even_rows, odd_rows)[6:7], 0.0)
        high = jnp.where(index < last, jnp.where(odd, odd_rows, even_rows)[4:5], 0.0)
        middle = jnp.zeros((LANES - 2, LANES), jnp.float32)
        more = jnp.concatenate([low, middle, high], axis=0).T
        for i in range(per):
            x = k * per + i
            score_ref[x] = score_in[x] + more[i * size_y : (i + 1) * size_y]


Y_BLOCKS = 4


def y_sweep(refs, tables, start, out_ref, scale, span=None):
    size_x, size_y, _ = out_ref.shape
    span = span or range(size_y // 8)
    for first in range(span[0], span[-1] + 1, Y_BLOCKS):
        blocks = range(first, first + Y_BLOCKS)
        accs = []
        for b in blocks:
            span = slice(8 * b, 8 * b + 8)
            blank = jnp.full((8, LANES), HUGE, jnp.float32)
            accs.append([blank if start is None else start[x, span, :] for x in range(size_x)])
        for ref, table in zip(refs, tables):

            def read(j, ref=ref):
                return [ref[x, pl.ds(pl.multiple_of(8 * j, 8), 8), :] for x in range(size_x)]

            accs = sweep(accs, blocks, read, table, size_y - 8, 0, size_y // 8)
        for b, row in zip(blocks, accs):
            for x, v in enumerate(row):
                out_ref[x, 8 * b : 8 * b + 8, :] = v if scale == 1.0 else v * scale


def y_near_kernel(own_ref, code_ref, out_ref, table_2, table_3, block, table_0, table_1):
    for hop, table in enumerate((table_0, table_1, table_2, table_3)):
        y_table("gy", hop, own_ref.shape[1], table)
    block[...] = decode(code_ref[...])
    y_sweep((own_ref, block), (table_0, table_1), None, out_ref, 1.0)


def y_across_kernel(start_ref, code_ref, table, out_ref, block):
    block[...] = decode(code_ref[...])
    y_sweep((block,), (table,), start_ref, out_ref, 1.0)


def y_last_kernel(start_ref, code_ref, table, score_ref, depth_hbm, score_hbm, block, depth, sems):
    index = lax.axis_index("gy")
    near = jnp.abs((index ^ 3) - index) < 3
    size_y = depth.shape[1]
    scores = pltpu.make_async_copy(score_ref, score_hbm, sems.at[0])
    scores.start()
    parts = [
        pltpu.make_async_copy(depth.at[:, rows], depth_hbm.at[:, rows], sems.at[1 + i])
        for i, rows in enumerate(pl.ds(f, size_y // 2) for f in (0, size_y // 2))
    ]

    @pl.when(near)
    def _():
        block[...] = decode(code_ref[...])
        half = size_y // 16
        for i, part in enumerate(parts):
            y_sweep((block,), (table,), start_ref, depth, 1.0 / RADIUS, range(i * half, (i + 1) * half))
            part.start()

    @pl.when(jnp.logical_not(near))
    def _():
        depth[...] = start_ref[...] * (1.0 / RADIUS)
        for part in parts:
            part.start()

    for copy in (scores, *parts):
        copy.wait()


def swap(value, axis, hop):
    n = lax.axis_size(axis)
    return lax.ppermute(value, axis, [(i, i ^ hop) for i in range(n)])


def swap_xy(value, hop_x, hop_y):
    nx, ny = lax.axis_size("gx"), lax.axis_size("gy")
    pairs = [(x * ny + y, (x ^ hop_x) * ny + (y ^ hop_y)) for x in range(nx) for y in range(ny)]
    return lax.ppermute(value, ("gx", "gy"), pairs)


def neighbours(low, high, axis, beyond=0.0):
    n, index = lax.axis_size(axis), lax.axis_index(axis)
    odd = index % 2 == 1
    pairs = [(i, i + 1 if i % 2 else i - 1) for i in range(1, n - 1)]
    got_odd = lax.ppermute(jnp.where(odd, high, low), axis, pairs)
    got_even = lax.ppermute(jnp.where(odd, low, high), axis, [(i, i ^ 1) for i in range(n)])
    from_low = jnp.where(odd, got_even, got_odd)
    from_high = jnp.where(odd, got_odd, got_even)
    return jnp.where(index == 0, beyond, from_low), jnp.where(index == n - 1, beyond, from_high)


def z_swaps(value):
    nx, ny, n = (lax.axis_size(axis) for axis in ("gx", "gy", "gz"))
    even = lax.ppermute(value, "gz", [(i, i ^ 1) for i in range(n)])
    pairs = []
    for i in range(nx * ny * n):
        xy, z = i // n, i % n
        pairs.append((i, (xy ^ 1) * n + z if z in (0, n - 1) else xy * n + (z + 1 if z % 2 else z - 1)))
    return even, lax.ppermute(value, ("gx", "gy", "gz"), pairs)


def corner_swap(value):
    nx, ny = lax.axis_size("gx"), lax.axis_size("gy")
    pairs = []
    for i in range(nx * ny):
        x, y = i // ny, i % ny
        pairs.append((i, (x ^ 1) * ny + y if y in (0, ny - 1) else x * ny + (y + 1 if y % 2 else y - 1)))
    return lax.ppermute(value, ("gx", "gy"), pairs)


def conv(features, conv_weight, mask, planes, count, paired):
    channels, size_x, size_y, _ = features.shape
    return call(
        functools.partial(conv_kernel, planes, paired),
        [(size_x, size_y, LANES), (count * size_y + 8, LANES), (16, LANES), (16, LANES)],
        [
            pltpu.VMEM(features.shape, jnp.bfloat16),
            pltpu.VMEM(conv_weight.shape, jnp.bfloat16),
            pltpu.VMEM(mask.shape, jnp.int32),
            pltpu.VMEM((9 * ROWS + 8, channels * 16), jnp.bfloat16),
            pltpu.VMEM((size_x + 2, 3, ROWS, size_y // 16 * LANES), jnp.float32),
            pltpu.SemaphoreType.DMA((size_x + 2,)),
        ],
        mib=24,
        in_specs=[HBM] * 3,
    )(*(pltpu.with_memory_space_constraint(v, pltpu.HBM) for v in (features, conv_weight, mask)))


def halo_with_partner(features, conv_weight, mask):
    _, size_x, size_y, _ = features.shape

    def planes():
        return [*range(1, size_x + 1), jnp.where(lax.axis_index("gx") == 0, size_x + 1, 0)]

    s, own, chip, cross = conv(features, conv_weight, mask, planes, size_x + 1, True)
    far = swap_xy(own, 1, 0)
    sides = [swap_xy(cross, 0, 3), swap_xy(cross, 1, 3), swap_xy(chip, 0, 1), swap_xy(chip, 1, 1)]
    lines = size_x * size_y
    words = jax.ShapeDtypeStruct((LANES // 2 + 8, lines), jnp.int32)
    return call(turn_kernel, [(size_x, size_y, LANES), (LANES + 8, lines), words])(s, own, far, *sides)


def halo_in_rounds(features, conv_weight, mask):
    _, size_x, size_y, _ = features.shape
    groups = size_y // 8
    planes = [*range(1, size_x + 1), 0, size_x + 1]
    s, rest, down, up = conv(features, conv_weight, mask, lambda: planes, size_x + 2, False)

    def whole(k):
        h = jnp.roll(rest[len(planes) * size_y :], -16 * k, 1)
        part = s[k] if k < size_x else rest[k * size_y : (k + 1) * size_y]
        return jnp.concatenate([part, h, *(e[i : i + 1] for e in (down, up) for i in (k, 8 + k))], axis=0)

    low, high = neighbours(whole(size_x), whole(size_x + 1), "gx")
    own = jnp.stack([whole(k) for k in range(size_x)]).at[0].add(low).at[size_x - 1].add(high)
    e = own[:, size_y + 8 :]
    low, high = neighbours(e[:, 0:2], e[:, 2:4], "gy")
    own = own.at[:, 0].add(low[:, 0]).at[:, size_y - 1].add(high[:, 0])
    own = own.at[:, size_y].add(low[:, 1]).at[:, size_y + 7].add(high[:, 1])
    score, h = own[:, :size_y], own[:, size_y : size_y + 8]

    def line(value):
        return value.reshape(1, size_x * size_y)

    up = jnp.swapaxes(h[:, :, 0 : 2 * groups : 2], 1, 2)
    down = jnp.swapaxes(jnp.roll(h, 1, 2)[:, :, 0 : 2 * groups : 2], 1, 2)
    masked = jnp.where(mask == 1, HUGE, score)
    rows = jnp.transpose(cost_of(masked), (2, 0, 1)).reshape(LANES, size_x * size_y)
    ends = [line(v) for v in (masked[:, :, 0], masked[:, :, LANES - 1], down, up)]
    blank = [jnp.full_like(ends[0], HUGE)] * 2 + [jnp.zeros_like(ends[0])] * 2
    pairs = [v for pair in zip(ends, blank) for v in pair]
    ends = jnp.concatenate(pairs, axis=0)
    return score, jnp.concatenate([rows, ends], axis=0), pack_z(rows, ends)


def x_minima(value, size_x):
    n, index = lax.axis_size("gx"), lax.axis_index("gx")
    every = lax.all_gather(value, "gx", axis=0, tiled=True)
    at = index * size_x + jnp.arange(size_x)
    d = (at[:, None] - jnp.arange(n * size_x)[None, :]).astype(jnp.float32)
    return jnp.min(every[None] + (d * d)[:, :, None, None], axis=1)


def shards(features, conv_weight, mask):
    _, size_x, size_y, size_z = features.shape
    gx, gy = lax.axis_size("gx"), lax.axis_size("gy")
    assert size_x == 4 and size_z == LANES and size_y % 16 == 0 and LANES % size_y == 0 and gy == 4
    brick = (size_x, size_y, LANES)
    lines = size_x * size_y
    partner = gx == 2

    halo = halo_with_partner if partner else halo_in_rounds
    score, zm, words = halo(features, conv_weight, mask)

    even, odd = z_swaps(words)
    tables = (2 * size_y - 8, 8, LANES)
    best, table = call(z_own_kernel, [(LANES, lines), (LANES - Z_FLOOR, 8, LANES)])(zm)
    work = [pltpu.VMEM((LANES, lines), jnp.float32)] * 2
    coded = jax.ShapeDtypeStruct(brick, jnp.int16)
    for first, got, shapes in ((True, even, [(LANES, lines)]), (False, odd, [brick, coded])):
        far = functools.partial(z_far_kernel, first, partner, size_x, size_y)
        best, *code = call(far, shapes, work)(best, table, zm, got)
    if not partner:
        best = x_minima(best, size_x)
        code = [encode(best).astype(jnp.int16)]

    code = code[0]
    chip, across, corner = swap(code, "gy", 1), swap(code, "gy", 2), corner_swap(code)
    block = [pltpu.VMEM(brick, jnp.float32)]
    scratch = [*block, *[pltpu.VMEM(tables, jnp.float32)] * 2]
    near, table_2, table_3 = call(y_near_kernel, [brick, tables, tables], scratch)(best, chip)
    (near,) = call(y_across_kernel, [brick], block)(near, across, table_2)
    (score,) = call(score_kernel, [brick])(score, even, odd, near)
    last = [*block, *block, pltpu.SemaphoreType.DMA((3,))]
    depth, score = call(y_last_kernel, [brick, brick], last, out_spec=HBM)(near, corner, table_3, score)
    return score, depth


def solution(mesh):
    in_specs = (P(None, "gx", "gy", "gz"), P(), P("gx", "gy", "gz"))
    out_specs = (P("gx", "gy", "gz"), P("gx", "gy", "gz"))
    return jax.shard_map(shards, mesh=mesh, in_specs=in_specs, out_specs=out_specs, check_vma=False)
```

```python
import functools

import jax
import jax.numpy as jnp
from jax import lax
from jax.experimental import pallas as pl
from jax.experimental.pallas import tpu as pltpu
from jax.sharding import PartitionSpec as P

RADIUS = 128
CEILING = float(RADIUS * RADIUS)
HUGE = 1e30
LANES = 128
ROWS = 24
VMEM = pl.BlockSpec(memory_space=pltpu.VMEM)
HBM = pl.BlockSpec(memory_space=pltpu.HBM)


def call(kernel, outs, scratch=(), mib=8, in_specs=None, kind=jnp.float32, out_spec=VMEM):
    shapes = [s if isinstance(s, jax.ShapeDtypeStruct) else jax.ShapeDtypeStruct(s, kind) for s in outs]

    def run(*args):
        return pl.pallas_call(
            kernel,
            out_shape=shapes,
            in_specs=in_specs or [VMEM] * len(args),
            out_specs=[out_spec] * len(shapes),
            scratch_shapes=list(scratch),
            compiler_params=pltpu.CompilerParams(vmem_limit_bytes=mib * 1024 * 1024),
        )(*args)

    return run


def lane_of(shape):
    return lax.broadcasted_iota(jnp.int32, shape, len(shape) - 1)


def row_of(shape):
    return lax.broadcasted_iota(jnp.int32, shape, len(shape) - 2)


def cost_of(score):
    return CEILING / (1.0 + jnp.exp(-score))


def conv_kernel(
    planes, paired, f_hbm, w_hbm, mask_hbm, s_ref, m_ref, e_ref, d_ref, f_vmem, w_vmem, mask_vmem, w_big, acc, sems
):
    channels, size_x, size_y, _ = f_vmem.shape
    tiles = size_y // 16
    depth = channels * 16
    weights = pltpu.make_async_copy(w_hbm, w_vmem, sems.at[size_x])
    weights.start()
    copies = [
        pltpu.make_async_copy(f_hbm.at[:, x], f_vmem.at[:, x], sems.at[x]) for x in range(size_x)
    ]
    masks = pltpu.make_async_copy(mask_hbm, mask_vmem, sems.at[size_x + 1])
    masks.start()
    for copy in copies:
        copy.start()

    spread = (
        lax.broadcasted_iota(jnp.int32, (channels, depth), 1) // 16
        == lax.broadcasted_iota(jnp.int32, (channels, depth), 0)
    ).astype(jnp.bfloat16)
    row = lax.broadcasted_iota(jnp.int32, (ROWS, depth), 0)
    y_in = lax.broadcasted_iota(jnp.int32, (ROWS, depth), 1) % 16
    y_out = jnp.where(row <= 16, row, jnp.where(row == ROWS - 1, -1, 64))
    tap = y_in - y_out + 1
    weights.wait()
    wide = jnp.dot(w_vmem[...], spread, preferred_element_type=jnp.float32)
    blocks = []
    for a in range(3):
        for c in range(3):
            block = jnp.zeros((ROWS, depth), jnp.float32)
            for b in range(3):
                k = 9 * a + 3 * b + c
                block = jnp.where(tap == b, wide[k : k + 1, :], block)
            blocks.append(block)
    blocks.append(jnp.zeros((8, depth), jnp.float32))
    w_big[...] = jnp.concatenate(blocks, axis=0).astype(jnp.bfloat16)

    shape = (8, LANES)
    row, lane = row_of(shape), lane_of(shape)
    groups = size_y // 8
    to_first = lax.axis_index("gy") % 2 == 1 if paired else True
    folds = []

    def finish(p, at):
        fold = None
        for g in range(groups + 1):
            sums = []
            for c in range(3):

                def piece(tile, low, c=c):
                    return acc[at, c, low : low + 8, tile * LANES : tile * LANES + LANES]

                if g == groups:
                    part = jnp.where(row == 0, piece(tiles - 1, 16), piece(0, 16))
                else:
                    tile, low = g // 2, 8 * (g % 2)
                    part = piece(tile, low)
                    if low == 0 and tile > 0:
                        part = part + jnp.where(row == 0, piece(tile - 1, 16), 0.0)
                    if low == 8 and tile < tiles - 1:
                        part = part + jnp.where(row == 7, piece(tile + 1, 16), 0.0)
                sums.append(part)
            ahead = pltpu.roll(sums[0], 1, 1)
            behind = pltpu.roll(sums[2], LANES - 1, 1)
            inner = (
                sums[1] + jnp.where(lane == 0, 0.0, ahead) + jnp.where(lane == LANES - 1, 0.0, behind)
            )
            outer = jnp.where(lane == 0, ahead, jnp.where(lane == LANES - 1, behind, 0.0))
            if g == groups:
                for up, down, at_row in (
                    (inner, inner, p),
                    (outer, pltpu.roll(outer, 2 * (groups - 1), 1), 8 + p),
                ):
                    e_ref[at_row : at_row + 1, :] = jnp.where(to_first, down[7:8], up[0:1])
                    d_ref[at_row : at_row + 1, :] = jnp.where(to_first, up[0:1], down[7:8])
            else:
                span = slice(8 * g, 8 * g + 8)
                if p < size_x:
                    s_ref[p, span, :] = inner
                    inner = jnp.where(mask_vmem[p, span, :] == 1, HUGE, inner)
                m_ref[p * size_y + 8 * g : p * size_y + 8 * g + 8, :] = inner
                shift = 16 * p + 2 * g
                outer = pltpu.roll(outer, shift, 1) if shift else outer
                fold = outer if g == 0 else fold + outer
        folds.append(fold)

    at_plane = planes()
    half = size_x // 2
    for x in range(size_x):
        if x % half == 0:
            for copy in copies[x : x + half]:
                copy.wait()
            if x:
                masks.wait()
                finish(x - half, at_plane[x - half])
        right = jnp.concatenate(
            [f_vmem[:, x, 16 * t : 16 * t + 16, :].reshape(depth, LANES) for t in range(tiles)],
            axis=1,
        )
        if x == size_x - 1:
            finish(x - 2, at_plane[x - 2])
        got = jnp.dot(w_big[...], right, preferred_element_type=jnp.float32)
        for a in range(3):
            at = x + 2 - a
            for c in range(3):
                first = (3 * a + c) * ROWS
                part = got[first : first + ROWS, :]
                acc[at, c] = part if a == 0 or x == 0 else acc[at, c] + part
    for p in range(size_x - 2, len(at_plane)):
        finish(p, at_plane[p])
    m_ref[len(folds) * size_y :, :] = functools.reduce(jnp.add, folds)


CODES = 4681.0
LN2 = 0.6931471805599453
TOP = 2.0**30


def encode(value):
    code = jnp.round(jnp.log(value + 1.0) * (CODES / LN2) - 32768.0)
    return jnp.minimum(code, 32767.0).astype(jnp.int32)


def decode(code):
    level = code.astype(jnp.int32).astype(jnp.float32)
    return jnp.exp(level * (LN2 / CODES) + 32768.0 * (LN2 / CODES)) - 1.0


def pack_z(rows, ends):
    half = LANES // 2
    code = encode(rows)
    masked = ends >= 0.5 * HUGE
    most = jnp.max(jnp.where(masked, 0.0, jnp.abs(ends)), axis=1, keepdims=True)
    most = jnp.max(most, axis=0, keepdims=True)
    power = jnp.ceil(jnp.log(jnp.maximum(most, 1e-18)) * (1.0 / LN2)) + 1.0
    scores = jnp.round(jnp.where(masked, TOP, ends * (jnp.exp(power * -LN2) * TOP))).astype(jnp.int32)
    first = jnp.where(row_of((half, rows.shape[1])) == 0, power.astype(jnp.int32), code[:half])
    return jnp.concatenate([(first << 16) | (code[half:] & 0xFFFF), scores], axis=0)


def unpack_rows(words):
    return decode(words >> 16), decode((words << 16) >> 16)


def unpack_ends(ref):
    half = LANES // 2
    power = (ref[0:8, :] >> 16)[0:1].astype(jnp.float32)
    scores = ref[half : half + 8, :].astype(jnp.float32)
    return jnp.where(scores >= 0.75 * TOP, HUGE, scores * (jnp.exp(power * LN2) * (1.0 / TOP)))


def y_masks(axis, chip):
    row = row_of((8, LANES))
    index, last = lax.axis_index(axis), lax.axis_size(axis) - 1
    odd = index % 2
    if chip:
        low, high = odd == 1, odd == 0
    else:
        low, high = (odd == 0) & (index > 0), (odd == 1) & (index < last)
    return row == jnp.where(low, 0, -1), row == jnp.where(high, 7, -1)


def edge_rows(masks, part, size_y):
    low, high = masks
    return jnp.concatenate(
        [
            jnp.where(low, part, 0.0),
            jnp.zeros((size_y - 16, LANES), jnp.float32),
            jnp.where(high, part, 0.0),
        ],
        axis=0,
    )


def turn_kernel(s_ref, own_ref, far_ref, cross_ref, xcross_ref, chip_ref, xchip_ref, score_ref, zm_ref, words_ref):
    size_x, size_y, _ = s_ref.shape
    chip, cross = y_masks("gy", True), y_masks("gy", False)
    first = lax.axis_index("gx") == 0
    lane = lane_of((size_y, LANES))
    border = (lane == 0) | (lane == LANES - 1)
    faces_own = {size_x - 1: jnp.where(first, 1.0, 0.0), 0: jnp.where(first, 0.0, 1.0)}
    faces_far = {0: faces_own[size_x - 1], size_x - 1: faces_own[0]}

    def plane(ref, p):
        return ref[p * size_y : (p + 1) * size_y, :]

    def fold(ref, p):
        rest = ref[(size_x + 1) * size_y :, :]
        return pltpu.roll(rest, LANES - 16 * p, 1) if p else rest

    def complete(p, base, folded, face_ref, sides, faces):
        if p in faces:
            base = base + faces[p] * plane(face_ref, size_x)
            folded = folded + faces[p] * fold(face_ref, size_x)
        for masks, same, other in sides:
            part, part_h = same[p : p + 1], same[8 + p : 9 + p]
            if p in faces:
                part = part + faces[p] * other[size_x : size_x + 1]
                part_h = part_h + faces[p] * other[8 + size_x : 9 + size_x]
            base = base + edge_rows(masks, part, size_y)
            folded = folded + jnp.where(masks[0] | masks[1], part_h, 0.0)
        return base, folded

    costs, turned = [], []
    for far in range(2):
        for p in range(size_x):
            if far:
                sides = ((chip, xchip_ref, chip_ref), (cross, xcross_ref, cross_ref))
                masked, h = complete(p, plane(far_ref, p), fold(far_ref, p), own_ref, sides, faces_far)
            else:
                sides = ((chip, chip_ref, xchip_ref), (cross, cross_ref, xcross_ref))
                full, h = complete(p, s_ref[p], fold(own_ref, p), far_ref, sides, faces_own)
                score_ref[p] = full
                masked = jnp.where(plane(own_ref, p) == HUGE, HUGE, full)
            costs.append(cost_of(masked))
            wide = jnp.concatenate(
                [pltpu.roll(h, (2 - 2 * g) % LANES, 1) for g in range(size_y // 8)], axis=0
            )
            turned.append(jnp.where(border, masked, wide))
    away = jnp.where(first, float(size_x), -float(size_x))
    lines = []
    for i in range(size_x):
        best = costs[i]
        for j in range(size_x):
            if j != i:
                best = jnp.minimum(best, costs[j] + float((i - j) ** 2))
            d = float(j - i) + away
            best = jnp.minimum(best, costs[size_x + j] + d * d)
        lines.append(best)
    width = size_x * size_y
    rows = jnp.concatenate(lines, axis=0).T
    ends = jnp.concatenate(turned, axis=0).T
    ends = jnp.concatenate(
        [ends[r : r + 1, k * width : (k + 1) * width] for r in (0, LANES - 1, 1, 2) for k in range(2)],
        axis=0,
    )
    zm_ref[0:LANES, :] = rows
    zm_ref[LANES : LANES + 8, :] = ends
    words_ref[...] = pack_z(rows, ends)


Z_FLOOR = -(LANES + 6)


def sweep(accs, blocks, read, table, shift, low, high):
    parts = len(accs[0])

    def body(j, flat):
        flat = list(flat)
        tiles = read(j)
        squares = table.at[pl.ds(shift + 8 * blocks[0] - 8 * j, 8 * len(blocks))]
        for r in range(8):
            rows = [jnp.broadcast_to(t[r : r + 1, :], (8, LANES)) for t in tiles]
            for i in range(len(blocks)):
                square = squares[8 * i + 7 - r]
                for k in range(parts):
                    at = i * parts + k
                    flat[at] = jnp.minimum(flat[at], rows[k] + square)
        return tuple(flat)

    flat = lax.fori_loop(low, high, body, tuple(v for row in accs for v in row))
    return [list(flat[i * parts : (i + 1) * parts]) for i in range(len(blocks))]


def tiles_of(ref, j):
    rows = pl.ds(pl.multiple_of(8 * j, 8), 8)
    return [ref[rows, k * LANES : (k + 1) * LANES] for k in range(ref.shape[1] // LANES)]


def load_blocks(ref, blocks):
    return [tiles_of(ref, b) for b in blocks]


def save_blocks(ref, blocks, accs):
    for b, row in zip(blocks, accs):
        for k, v in enumerate(row):
            ref[8 * b : 8 * b + 8, k * LANES : (k + 1) * LANES] = v


def y_table(axis, hop, size_y, table):
    index = lax.axis_index(axis)
    away = (((index ^ hop) - index) * size_y).astype(jnp.float32)
    s = row_of((8, LANES)).astype(jnp.float32) - away
    for d in range(1 - size_y, size_y - 7):
        v = s + float(d)
        table[d - (1 - size_y)] = v * v


def z_own_kernel(size_y, zm_ref, out_ref, table, *y_tables):
    count, half = LANES // 8, LANES // 16
    for hop, y_one in enumerate(y_tables):
        y_table("gy", hop, size_y, y_one)
    s = row_of((8, LANES)).astype(jnp.float32)
    for d in range(Z_FLOOR, LANES):
        v = s + float(d)
        table[d - Z_FLOOR] = v * v

    def read(j):
        at = row_of((8, LANES)) + 8 * j
        hide = (at == 0) | (at == LANES - 1)
        return [jnp.where(hide, HUGE, t) for t in tiles_of(zm_ref, j)]

    for first in (0, half):
        blocks = range(first, first + half)
        accs = [[jnp.full((8, LANES), HUGE, jnp.float32)] * (out_ref.shape[1] // LANES) for _ in blocks]
        save_blocks(out_ref, blocks, sweep(accs, blocks, read, table, -7 - Z_FLOOR, 0, count))


def border_minima(cost, size_x, size_y, partner):
    if not partner:
        return cost
    width = cost.shape[1]
    shape = (8, width)
    row, plane = row_of(shape), lane_of(shape) // size_y
    away = jnp.where(lax.axis_index("gx") == 0, size_x, -size_x)
    shift = jnp.where(row % 2 == 1, away, 0)
    best = None
    for r in range(size_x):
        source = jnp.where(plane >= r, plane - r, plane - r + size_x)
        d = (source + shift - plane).astype(jnp.float32)
        if r == 0:
            moved = cost
        else:
            cut = width - r * size_y
            moved = jnp.concatenate([cost[:, cut:], cost[:, :cut]], axis=1)
        moved = moved + d * d
        best = moved if best is None else jnp.minimum(best, moved)
    return jnp.minimum(best, pltpu.roll(best, 7, 0))


def z_far_kernel(even, partner, size_x, size_y, acc_ref, table, zm_ref, got_ref, out_ref, *refs):
    *code_ref, source, work = refs
    index, last = lax.axis_index("gz"), lax.axis_size("gz") - 1
    odd = index % 2 == 1
    low = odd if even else jnp.logical_not(odd)
    valid = jnp.where(low, index > 0, index < last)
    count, half = LANES // 8, LANES // 16
    out = out_ref if even else work
    own, got = zm_ref[LANES : LANES + 8, :], unpack_ends(got_ref)
    lanes = [slice(k * LANES, (k + 1) * LANES) for k in range(zm_ref.shape[1] // LANES)]
    source[0 : LANES // 2, :], source[LANES // 2 :, :] = unpack_rows(got_ref[0 : LANES // 2, :])

    def minima(mine, theirs):
        ends = cost_of(jnp.concatenate([mine, theirs, mine, theirs], axis=0))
        return border_minima(ends, size_x, size_y, partner)

    def add_ends(ends, start, places):
        for b in range(count):
            span = slice(8 * b, 8 * b + 8)
            for cols in lanes:
                best = start[span, cols]
                for i, place in enumerate(places):
                    row = jnp.broadcast_to(ends[2 * i : 2 * i + 1, cols], (8, LANES))
                    best = jnp.minimum(best, row + table[8 * b - place - Z_FLOOR])
                out[span, cols] = best

    def slanted(accs, blocks, offset, skip, reach):
        for j in blocks:
            tile = tiles_of(source, j)
            for r in range(8):
                q = 8 * j + r
                rows = [jnp.broadcast_to(t[r : r + 1, :], (8, LANES)) for t in tile]
                for i, b in enumerate(blocks):
                    if reach(b, q) and q != skip:
                        square = table[8 * b - q + offset - Z_FLOOR]
                        accs[i] = [jnp.minimum(v, row + square) for v, row in zip(accs[i], rows)]
        return accs

    def far(offset, skip, reach, more):
        source[skip : skip + 1, :] = jnp.full((1, zm_ref.shape[1]), HUGE, jnp.float32)
        for first in (0, half):
            blocks = range(first, first + half)
            accs = slanted(load_blocks(acc_ref, blocks), blocks, offset, skip, reach)
            if more(first):
                read = functools.partial(tiles_of, source)
                accs = sweep(accs, blocks, read, table, offset - 7 - Z_FLOOR, *more(first))
            save_blocks(out, blocks, accs)

    @pl.when(valid & low)
    def _():
        ends = minima(own[0:2] + got[6:8], got[2:4] + own[4:6])
        far(LANES, LANES - 1, lambda b, q: 8 * b < q, lambda first: None if first else (half, count))
        add_ends(ends, out, (0, -1))

    @pl.when(valid & jnp.logical_not(low))
    def _():
        ends = minima(own[2:4] + got[4:6], got[0:2] + own[6:8])
        far(-LANES, 0, lambda b, q: q < 8 * b + 7, lambda first: (0, first) if first else None)
        add_ends(ends, out, (LANES - 1, LANES))

    @pl.when(jnp.logical_not(valid) & low)
    def _():
        add_ends(minima(own[0:2], own[0:2]), acc_ref, (0,))

    @pl.when(jnp.logical_not(valid) & jnp.logical_not(low))
    def _():
        add_ends(minima(own[2:4], own[2:4]), acc_ref, (LANES - 1,))

    if not even:
        per = LANES // size_y
        for k, cols in enumerate(lanes):
            best = work[:, cols].T
            code = encode(best).astype(jnp.int16)
            for i in range(per):
                out_ref[k * per + i] = best[i * size_y : (i + 1) * size_y]
                code_ref[0][k * per + i] = code[i * size_y : (i + 1) * size_y]


def score_kernel(score_in, even_ref, odd_ref, _, score_ref):
    index, last = lax.axis_index("gz"), lax.axis_size("gz") - 1
    odd = index % 2 == 1
    size_y = score_in.shape[1]
    per = LANES // size_y
    even_ends, odd_ends = unpack_ends(even_ref), unpack_ends(odd_ref)
    for k in range(even_ref.shape[1] // LANES):
        cols = slice(k * LANES, (k + 1) * LANES)
        even_rows, odd_rows = even_ends[:, cols], odd_ends[:, cols]
        low = jnp.where(index > 0, jnp.where(odd, even_rows, odd_rows)[6:7], 0.0)
        high = jnp.where(index < last, jnp.where(odd, odd_rows, even_rows)[4:5], 0.0)
        middle = jnp.zeros((LANES - 2, LANES), jnp.float32)
        more = jnp.concatenate([low, middle, high], axis=0).T
        for i in range(per):
            x = k * per + i
            score_ref[x] = score_in[x] + more[i * size_y : (i + 1) * size_y]


Y_BLOCKS = 4


def y_sweep(refs, tables, start, out_ref, scale, span=None):
    size_x, size_y, _ = out_ref.shape
    span = span or range(size_y // 8)
    for first in range(span[0], span[-1] + 1, Y_BLOCKS):
        blocks = range(first, first + Y_BLOCKS)
        accs = []
        for b in blocks:
            span = slice(8 * b, 8 * b + 8)
            blank = jnp.full((8, LANES), HUGE, jnp.float32)
            accs.append([blank if start is None else start[x, span, :] for x in range(size_x)])
        for ref, table in zip(refs, tables):

            def read(j, ref=ref):
                return [ref[x, pl.ds(pl.multiple_of(8 * j, 8), 8), :] for x in range(size_x)]

            accs = sweep(accs, blocks, read, table, size_y - 8, 0, size_y // 8)
        for b, row in zip(blocks, accs):
            for x, v in enumerate(row):
                out_ref[x, 8 * b : 8 * b + 8, :] = v if scale == 1.0 else v * scale


def y_near_kernel(own_ref, code_ref, table_0, table_1, out_ref, block):
    block[...] = decode(code_ref[...])
    y_sweep((own_ref, block), (table_0, table_1), None, out_ref, 1.0)


def y_across_kernel(start_ref, code_ref, table, out_ref, block):
    block[...] = decode(code_ref[...])
    y_sweep((block,), (table,), start_ref, out_ref, 1.0)


def y_last_kernel(start_ref, code_ref, table, score_ref, depth_hbm, score_hbm, block, depth, sems):
    index = lax.axis_index("gy")
    near = jnp.abs((index ^ 3) - index) < 3
    size_y = depth.shape[1]
    scores = pltpu.make_async_copy(score_ref, score_hbm, sems.at[0])
    scores.start()
    parts = [
        pltpu.make_async_copy(depth.at[:, rows], depth_hbm.at[:, rows], sems.at[1 + i])
        for i, rows in enumerate(pl.ds(f, size_y // 2) for f in (0, size_y // 2))
    ]

    @pl.when(near)
    def _():
        block[...] = decode(code_ref[...])
        half = size_y // 16
        for i, part in enumerate(parts):
            y_sweep((block,), (table,), start_ref, depth, 1.0 / RADIUS, range(i * half, (i + 1) * half))
            part.start()

    @pl.when(jnp.logical_not(near))
    def _():
        depth[...] = start_ref[...] * (1.0 / RADIUS)
        for part in parts:
            part.start()

    for copy in (scores, *parts):
        copy.wait()


def swap(value, axis, hop):
    n = lax.axis_size(axis)
    return lax.ppermute(value, axis, [(i, i ^ hop) for i in range(n)])


def swap_xy(value, hop_x, hop_y):
    nx, ny = lax.axis_size("gx"), lax.axis_size("gy")
    pairs = [(x * ny + y, (x ^ hop_x) * ny + (y ^ hop_y)) for x in range(nx) for y in range(ny)]
    return lax.ppermute(value, ("gx", "gy"), pairs)


def neighbours(low, high, axis, beyond=0.0):
    n, index = lax.axis_size(axis), lax.axis_index(axis)
    odd = index % 2 == 1
    pairs = [(i, i + 1 if i % 2 else i - 1) for i in range(1, n - 1)]
    got_odd = lax.ppermute(jnp.where(odd, high, low), axis, pairs)
    got_even = lax.ppermute(jnp.where(odd, low, high), axis, [(i, i ^ 1) for i in range(n)])
    from_low = jnp.where(odd, got_even, got_odd)
    from_high = jnp.where(odd, got_odd, got_even)
    return jnp.where(index == 0, beyond, from_low), jnp.where(index == n - 1, beyond, from_high)


def z_swaps(value):
    nx, ny, n = (lax.axis_size(axis) for axis in ("gx", "gy", "gz"))
    even = lax.ppermute(value, "gz", [(i, i ^ 1) for i in range(n)])
    pairs = []
    for i in range(nx * ny * n):
        xy, z = i // n, i % n
        pairs.append((i, (xy ^ 1) * n + z if z in (0, n - 1) else xy * n + (z + 1 if z % 2 else z - 1)))
    return even, lax.ppermute(value, ("gx", "gy", "gz"), pairs)


def corner_swap(value):
    nx, ny = lax.axis_size("gx"), lax.axis_size("gy")
    pairs = []
    for i in range(nx * ny):
        x, y = i // ny, i % ny
        pairs.append((i, (x ^ 1) * ny + y if y in (0, ny - 1) else x * ny + (y + 1 if y % 2 else y - 1)))
    return lax.ppermute(value, ("gx", "gy"), pairs)


def conv(features, conv_weight, mask, planes, count, paired):
    channels, size_x, size_y, _ = features.shape
    return call(
        functools.partial(conv_kernel, planes, paired),
        [(size_x, size_y, LANES), (count * size_y + 8, LANES), (16, LANES), (16, LANES)],
        [
            pltpu.VMEM(features.shape, jnp.bfloat16),
            pltpu.VMEM(conv_weight.shape, jnp.bfloat16),
            pltpu.VMEM(mask.shape, jnp.int32),
            pltpu.VMEM((9 * ROWS + 8, channels * 16), jnp.bfloat16),
            pltpu.VMEM((size_x + 2, 3, ROWS, size_y // 16 * LANES), jnp.float32),
            pltpu.SemaphoreType.DMA((size_x + 2,)),
        ],
        mib=24,
        in_specs=[HBM] * 3,
    )(*(pltpu.with_memory_space_constraint(v, pltpu.HBM) for v in (features, conv_weight, mask)))


def halo_with_partner(features, conv_weight, mask):
    _, size_x, size_y, _ = features.shape

    def planes():
        return [*range(1, size_x + 1), jnp.where(lax.axis_index("gx") == 0, size_x + 1, 0)]

    s, own, chip, cross = conv(features, conv_weight, mask, planes, size_x + 1, True)
    far = swap_xy(own, 1, 0)
    sides = [swap_xy(cross, 0, 3), swap_xy(cross, 1, 3), swap_xy(chip, 0, 1), swap_xy(chip, 1, 1)]
    lines = size_x * size_y
    words = jax.ShapeDtypeStruct((LANES // 2 + 8, lines), jnp.int32)
    return call(turn_kernel, [(size_x, size_y, LANES), (LANES + 8, lines), words])(s, own, far, *sides)


def halo_in_rounds(features, conv_weight, mask):
    _, size_x, size_y, _ = features.shape
    groups = size_y // 8
    planes = [*range(1, size_x + 1), 0, size_x + 1]
    s, rest, down, up = conv(features, conv_weight, mask, lambda: planes, size_x + 2, False)

    def whole(k):
        h = jnp.roll(rest[len(planes) * size_y :], -16 * k, 1)
        part = s[k] if k < size_x else rest[k * size_y : (k + 1) * size_y]
        return jnp.concatenate([part, h, *(e[i : i + 1] for e in (down, up) for i in (k, 8 + k))], axis=0)

    low, high = neighbours(whole(size_x), whole(size_x + 1), "gx")
    own = jnp.stack([whole(k) for k in range(size_x)]).at[0].add(low).at[size_x - 1].add(high)
    e = own[:, size_y + 8 :]
    low, high = neighbours(e[:, 0:2], e[:, 2:4], "gy")
    own = own.at[:, 0].add(low[:, 0]).at[:, size_y - 1].add(high[:, 0])
    own = own.at[:, size_y].add(low[:, 1]).at[:, size_y + 7].add(high[:, 1])
    score, h = own[:, :size_y], own[:, size_y : size_y + 8]

    def line(value):
        return value.reshape(1, size_x * size_y)

    up = jnp.swapaxes(h[:, :, 0 : 2 * groups : 2], 1, 2)
    down = jnp.swapaxes(jnp.roll(h, 1, 2)[:, :, 0 : 2 * groups : 2], 1, 2)
    masked = jnp.where(mask == 1, HUGE, score)
    rows = jnp.transpose(cost_of(masked), (2, 0, 1)).reshape(LANES, size_x * size_y)
    ends = [line(v) for v in (masked[:, :, 0], masked[:, :, LANES - 1], down, up)]
    blank = [jnp.full_like(ends[0], HUGE)] * 2 + [jnp.zeros_like(ends[0])] * 2
    pairs = [v for pair in zip(ends, blank) for v in pair]
    ends = jnp.concatenate(pairs, axis=0)
    return score, jnp.concatenate([rows, ends], axis=0), pack_z(rows, ends)


def x_minima(value, size_x):
    n, index = lax.axis_size("gx"), lax.axis_index("gx")
    every = lax.all_gather(value, "gx", axis=0, tiled=True)
    at = index * size_x + jnp.arange(size_x)
    d = (at[:, None] - jnp.arange(n * size_x)[None, :]).astype(jnp.float32)
    return jnp.min(every[None] + (d * d)[:, :, None, None], axis=1)


def shards(features, conv_weight, mask):
    _, size_x, size_y, size_z = features.shape
    gx, gy = lax.axis_size("gx"), lax.axis_size("gy")
    assert size_x == 4 and size_z == LANES and size_y % 16 == 0 and LANES % size_y == 0 and gy == 4
    brick = (size_x, size_y, LANES)
    lines = size_x * size_y
    partner = gx == 2

    halo = halo_with_partner if partner else halo_in_rounds
    score, zm, words = halo(features, conv_weight, mask)

    even, odd = z_swaps(words)
    tables = (2 * size_y - 8, 8, LANES)
    own = functools.partial(z_own_kernel, size_y)
    best, table, *kept = call(own, [(LANES, lines), (LANES - Z_FLOOR, 8, LANES)] + [tables] * 4)(zm)
    work = [pltpu.VMEM((LANES, lines), jnp.float32)] * 2
    coded = jax.ShapeDtypeStruct(brick, jnp.int16)
    for first, got, shapes in ((True, even, [(LANES, lines)]), (False, odd, [brick, coded])):
        far = functools.partial(z_far_kernel, first, partner, size_x, size_y)
        best, *code = call(far, shapes, work)(best, table, zm, got)
    if not partner:
        best = x_minima(best, size_x)
        code = [encode(best).astype(jnp.int16)]

    code = code[0]
    chip, across, corner = swap(code, "gy", 1), swap(code, "gy", 2), corner_swap(code)
    block = [pltpu.VMEM(brick, jnp.float32)]
    (near,) = call(y_near_kernel, [brick], block)(best, chip, kept[0], kept[1])
    (near,) = call(y_across_kernel, [brick], block)(near, across, kept[2])
    (score,) = call(score_kernel, [brick])(score, even, odd, near)
    last = [*block, *block, pltpu.SemaphoreType.DMA((3,))]
    depth, score = call(y_last_kernel, [brick, brick], last, out_spec=HBM)(near, corner, kept[3], score)
    return score, depth


def solution(mesh):
    in_specs = (P(None, "gx", "gy", "gz"), P(), P("gx", "gy", "gz"))
    out_specs = (P("gx", "gy", "gz"), P("gx", "gy", "gz"))
    return jax.shard_map(shards, mesh=mesh, in_specs=in_specs, out_specs=out_specs, check_vma=False)
```
